32 devices in a mesh: parts: 2 (over y), row: 4 (over z), col: 2 (over x), chan: 2 (over core).
Axes of the slice: x: 2, y: 2, z: 4, core: 2. Of those that a mesh axis runs over, the one named last changes fastest.
Arguments:
- pair: bfloat16 [32, 128, 4096], P(('parts', 'row', 'col'), 'chan'), parts along dimension 0, may hold values from -40 to 40
- ln_in_gain: float32 [128], replicated, may hold values from 0.1 to 1.9
- a_weight: bfloat16 [2, 128, 128], P(None, None, 'chan'), may hold values from -0.5 to 0.5
- b_weight: bfloat16 [2, 128, 128], P(None, None, 'chan'), may hold values from -0.5 to 0.5
- ln_out_gain: float32 [128], replicated, may hold values from 0.1 to 1.9
- out_gate_weight: bfloat16 [128, 128], P(None, 'chan'), may hold values from -0.5 to 0.5
- out_weight: bfloat16 [128, 128], P(None, 'chan'), may hold values from -0.5 to 0.5
- a_slots: int32 [32, 4], P('parts'), parts along dimension 0, may hold values from 0 to 15, as said below
- b_slots: int32 [32, 4], P('parts'), parts along dimension 0, may hold values from 0 to 15, as said below
- counts: int32 [32], P('parts'), parts along dimension 0, may hold values from 1 to 4, as said below
Outputs:
- updated: bfloat16 [32, 128, 4096], P(('parts', 'row', 'col'), 'chan'), parts along dimension 0
The draws below stay inside these ranges and needn't reach their ends.
There are 2 independent parts, one for each index of `parts`. The reference program is written for one: setup_inputs(seed, part) draws one part's arguments, and reference() takes and returns one part's arrays. A program takes and returns all parts, laid end to end along the dimension named above; an argument that names none is the same for every part. Nothing has to cross between parts.
Inputs may be any that keep to these rules, and one draw needn't show every extreme that they name: `counts`: block s lies on the tile of index s // 2 = row * 2 + col. Each output block has one to 4 used triplets; tiles with 4 for all their blocks exist in every draw, and loads differ strongly between tiles. `a_slots`: used entries (m < counts[s]) name a block on a tile of the same col whose row is within 1 row of block s's row, counted cyclically over the rows; the used entries of one output block are all different. The other entries may name any block. `b_slots`: used entries (m < counts[s]) name a block on a tile of the same col whose row is within 1 row of block s's row, counted cyclically over the rows; the used entries of one output block are all different. The used entries of a_slots and b_slots of one tile's output blocks together name at most 1 distinct blocks of any one other tile, and in every draw some tile names exactly 1 block of every other tile within reach. The other entries may name any block.
All inputs are finite; a program needn't handle non-finite values.
Results may differ from the reference program's by a relative error of at most 0.0083.
Values may be sent and summed in bfloat16 or wider, within the bound.
No kernel may reach another device: no remote copies, remote signals or barrier semaphores. Data moves between devices by JAX's collectives and lax.ppermute only.
A program may use at most 128 MiB of HBM per device.

```python
import math
import jax
import jax.numpy as jnp
from jax import lax

C = 128
BLK = 64
SLOTS = 2
TMAX = 4
REACH = 1
CAP = 1
NBLK = 16
POS = 4096
N_ROW = 4
N_COL = 2


def distinct_order(key, shape):
    scores = jax.random.randint(key, shape, 0, 1 << 20)
    scores = scores * shape[-1] + jnp.arange(shape[-1], dtype=jnp.int32)
    return jnp.argsort(scores, axis=-1).astype(jnp.int32)


def triplet_plan(key):
    devices_all = N_ROW * N_COL
    listed = SLOTS + 2 * REACH * CAP
    keys = jax.random.split(key, 10)
    device_ids = jnp.arange(devices_all, dtype=jnp.int32)
    grid_row = device_ids // N_COL
    grid_col = device_ids % N_COL
    offsets = jnp.concatenate([jnp.arange(-REACH, 0, dtype=jnp.int32), jnp.arange(1, REACH + 1, dtype=jnp.int32)])
    senders = (grid_row[:, None] + offsets[None, :]) % N_ROW * N_COL + grid_col[:, None]
    order = distinct_order(keys[0], (devices_all, 2 * REACH, SLOTS))[:, :, :CAP]
    others = (senders[:, :, None] * SLOTS + order).reshape(devices_all, 2 * REACH * CAP)
    own = device_ids[:, None] * SLOTS + jnp.arange(SLOTS, dtype=jnp.int32)[None, :]
    pool = jnp.concatenate([own, others], axis=1)
    ranking = jax.random.permutation(keys[1], devices_all)
    heavy = ranking < max(1, devices_all // 8)
    first = jax.random.randint(keys[2], (devices_all, SLOTS), 0, TMAX)
    second = jax.random.randint(keys[3], (devices_all, SLOTS), 0, TMAX)
    light_counts = 1 + first * second // (TMAX - 1)
    counts_all = jnp.where(heavy[:, None], TMAX, light_counts).astype(jnp.int32)
    sequence = jnp.arange(SLOTS, dtype=jnp.int32)[:, None] * TMAX + jnp.arange(TMAX, dtype=jnp.int32)[None, :]
    tile_a = distinct_order(keys[4], (devices_all, listed))
    tile_b = distinct_order(keys[5], (devices_all, listed))
    heavy_a = jnp.take_along_axis(tile_a, (sequence % listed).reshape(1, -1) + jnp.zeros((devices_all, 1), jnp.int32), axis=1)
    heavy_b = jnp.take_along_axis(tile_b, ((sequence + 1) % listed).reshape(1, -1) + jnp.zeros((devices_all, 1), jnp.int32), axis=1)
    light_a = distinct_order(keys[6], (devices_all, SLOTS, listed))[:, :, :TMAX].reshape(devices_all, SLOTS * TMAX)
    light_b = distinct_order(keys[7], (devices_all, SLOTS, listed))[:, :, :TMAX].reshape(devices_all, SLOTS * TMAX)
    which_a = jnp.where(heavy[:, None], heavy_a, light_a)
    which_b = jnp.where(heavy[:, None], heavy_b, light_b)
    left_used = jnp.take_along_axis(pool, which_a, axis=1).reshape(devices_all, SLOTS, TMAX)
    right_used = jnp.take_along_axis(pool, which_b, axis=1).reshape(devices_all, SLOTS, TMAX)
    left_spare = jax.random.randint(keys[8], (devices_all, SLOTS, TMAX), 0, NBLK)
    right_spare = jax.random.randint(keys[9], (devices_all, SLOTS, TMAX), 0, NBLK)
    active = jnp.arange(TMAX, dtype=jnp.int32)[None, None, :] < counts_all[:, :, None]
    left_all = jnp.where(active, left_used, left_spare).reshape(NBLK, TMAX).astype(jnp.int32)
    right_all = jnp.where(active, right_used, right_spare).reshape(NBLK, TMAX).astype(jnp.int32)
    return (left_all, right_all, counts_all.reshape(NBLK))


def draw_a_slots(key, part):
    shared_plan = triplet_plan(key)
    return shared_plan[0]


def draw_b_slots(key, part):
    shared_plan = triplet_plan(key)
    return shared_plan[1]


def draw_counts(key, part):
    shared_plan = triplet_plan(key)
    return shared_plan[2]


def draw_pair(key, part):
    key = jax.random.fold_in(key, 17)
    noise_key, chan_key, cell_key = jax.random.split(key, 3)
    chan_scale = jnp.exp(jax.random.uniform(chan_key, (1, C, 1), jnp.float32, 0.0, math.log(10.0)))
    cell_scale = jnp.exp(jax.random.uniform(cell_key, (NBLK, 1, POS), jnp.float32, 0.0, math.log(10.0)))
    values = jax.random.normal(noise_key, (NBLK, C, POS), jnp.float32) * chan_scale * cell_scale
    return jnp.clip(0.1 * values, -40.0, 40.0).astype(jnp.bfloat16)


def level_of(rng, shape, pieces, least, top_value):
    def one(axis_at, shards_of):
        steps = jax.random.uniform(jax.random.fold_in(jax.random.fold_in(rng, 6), axis_at), (shards_of,), jnp.float32, least / len(pieces), top_value / len(pieces))
        return jnp.repeat(jnp.exp(steps), shape[axis_at] // shards_of).reshape((-1,) + (1,) * (len(shape) - axis_at - 1))

    loudness = one(*pieces[0])
    for cut in pieces[1:]:
        loudness = loudness * one(*cut)
    return loudness


def scatter_about(key, dims, deviation, reach, cuts=(), held_as=jnp.bfloat16):
    result = jax.random.normal(key, dims, jnp.float32) * deviation
    if len(cuts) > 0:
        result = level_of(key, dims, cuts, -0.22, 0.18) * result
    return jnp.clip(result, min=-reach, max=reach).astype(held_as)


def setup_inputs(seed: int = 0, part: int = 0) -> dict:
    key_list = jax.random.split(jax.random.key(seed), 11)
    part_keys = jax.random.split(jax.random.fold_in(key_list[10], part), 11)
    return {
        "pair": draw_pair(jax.random.fold_in(jax.random.fold_in(key_list[10], part), 71), part),
        "ln_in_gain": jnp.clip(1.0 + 0.18 * jax.random.normal(key_list[1], (C,), jnp.float32), 0.1, 1.9),
        "a_weight": scatter_about(key_list[2], (2, C, C), C ** -0.5, 0.5, ((2, 2),)),
        "b_weight": scatter_about(key_list[3], (2, C, C), C ** -0.5, 0.5, ((2, 2),)),
        "ln_out_gain": jnp.clip(1.0 + 0.18 * jax.random.normal(key_list[4], (C,), jnp.float32), 0.1, 1.9),
        "out_gate_weight": scatter_about(key_list[5], (C, C), C ** -0.5, 0.5, ((1, 2),)),
        "out_weight": scatter_about(key_list[6], (C, C), C ** -0.5, 0.5, ((1, 2),)),
        "a_slots": draw_a_slots(jax.random.fold_in(jax.random.fold_in(key_list[10], part), 71), part),
        "b_slots": draw_b_slots(jax.random.fold_in(jax.random.fold_in(key_list[10], part), 71), part),
        "counts": draw_counts(jax.random.fold_in(jax.random.fold_in(key_list[10], part), 71), part),
    }


epsilon = 1e-05

def layer_norm(values, norm_gain):
    average = lax.optimization_barrier(jnp.mean(values, axis=-2, keepdims=True))
    centred = values - average
    spread = lax.optimization_barrier(jnp.mean(centred * centred, axis=-2, keepdims=True))
    return centred * lax.rsqrt(spread + epsilon) * norm_gain[:, None]

def gated_proj(normed, weight):
    gate_part = jnp.dot(weight[0].T, normed, preferred_element_type=jnp.float32)
    value_part = jnp.dot(weight[1].T, normed, preferred_element_type=jnp.float32)
    return (jax.nn.sigmoid(gate_part) * value_part).astype(jnp.bfloat16)

def reference(pair, ln_in_gain, a_weight, b_weight, ln_out_gain, out_gate_weight, out_weight, a_slots, b_slots, counts):

    def project(block):
        normed = layer_norm(block.astype(jnp.float32), ln_in_gain).astype(jnp.bfloat16)
        return (normed, gated_proj(normed, a_weight), gated_proj(normed, b_weight))
    normed_all, left_side, right_side = lax.map(project, pair)

    def combine(index):
        active = (jnp.arange(TMAX, dtype=jnp.int32) < counts[index]).astype(jnp.float32)
        left_blocks = jnp.take(left_side, a_slots[index], axis=0).astype(jnp.float32)
        right_blocks = jnp.take(right_side, b_slots[index], axis=0).astype(jnp.float32)
        left_blocks = left_blocks.reshape(TMAX, C, BLK, BLK) * active[:, None, None, None]
        right_blocks = right_blocks.reshape(TMAX, C, BLK, BLK)
        product = jnp.einsum('mcik,mcjk->cij', left_blocks, right_blocks)
        return product.reshape(C, BLK * BLK).astype(jnp.bfloat16)
    update = lax.map(combine, jnp.arange(NBLK, dtype=jnp.int32))

    def finish(items):
        normed, block_update = items
        update_normed = layer_norm(block_update.astype(jnp.float32), ln_out_gain).astype(jnp.bfloat16)
        out_gating = jax.nn.sigmoid(jnp.dot(out_gate_weight.T, normed, preferred_element_type=jnp.float32))
        projected = jnp.dot(out_weight.T, update_normed, preferred_element_type=jnp.float32)
        return (out_gating * projected).astype(jnp.bfloat16)
    return lax.map(finish, (normed_all, update))
```

```python
import functools

import jax
import jax.numpy as jnp
from jax import lax
from jax.experimental import pallas as pl
from jax.experimental.pallas import tpu as pltpu
from jax.sharding import PartitionSpec as P

BLK = 64
LANES = 128
epsilon = 1e-05
VMEM_LIMIT = 48 * 1024 * 1024
F32 = jnp.float32
BF16 = jnp.bfloat16


def sigmoid(x):
    return 0.5 * jnp.tanh(0.5 * x) + 0.5


def tile_of(row, col):
    return row * lax.axis_size("col") + col


def neighbour_tiles():
    rows = lax.axis_size("row")
    row, col = lax.axis_index("row"), lax.axis_index("col")
    behind = lax.rem(row + rows - 1, rows)
    ahead = lax.rem(row + 1, rows)
    return tile_of(row, col), tile_of(behind, col), tile_of(ahead, col)


def select_kernel(slots, triplets, a_ref, b_ref, n_ref, pair_ref, ahead_ref, behind_ref, sems):
    me, behind, ahead = neighbour_tiles()
    copies = []
    for at, (target, out_ref) in enumerate(((ahead, ahead_ref), (behind, behind_ref))):
        pick = jnp.int32(0)
        for s in range(slots):
            count = n_ref[target * slots + s]
            for m in range(triplets):
                for ids in (a_ref, b_ref):
                    name = ids[target * slots + s, m]
                    mine = jnp.logical_and(m < count, name // slots == me)
                    pick = jnp.where(mine, name % slots, pick)
        copies.append(pltpu.make_async_copy(pair_ref.at[pick], out_ref, sems.at[at]))
        copies[-1].start()
    for copy in copies:
        copy.wait()


def select_blocks(pair, a_slots, b_slots, counts):
    slots, channels, cells = pair.shape
    smem = pl.BlockSpec(memory_space=pltpu.SMEM)
    block = jax.ShapeDtypeStruct((channels, cells), pair.dtype)
    return pl.pallas_call(
        functools.partial(select_kernel, slots, a_slots.shape[1]),
        out_shape=(block, block),
        in_specs=[smem, smem, smem, pl.BlockSpec(memory_space=pl.ANY)],
        out_specs=(pl.BlockSpec(memory_space=pl.ANY), pl.BlockSpec(memory_space=pl.ANY)),
        scratch_shapes=[pltpu.SemaphoreType.DMA((2,))],
        name="select_blocks",
    )(a_slots, b_slots, counts, pair)


def normed_of(mine, theirs, gain):
    half = mine.shape[0]
    total = 2 * half
    mine = mine.astype(F32)
    theirs = theirs.astype(F32)
    mean = (jnp.sum(mine, axis=0, keepdims=True) + jnp.sum(theirs, axis=0, keepdims=True)) / total
    mine = mine - mean
    theirs = theirs - mean
    spread = (
        jnp.sum(mine * mine, axis=0, keepdims=True) + jnp.sum(theirs * theirs, axis=0, keepdims=True)
    ) / total
    scale = lax.rsqrt(spread + epsilon)
    return jnp.concatenate(
        [(mine * scale * gain[:half]).astype(BF16), (theirs * scale * gain[half:]).astype(BF16)],
        axis=0,
    )


def project_kernel(piece, gated, *refs):
    m0, t0, m1, t1, w_ref, g_ref = refs[:6]
    refs = refs[6:] if gated else refs[8:]
    if gated:
        l_ref, p_ref, gate_ref, sl, sp, sq = refs
    else:
        l_ref, p_ref, sl, sp, sq = refs
    chunk = m0.shape[-1]
    half = m0.shape[-2]
    weight = w_ref[...]
    gain = g_ref[...]
    low = lax.broadcasted_iota(jnp.int32, (half, LANES), 1) < BLK
    for start in range(0, chunk, piece):
        sides = []
        for x, (m, t) in enumerate(((m0, t0), (m1, t1))):
            normed = normed_of(m[:, start : start + piece], t[:, start : start + piece], gain)
            y = jnp.dot(weight, normed, preferred_element_type=F32)
            left = sigmoid(y[:half]) * y[half : 2 * half]
            right = sigmoid(y[2 * half : 3 * half]) * y[3 * half : 4 * half]
            sides.append((left, right))
            if gated:
                gate_ref[x, :, start : start + piece] = sigmoid(y[4 * half :]).astype(BF16)
        for sub in range(0, piece, LANES):
            i = (start + sub) // BLK
            even = pl.ds(i * half, half)
            odd = pl.ds((i + 1) * half, half)
            l0, l1 = (side[0][:, sub : sub + LANES] for side in sides)
            r0, r1 = (side[1][:, sub : sub + LANES] for side in sides)
            l0r, l1r, r0r, r1r = (pltpu.roll(v, BLK, 1) for v in (l0, l1, r0, r1))
            sl[even, :] = jnp.where(low, l0, l1r)
            sl[odd, :] = jnp.where(low, l0r, l1)
            sp[even, :] = jnp.where(low, r0, r1r)
            sp[odd, :] = jnp.where(low, r0r, r1)
            sq[even, :] = jnp.where(low, r1, r0r)
            sq[odd, :] = jnp.where(low, r1r, r0)
    rows = chunk // BLK

    @pl.loop(0, half, unroll=8)
    def _(c):
        take = pl.ds(c, rows, stride=half)
        l_ref[0, c] = sl[take, :].astype(BF16)
        p_ref[0, c] = sp[take, :].astype(BF16)
        p_ref[1, c] = sq[take, :].astype(BF16)


def project(blocks, weight, gain, chunk, piece, gated, held=None):
    half, cells = blocks[0].shape[-2:]
    pair_of = 0 if gated else 1
    in_specs = []
    for block, at in blocks_with_index(blocks):
        if block.ndim == 3:
            in_specs.append(
                pl.BlockSpec((None, half, chunk), functools.partial(lambda x, n: (x, 0, n), at))
            )
        else:
            in_specs.append(pl.BlockSpec((half, chunk), lambda n: (0, n)))
    rows = chunk // BLK
    whole = lambda a: pl.BlockSpec(a.shape, lambda n: (0,) * a.ndim)
    in_specs += [whole(weight), whole(gain)]
    operands = [*blocks, weight, gain]
    out_shape = [
        jax.ShapeDtypeStruct((2, half, BLK, LANES), BF16),
        jax.ShapeDtypeStruct((4, half, BLK, LANES), BF16),
    ]
    out_specs = [
        pl.BlockSpec((1, half, rows, LANES), lambda n: (pair_of, 0, n, 0)),
        pl.BlockSpec((2, half, rows, LANES), lambda n: (pair_of, 0, n, 0)),
    ]
    aliases = {}
    if gated:
        out_shape.append(jax.ShapeDtypeStruct((2, half, cells), BF16))
        out_specs.append(pl.BlockSpec((2, half, chunk), lambda n: (0, 0, n)))
    else:
        in_specs += [pl.BlockSpec(memory_space=pl.ANY)] * 2
        aliases = {len(operands): 0, len(operands) + 1: 1}
        operands += held
    return pl.pallas_call(
        functools.partial(project_kernel, piece, gated),
        grid=(cells // chunk,),
        in_specs=in_specs,
        out_specs=out_specs,
        out_shape=out_shape,
        scratch_shapes=[pltpu.VMEM((rows * half, LANES), F32)] * 3,
        input_output_aliases=aliases,
        compiler_params=pltpu.CompilerParams(vmem_limit_bytes=VMEM_LIMIT),
        cost_estimate=pl.CostEstimate(
            flops=2 * 2 * cells * weight.shape[0] * weight.shape[1],
            bytes_accessed=8 * 1024 * 1024,
            transcendentals=4 * half * cells,
        ),
        name="project_own" if gated else "project_fetched",
    )(*operands)


def blocks_with_index(blocks):
    return [(block, at // 2) for at, block in enumerate(blocks)]


def triplet_kernel(slots, triplets, group, a_ref, b_ref, n_ref, l_ref, p_ref, out_ref, acc):
    me, behind, ahead = neighbour_tiles()
    lane = lax.broadcasted_iota(jnp.int32, (1, LANES), 1)
    low = (lane < BLK).astype(F32)
    high = 1.0 - low
    picks = []
    for s in range(slots):
        block = me * slots + s
        count = n_ref[block]
        for pair_at in range(2):
            halves = []
            for part in range(2):
                chosen = jnp.int32(0)
                used = jnp.int32(0)
                for m in range(triplets):
                    left = a_ref[block, m]
                    right = b_ref[block, m]
                    if pair_at == 0:
                        hit = left == me * slots + part
                    else:
                        hit = left // slots == (behind, ahead)[part]
                    hit = jnp.logical_and(hit, m < count)
                    tile = right // slots
                    place = jnp.where(
                        tile == me, right % slots, jnp.where(tile == behind, 2, 3)
                    )
                    chosen = jnp.where(hit, place, chosen)
                    used = jnp.where(hit, 1, used)
                if part == 1:
                    chosen = chosen + 1 - 2 * lax.rem(chosen, 2)
                weight = (low, high)[part] * used.astype(F32)
                halves.append((chosen, weight.astype(BF16)))
            picks.append(halves)

    @pl.loop(0, group, unroll=4)
    def _(c):
        lhs = jnp.concatenate([l_ref[0, c], l_ref[1, c]], axis=1)
        rows = []
        for s in range(slots):
            parts = []
            for pair_at in range(2):
                (low_pick, low_mask), (high_pick, high_mask) = picks[2 * s + pair_at]
                parts.append(p_ref[low_pick, c] * low_mask + p_ref[high_pick, c] * high_mask)
            rows.append(jnp.concatenate(parts, axis=1))
        rhs = jnp.concatenate(rows, axis=0)
        acc[pl.ds(c, BLK, stride=group), :] = lax.dot_general(
            lhs, rhs, (((1,), (1,)), ((), ())), preferred_element_type=F32
        )

    take_low = lax.broadcasted_iota(jnp.int32, (group, LANES), 1) < BLK
    for t in range(BLK // 2):
        even = acc[2 * t * group : (2 * t + 1) * group, :]
        odd = acc[(2 * t + 1) * group : (2 * t + 2) * group, :]
        to = pl.ds(t * LANES, LANES)
        out_ref[0, :, to] = jnp.where(take_low, even, pltpu.roll(odd, BLK, 1)).astype(BF16)
        out_ref[1, :, to] = jnp.where(take_low, pltpu.roll(even, BLK, 1), odd).astype(BF16)


def triplet_sum(lefts, rights, a_slots, b_slots, counts, slots, group):
    half = lefts.shape[1]
    smem = pl.BlockSpec(memory_space=pltpu.SMEM)
    return pl.pallas_call(
        functools.partial(triplet_kernel, slots, a_slots.shape[1], group),
        grid=(half // group,),
        in_specs=[
            smem,
            smem,
            smem,
            pl.BlockSpec((2, group, BLK, LANES), lambda n: (0, n, 0, 0)),
            pl.BlockSpec((4, group, BLK, LANES), lambda n: (0, n, 0, 0)),
        ],
        out_specs=pl.BlockSpec((slots, group, BLK * BLK), lambda n: (0, n, 0)),
        out_shape=jax.ShapeDtypeStruct((slots, half, BLK * BLK), BF16),
        scratch_shapes=[pltpu.VMEM((BLK * group, LANES), F32)],
        compiler_params=pltpu.CompilerParams(vmem_limit_bytes=VMEM_LIMIT),
        name="triplets",
    )(a_slots, b_slots, counts, lefts, rights)


def finish_kernel(piece, mine_ref, theirs_ref, gate_ref, w_ref, g_ref, out_ref):
    weight = w_ref[...]
    gain = g_ref[...]
    for s in range(mine_ref.shape[0]):
        for start in range(0, mine_ref.shape[-1], piece):
            to = slice(start, start + piece)
            normed = normed_of(mine_ref[s, :, to], theirs_ref[s, :, to], gain)
            projected = jnp.dot(weight, normed, preferred_element_type=F32)
            out_ref[s, :, to] = (gate_ref[s, :, to].astype(F32) * projected).astype(BF16)


def finish(mine, theirs, gate, weight, gain, chunk, piece):
    slots, half, cells = mine.shape
    cut = pl.BlockSpec((slots, half, chunk), lambda n: (0, 0, n))
    return pl.pallas_call(
        functools.partial(finish_kernel, piece),
        grid=(cells // chunk,),
        in_specs=[
            cut,
            cut,
            cut,
            pl.BlockSpec(weight.shape, lambda n: (0, 0)),
            pl.BlockSpec(gain.shape, lambda n: (0, 0)),
        ],
        out_specs=cut,
        out_shape=jax.ShapeDtypeStruct(mine.shape, BF16),
        compiler_params=pltpu.CompilerParams(vmem_limit_bytes=VMEM_LIMIT),
        name="finish",
    )(mine, theirs, gate, weight, gain)


def per_device(
    pair,
    ln_in_gain,
    a_weight,
    b_weight,
    ln_out_gain,
    out_gate_weight,
    out_weight,
    a_slots,
    b_slots,
    counts,
):
    slots, half, cells = pair.shape
    rows = lax.axis_size("row")
    up = [(i, (i + 1) % rows) for i in range(rows)]
    down = [(i, (i - 1) % rows) for i in range(rows)]
    swap = [(0, 1), (1, 0)]
    chan = lax.axis_index("chan")

    to_ahead, to_behind = select_blocks(pair, a_slots, b_slots, counts)
    from_behind = lax.ppermute(to_ahead, "row", up)
    from_ahead = lax.ppermute(to_behind, "row", down)
    pair_other = lax.ppermute(pair, "chan", swap)

    def own_first(values, axis):
        return jnp.where(chan == 0, values, jnp.roll(values, half, axis))

    weight = jnp.concatenate(
        [a_weight[0], a_weight[1], b_weight[0], b_weight[1], out_gate_weight], axis=1
    )
    weight = own_first(weight, 0).T
    last_weight = own_first(out_weight, 0).T
    gain = own_first(ln_in_gain, 0)[:, None]
    last_gain = own_first(ln_out_gain, 0)[:, None]

    lefts, rights, gate = project(
        [pair, pair_other, pair, pair_other], weight, gain, 1024, 256, True
    )
    behind_other = lax.ppermute(from_behind, "chan", swap)
    ahead_other = lax.ppermute(from_ahead, "chan", swap)
    lefts, rights = project(
        [from_behind, behind_other, from_ahead, ahead_other],
        weight[: 4 * half],
        gain,
        1024,
        256,
        False,
        [lefts, rights],
    )
    update = triplet_sum(lefts, rights, a_slots, b_slots, counts, slots, 16)
    update_other = lax.ppermute(update, "chan", swap)
    return finish(update, update_other, gate, last_weight, last_gain, 1024, 256)


def solution(mesh):
    in_specs = (
        P(("parts", "row", "col"), "chan", None),
        P(),
        P(None, None, "chan"),
        P(None, None, "chan"),
        P(),
        P(None, "chan"),
        P(None, "chan"),
        P("parts", None),
        P("parts", None),
        P("parts"),
    )
    out_specs = P(("parts", "row", "col"), "chan", None)
    return jax.shard_map(
        per_device, mesh=mesh, in_specs=in_specs, out_specs=out_specs, check_vma=False
    )
```

```python
import functools

import jax
import jax.numpy as jnp
from jax import lax
from jax.experimental import pallas as pl
from jax.experimental.pallas import tpu as pltpu
from jax.sharding import PartitionSpec as P

BLK = 64
LANES = 128
epsilon = 1e-05
VMEM_LIMIT = 48 * 1024 * 1024
F32 = jnp.float32
BF16 = jnp.bfloat16


def sigmoid(x):
    return 0.5 * jnp.tanh(0.5 * x) + 0.5


def tile_of(row, col):
    return row * lax.axis_size("col") + col


def neighbour_tiles():
    rows = lax.axis_size("row")
    row, col = lax.axis_index("row"), lax.axis_index("col")
    behind = lax.rem(row + rows - 1, rows)
    ahead = lax.rem(row + 1, rows)
    return tile_of(row, col), tile_of(behind, col), tile_of(ahead, col)


def select_kernel(slots, triplets, a_ref, b_ref, n_ref, pair_ref, first_ref, second_ref, sems):
    me, behind, ahead = neighbour_tiles()
    core = lax.axis_index("chan")
    targets = (jnp.where(core == 0, ahead, behind), jnp.where(core == 0, behind, ahead))
    copies = []
    for at, (target, out_ref) in enumerate(zip(targets, (first_ref, second_ref))):
        pick = jnp.int32(0)
        for s in range(slots):
            count = n_ref[target * slots + s]
            for m in range(triplets):
                for ids in (a_ref, b_ref):
                    name = ids[m, target * slots + s] - me * slots
                    mine = jnp.logical_and(name >= 0, name < slots)
                    pick = jnp.where(jnp.logical_and(m < count, mine), name, pick)
        copies.append(pltpu.make_async_copy(pair_ref.at[pick], out_ref, sems.at[at]))
        copies[-1].start()
    for copy in copies:
        copy.wait()


def select_blocks(pair, a_slots, b_slots, counts):
    slots, channels, cells = pair.shape
    smem = pl.BlockSpec(memory_space=pltpu.SMEM)
    vmem = pl.BlockSpec(memory_space=pltpu.VMEM)
    block = jax.ShapeDtypeStruct((channels, cells), pair.dtype)
    return pl.pallas_call(
        functools.partial(select_kernel, slots, a_slots.shape[0]),
        out_shape=(block, block),
        in_specs=[smem, smem, smem, pl.BlockSpec(memory_space=pltpu.HBM)],
        out_specs=(vmem, vmem),
        scratch_shapes=[pltpu.SemaphoreType.DMA((2,))],
        name="select_blocks",
    )(a_slots, b_slots, counts, pair)


def own_lanes_first(weight):
    wide = weight.astype(F32)
    wide = jnp.where(lax.axis_index("chan") == 0, wide, pltpu.roll(wide, weight.shape[1] // 2, 1))
    return wide.astype(BF16)


def gains_of(g_ref):
    half = g_ref.shape[0] // 2
    chan = lax.axis_index("chan")
    mine = g_ref[pl.ds(pl.multiple_of(chan * half, half), half), :]
    theirs = g_ref[pl.ds(pl.multiple_of((1 - chan) * half, half), half), :]
    return mine, theirs


def normed_of(mine, theirs, gain):
    half = mine.shape[0]
    total = 2 * half
    mine = mine.astype(F32)
    theirs = theirs.astype(F32)
    mean = (jnp.sum(mine, axis=0, keepdims=True) + jnp.sum(theirs, axis=0, keepdims=True)) / total
    mine = mine - mean
    theirs = theirs - mean
    spread = (
        jnp.sum(mine * mine, axis=0, keepdims=True) + jnp.sum(theirs * theirs, axis=0, keepdims=True)
    ) / total
    scale = lax.rsqrt(spread + epsilon)
    return jnp.concatenate(
        [(mine * scale * gain[0]).astype(BF16), (theirs * scale * gain[1]).astype(BF16)],
        axis=0,
    )


def project_kernel(piece, gated, *refs):
    m0, t0, m1, t1, a_ref, b_ref, g_ref = refs[:7]
    weights = [a_ref[0], a_ref[1], b_ref[0], b_ref[1]]
    if gated:
        weights.append(refs[7][...])
        l_ref, p_ref, gate_ref, sl, sp, sq = refs[8:]
    else:
        l_ref, p_ref, sl, sp, sq = refs[9:]
    chunk = m0.shape[-1]
    half = m0.shape[-2]
    weight = own_lanes_first(jnp.concatenate(weights, axis=0))
    gain = gains_of(g_ref)
    low = lax.broadcasted_iota(jnp.int32, (half, LANES), 1) < BLK
    for start in range(0, chunk, piece):
        sides = []
        for x, (m, t) in enumerate(((m0, t0), (m1, t1))):
            normed = normed_of(m[:, start : start + piece], t[:, start : start + piece], gain)
            y = jnp.dot(weight, normed, preferred_element_type=F32)
            left = sigmoid(y[:half]) * y[half : 2 * half]
            right = sigmoid(y[2 * half : 3 * half]) * y[3 * half : 4 * half]
            sides.append((left, right))
            if gated:
                gate_ref[x, :, start : start + piece] = sigmoid(y[4 * half :]).astype(BF16)
        for sub in range(0, piece, LANES):
            i = (start + sub) // BLK
            even = pl.ds(i * half, half)
            odd = pl.ds((i + 1) * half, half)
            l0, l1 = (side[0][:, sub : sub + LANES] for side in sides)
            r0, r1 = (side[1][:, sub : sub + LANES] for side in sides)
            l0r, l1r, r0r, r1r = (pltpu.roll(v, BLK, 1) for v in (l0, l1, r0, r1))
            sl[even, :] = jnp.where(low, l0, l1r)
            sl[odd, :] = jnp.where(low, l0r, l1)
            sp[even, :] = jnp.where(low, r0, r1r)
            sp[odd, :] = jnp.where(low, r0r, r1)
            sq[even, :] = jnp.where(low, r1, r0r)
            sq[odd, :] = jnp.where(low, r1r, r0)
    rows = chunk // BLK

    @pl.loop(0, half, unroll=8)
    def _(c):
        take = pl.ds(c, rows, stride=half)
        l_ref[0, c] = sl[take, :].astype(BF16)
        p_ref[0, c] = sp[take, :].astype(BF16)
        p_ref[1, c] = sq[take, :].astype(BF16)


def project(blocks, weights, gain, chunk, piece, gated, held=None):
    half, cells = blocks[0].shape[-2:]
    pair_of = 0 if gated else 1
    in_specs = []
    for block, at in blocks_with_index(blocks):
        if block.ndim == 3:
            in_specs.append(
                pl.BlockSpec((None, half, chunk), functools.partial(lambda x, n: (x, 0, n), at))
            )
        else:
            in_specs.append(pl.BlockSpec((half, chunk), lambda n: (0, n)))
    rows = chunk // BLK
    whole = lambda a: pl.BlockSpec(a.shape, lambda n: (0,) * a.ndim)
    operands = [*blocks, weights[0], weights[1], gain]
    if gated:
        operands.append(weights[2])
    in_specs += [whole(value) for value in operands[4:]]
    out_shape = [
        jax.ShapeDtypeStruct((2, half, BLK, LANES), BF16),
        jax.ShapeDtypeStruct((4, half, BLK, LANES), BF16),
    ]
    out_specs = [
        pl.BlockSpec((1, half, rows, LANES), lambda n: (pair_of, 0, n, 0)),
        pl.BlockSpec((2, half, rows, LANES), lambda n: (pair_of, 0, n, 0)),
    ]
    aliases = {}
    if gated:
        out_shape.append(jax.ShapeDtypeStruct((2, half, cells), BF16))
        out_specs.append(pl.BlockSpec((2, half, chunk), lambda n: (0, 0, n)))
    else:
        in_specs += [pl.BlockSpec(memory_space=pl.ANY)] * 2
        aliases = {len(operands): 0, len(operands) + 1: 1}
        operands += held
    return pl.pallas_call(
        functools.partial(project_kernel, piece, gated),
        grid=(cells // chunk,),
        in_specs=in_specs,
        out_specs=out_specs,
        out_shape=out_shape,
        scratch_shapes=[pltpu.VMEM((rows * half, LANES), F32)] * 3,
        input_output_aliases=aliases,
        compiler_params=pltpu.CompilerParams(vmem_limit_bytes=VMEM_LIMIT),
        cost_estimate=pl.CostEstimate(
            flops=2 * 2 * cells * 8 * half * half,
            bytes_accessed=8 * 1024 * 1024,
            transcendentals=4 * half * cells,
        ),
        name="project_own" if gated else "project_fetched",
    )(*operands)


def blocks_with_index(blocks):
    return [(block, at // 2) for at, block in enumerate(blocks)]


def triplet_kernel(slots, triplets, group, a_ref, b_ref, n_ref, l_ref, p_ref, out_ref, acc):
    me, behind, ahead = neighbour_tiles()
    lane = lax.broadcasted_iota(jnp.int32, (1, LANES), 1)
    low = (lane < BLK).astype(F32)
    high = 1.0 - low
    picks = []
    for s in range(slots):
        block = me * slots + s
        count = n_ref[block]
        for pair_at in range(2):
            halves = []
            for part in range(2):
                chosen = jnp.int32(0)
                used = jnp.int32(0)
                for m in range(triplets):
                    left = a_ref[m, block]
                    if pair_at == 0:
                        hit = left == me * slots + part
                    else:
                        first = (behind, ahead)[part] * slots
                        hit = jnp.logical_and(left >= first, left < first + slots)
                    hit = jnp.logical_and(hit, m < count)
                    place = b_ref[m, block] - me * slots
                    from_me = jnp.logical_and(place >= 0, place < slots)
                    right = b_ref[m, block] - behind * slots
                    from_behind = jnp.logical_and(right >= 0, right < slots)
                    place = jnp.where(from_me, place, jnp.where(from_behind, 2, 3))
                    chosen = jnp.where(hit, place, chosen)
                    used = jnp.where(hit, 1, used)
                if part == 1:
                    chosen = chosen + 1 - 2 * (chosen & 1)
                weight = (low, high)[part] * used.astype(F32)
                halves.append((chosen, weight.astype(BF16)))
            picks.append(halves)

    @pl.loop(0, group, unroll=4)
    def _(c):
        lhs = jnp.concatenate([l_ref[0, c], l_ref[1, c]], axis=1)
        rows = []
        for s in range(slots):
            parts = []
            for pair_at in range(2):
                (low_pick, low_mask), (high_pick, high_mask) = picks[2 * s + pair_at]
                parts.append(p_ref[low_pick, c] * low_mask + p_ref[high_pick, c] * high_mask)
            rows.append(jnp.concatenate(parts, axis=1))
        rhs = jnp.concatenate(rows, axis=0)
        acc[pl.ds(c, BLK, stride=group), :] = lax.dot_general(
            lhs, rhs, (((1,), (1,)), ((), ())), preferred_element_type=F32
        )

    take_low = lax.broadcasted_iota(jnp.int32, (group, LANES), 1) < BLK
    for t in range(BLK // 2):
        even = acc[2 * t * group : (2 * t + 1) * group, :]
        odd = acc[(2 * t + 1) * group : (2 * t + 2) * group, :]
        to = pl.ds(t * LANES, LANES)
        out_ref[0, :, to] = jnp.where(take_low, even, pltpu.roll(odd, BLK, 1)).astype(BF16)
        out_ref[1, :, to] = jnp.where(take_low, pltpu.roll(even, BLK, 1), odd).astype(BF16)


def triplet_sum(lefts, rights, a_slots, b_slots, counts, slots, group):
    half = lefts.shape[1]
    smem = pl.BlockSpec(memory_space=pltpu.SMEM)
    return pl.pallas_call(
        functools.partial(triplet_kernel, slots, a_slots.shape[0], group),
        grid=(half // group,),
        in_specs=[
            smem,
            smem,
            smem,
            pl.BlockSpec((2, group, BLK, LANES), lambda n: (0, n, 0, 0)),
            pl.BlockSpec((4, group, BLK, LANES), lambda n: (0, n, 0, 0)),
        ],
        out_specs=pl.BlockSpec((slots, group, BLK * BLK), lambda n: (0, n, 0)),
        out_shape=jax.ShapeDtypeStruct((slots, half, BLK * BLK), BF16),
        scratch_shapes=[pltpu.VMEM((BLK * group, LANES), F32)],
        compiler_params=pltpu.CompilerParams(vmem_limit_bytes=VMEM_LIMIT),
        name="triplets",
    )(a_slots, b_slots, counts, lefts, rights)


def finish_kernel(piece, mine_ref, theirs_ref, gate_ref, w_ref, g_ref, out_ref):
    weight = own_lanes_first(w_ref[...])
    gain = gains_of(g_ref)
    for s in range(mine_ref.shape[0]):
        for start in range(0, mine_ref.shape[-1], piece):
            to = slice(start, start + piece)
            normed = normed_of(mine_ref[s, :, to], theirs_ref[s, :, to], gain)
            projected = jnp.dot(weight, normed, preferred_element_type=F32)
            out_ref[s, :, to] = (gate_ref[s, :, to].astype(F32) * projected).astype(BF16)


def finish(mine, theirs, gate, weight, gain, chunk, piece):
    slots, half, cells = mine.shape
    cut = pl.BlockSpec((slots, half, chunk), lambda n: (0, 0, n))
    return pl.pallas_call(
        functools.partial(finish_kernel, piece),
        grid=(cells // chunk,),
        in_specs=[
            cut,
            cut,
            cut,
            pl.BlockSpec(weight.shape, lambda n: (0, 0)),
            pl.BlockSpec(gain.shape, lambda n: (0, 0)),
        ],
        out_specs=cut,
        out_shape=jax.ShapeDtypeStruct(mine.shape, BF16),
        compiler_params=pltpu.CompilerParams(vmem_limit_bytes=VMEM_LIMIT),
        name="finish",
    )(mine, theirs, gate, weight, gain)


def per_device(
    pair,
    ln_in_gain,
    a_weight,
    b_weight,
    ln_out_gain,
    out_gate_weight,
    out_weight,
    a_slots,
    b_slots,
    counts,
):
    slots, half, cells = pair.shape
    rows = lax.axis_size("row")
    swap = [(0, 1), (1, 0)]
    chan = lax.axis_index("chan")
    core0_up = [(2 * i, 2 * ((i + 1) % rows)) for i in range(rows)]
    core0_down = [(2 * i, 2 * ((i - 1) % rows)) for i in range(rows)]
    core1_up = [(a + 1, b + 1) for a, b in core0_up]
    core1_down = [(a + 1, b + 1) for a, b in core0_down]

    a_slots, b_slots = a_slots.T, b_slots.T
    a_weight, b_weight = jnp.swapaxes(a_weight, 1, 2), jnp.swapaxes(b_weight, 1, 2)
    gain, last_gain = ln_in_gain[:, None], ln_out_gain[:, None]

    pair_other = lax.ppermute(pair, "chan", swap)
    first, second = select_blocks(pair, a_slots, b_slots, counts)
    first = lax.ppermute(first, ("row", "chan"), core0_up + core1_down)
    second = lax.ppermute(second, ("row", "chan"), core0_down + core1_up)
    weights = (a_weight, b_weight, out_gate_weight.T)
    lefts, rights, gate = project(
        [pair, pair_other, pair, pair_other], weights, gain, 1024, 256, True
    )
    first, second, lefts = lax.optimization_barrier((first, second, lefts))
    from_behind = jnp.where(chan == 0, first, second)
    from_ahead = jnp.where(chan == 0, second, first)
    behind_other = lax.ppermute(from_behind, "chan", swap)
    ahead_other = lax.ppermute(from_ahead, "chan", swap)
    lefts, rights = project(
        [from_behind, behind_other, from_ahead, ahead_other],
        weights,
        gain,
        1024,
        256,
        False,
        [lefts, rights],
    )
    update = triplet_sum(lefts, rights, a_slots, b_slots, counts, slots, 16)
    update_other = lax.ppermute(update, "chan", swap)
    return finish(update, update_other, gate, out_weight.T, last_gain, 1024, 256)


def solution(mesh):
    in_specs = (
        P(("parts", "row", "col"), "chan", None),
        P(),
        P(None, None, "chan"),
        P(None, None, "chan"),
        P(),
        P(None, "chan"),
        P(None, "chan"),
        P("parts", None),
        P("parts", None),
        P("parts"),
    )
    out_specs = P(("parts", "row", "col"), "chan", None)
    return jax.shard_map(
        per_device, mesh=mesh, in_specs=in_specs, out_specs=out_specs, check_vma=False
    )
```

```python
import functools

import jax
import jax.numpy as jnp
from jax import lax
from jax.experimental import pallas as pl
from jax.experimental.pallas import tpu as pltpu
from jax.sharding import PartitionSpec as P

BLK = 64
LANES = 128
epsilon = 1e-05
VMEM_LIMIT = 48 * 1024 * 1024
F32 = jnp.float32
BF16 = jnp.bfloat16


def sigmoid(x):
    return 0.5 * jnp.tanh(0.5 * x) + 0.5


def tile_of(row, col):
    return row * lax.axis_size("col") + col


def neighbour_tiles():
    rows = lax.axis_size("row")
    row, col = lax.axis_index("row"), lax.axis_index("col")
    behind = lax.rem(row + rows - 1, rows)
    ahead = lax.rem(row + 1, rows)
    return tile_of(row, col), tile_of(behind, col), tile_of(ahead, col)


def select_kernel(slots, triplets, cuts, a_ref, b_ref, n_ref, pair_ref, *refs):
    me, behind, ahead = neighbour_tiles()
    out_refs, sems = refs[:-1], refs[-1]
    picks = []
    for target in (ahead, behind):
        pick = jnp.int32(0)
        for s in range(slots):
            count = n_ref[target * slots + s]
            for m in range(triplets):
                for ids in (a_ref, b_ref):
                    name = ids[m, target * slots + s] - me * slots
                    mine = jnp.logical_and(name >= 0, name < slots)
                    pick = jnp.where(jnp.logical_and(m < count, mine), name, pick)
        picks.append(pick)
    copies = []
    for at, (start, size) in enumerate(cuts):
        for which, pick in enumerate(picks):
            out = 2 * at + which
            copies.append(
                pltpu.make_async_copy(
                    pair_ref.at[pick, :, pl.ds(start, size)], out_refs[out], sems.at[out]
                )
            )
            copies[-1].start()
    for copy in copies:
        copy.wait()


def select_blocks(pair, a_slots, b_slots, counts, cuts):
    slots, channels, cells = pair.shape
    smem = pl.BlockSpec(memory_space=pltpu.SMEM)
    vmem = pl.BlockSpec(memory_space=pltpu.VMEM)
    out_shape = [
        jax.ShapeDtypeStruct((channels, size), pair.dtype) for _, size in cuts for _ in range(2)
    ]
    return pl.pallas_call(
        functools.partial(select_kernel, slots, a_slots.shape[0], cuts),
        out_shape=out_shape,
        in_specs=[smem, smem, smem, pl.BlockSpec(memory_space=pltpu.HBM)],
        out_specs=[vmem] * len(out_shape),
        scratch_shapes=[pltpu.SemaphoreType.DMA((len(out_shape),))],
        name="select_blocks",
    )(a_slots, b_slots, counts, pair)


def own_lanes_first(weight):
    wide = weight.astype(F32)
    wide = jnp.where(lax.axis_index("chan") == 0, wide, pltpu.roll(wide, weight.shape[1] // 2, 1))
    return wide.astype(BF16)


def gains_of(g_ref):
    half = g_ref.shape[0] // 2
    chan = lax.axis_index("chan")
    mine = g_ref[pl.ds(pl.multiple_of(chan * half, half), half), :]
    theirs = g_ref[pl.ds(pl.multiple_of((1 - chan) * half, half), half), :]
    return mine, theirs


def normed_of(mine, theirs, gain):
    half = mine.shape[0]
    total = 2 * half
    mine = mine.astype(F32)
    theirs = theirs.astype(F32)
    mean = (jnp.sum(mine, axis=0, keepdims=True) + jnp.sum(theirs, axis=0, keepdims=True)) / total
    mine = mine - mean
    theirs = theirs - mean
    spread = (
        jnp.sum(mine * mine, axis=0, keepdims=True) + jnp.sum(theirs * theirs, axis=0, keepdims=True)
    ) / total
    scale = lax.rsqrt(spread + epsilon)
    return jnp.concatenate(
        [(mine * scale * gain[0]).astype(BF16), (theirs * scale * gain[1]).astype(BF16)],
        axis=0,
    )


def project_kernel(piece, gated, *refs):
    m0, t0, m1, t1, a_ref, b_ref, g_ref = refs[:7]
    weights = [a_ref[0], a_ref[1], b_ref[0], b_ref[1]]
    if gated:
        weights.append(refs[7][...])
        l_ref, p_ref, gate_ref, sl, sp, sq = refs[8:]
    else:
        l_ref, p_ref, sl, sp, sq = refs[9:]
    chunk = m0.shape[-1]
    half = m0.shape[-2]
    weight = own_lanes_first(jnp.concatenate(weights, axis=0))
    gain = gains_of(g_ref)
    low = lax.broadcasted_iota(jnp.int32, (half, LANES), 1) < BLK
    for start in range(0, chunk, piece):
        sides = []
        for x, (m, t) in enumerate(((m0, t0), (m1, t1))):
            normed = normed_of(m[:, start : start + piece], t[:, start : start + piece], gain)
            y = jnp.dot(weight, normed, preferred_element_type=F32)
            left = sigmoid(y[:half]) * y[half : 2 * half]
            right = sigmoid(y[2 * half : 3 * half]) * y[3 * half : 4 * half]
            sides.append((left, right))
            if gated:
                gate_ref[x, :, start : start + piece] = sigmoid(y[4 * half :]).astype(BF16)
        for sub in range(0, piece, LANES):
            i = (start + sub) // BLK
            even = pl.ds(i * half, half)
            odd = pl.ds((i + 1) * half, half)
            l0, l1 = (side[0][:, sub : sub + LANES] for side in sides)
            r0, r1 = (side[1][:, sub : sub + LANES] for side in sides)
            l0r, l1r, r0r, r1r = (pltpu.roll(v, BLK, 1) for v in (l0, l1, r0, r1))
            sl[even, :] = jnp.where(low, l0, l1r)
            sl[odd, :] = jnp.where(low, l0r, l1)
            sp[even, :] = jnp.where(low, r0, r1r)
            sp[odd, :] = jnp.where(low, r0r, r1)
            sq[even, :] = jnp.where(low, r1, r0r)
            sq[odd, :] = jnp.where(low, r1r, r0)
    rows = chunk // BLK

    @pl.loop(0, half, unroll=8)
    def _(c):
        take = pl.ds(c, rows, stride=half)
        l_ref[0, c] = sl[take, :].astype(BF16)
        p_ref[0, c] = sp[take, :].astype(BF16)
        p_ref[1, c] = sq[take, :].astype(BF16)


def project(blocks, weights, gain, chunk, piece, gated, held=None, offset=0):
    half, cells = blocks[0].shape[-2:]
    pair_of = 0 if gated else 1
    in_specs = []
    for block, at in blocks_with_index(blocks):
        if block.ndim == 3:
            in_specs.append(
                pl.BlockSpec((None, half, chunk), functools.partial(lambda x, n: (x, 0, n), at))
            )
        else:
            in_specs.append(pl.BlockSpec((half, chunk), lambda n: (0, n)))
    rows = chunk // BLK
    whole = lambda a: pl.BlockSpec(a.shape, lambda n: (0,) * a.ndim)
    operands = [*blocks, weights[0], weights[1], gain]
    if gated:
        operands.append(weights[2])
    in_specs += [whole(value) for value in operands[4:]]
    out_shape = [
        jax.ShapeDtypeStruct((2, half, BLK, LANES), BF16),
        jax.ShapeDtypeStruct((4, half, BLK, LANES), BF16),
    ]
    out_specs = [
        pl.BlockSpec((1, half, rows, LANES), lambda n: (pair_of, 0, n + offset // chunk, 0)),
        pl.BlockSpec((2, half, rows, LANES), lambda n: (pair_of, 0, n + offset // chunk, 0)),
    ]
    aliases = {}
    if gated:
        out_shape.append(jax.ShapeDtypeStruct((2, half, cells), BF16))
        out_specs.append(pl.BlockSpec((2, half, chunk), lambda n: (0, 0, n)))
    else:
        in_specs += [pl.BlockSpec(memory_space=pl.ANY)] * 2
        aliases = {len(operands): 0, len(operands) + 1: 1}
        operands += held
    return pl.pallas_call(
        functools.partial(project_kernel, piece, gated),
        grid=(cells // chunk,),
        in_specs=in_specs,
        out_specs=out_specs,
        out_shape=out_shape,
        scratch_shapes=[pltpu.VMEM((rows * half, LANES), F32)] * 3,
        input_output_aliases=aliases,
        compiler_params=pltpu.CompilerParams(vmem_limit_bytes=VMEM_LIMIT),
        cost_estimate=pl.CostEstimate(flops=1, bytes_accessed=1, transcendentals=0),
        name="project_own" if gated else "project_fetched",
    )(*operands)


def blocks_with_index(blocks):
    return [(block, at // 2) for at, block in enumerate(blocks)]


def triplet_kernel(s, slots, triplets, group, a_ref, b_ref, n_ref, l_ref, p_ref, out_ref, acc):
    me, behind, ahead = neighbour_tiles()
    lane = lax.broadcasted_iota(jnp.int32, (1, LANES), 1)
    low = (lane < BLK).astype(F32)
    high = 1.0 - low
    block = me * slots + s
    count = n_ref[block]
    picks = []
    for pair_at in range(2):
        for part in range(2):
            chosen = jnp.int32(0)
            used = jnp.int32(0)
            for m in range(triplets):
                left = a_ref[m, block]
                if pair_at == 0:
                    hit = left == me * slots + part
                else:
                    first = (behind, ahead)[part] * slots
                    hit = jnp.logical_and(left >= first, left < first + slots)
                hit = jnp.logical_and(hit, m < count)
                place = b_ref[m, block] - me * slots
                from_me = jnp.logical_and(place >= 0, place < slots)
                right = b_ref[m, block] - behind * slots
                from_behind = jnp.logical_and(right >= 0, right < slots)
                place = jnp.where(from_me, place, jnp.where(from_behind, 2, 3))
                chosen = jnp.where(hit, place, chosen)
                used = jnp.where(hit, 1, used)
            if part == 1:
                chosen = chosen + 1 - 2 * (chosen & 1)
            picks.append((chosen, ((low, high)[part] * used.astype(F32)).astype(BF16)))

    @pl.loop(0, group, unroll=8)
    def _(c):
        lhs = jnp.concatenate([l_ref[0, c], l_ref[1, c]], axis=1)
        parts = [p_ref[pick, c] * mask for pick, mask in picks]
        rhs = jnp.concatenate([parts[0] + parts[1], parts[2] + parts[3]], axis=1)
        acc[pl.ds(c, BLK, stride=group), :] = lax.dot_general(
            lhs,
            jnp.concatenate([rhs, rhs], axis=0),
            (((1,), (1,)), ((), ())),
            preferred_element_type=F32,
        )

    take_low = lax.broadcasted_iota(jnp.int32, (group, LANES), 1) < BLK
    for t in range(BLK // 2):
        even = acc[2 * t * group : (2 * t + 1) * group, :]
        odd = acc[(2 * t + 1) * group : (2 * t + 2) * group, :]
        out_ref[:, t * LANES : (t + 1) * LANES] = jnp.where(take_low, even, odd).astype(BF16)


def triplet_sum(s, lefts, rights, a_slots, b_slots, counts, slots, group):
    half = lefts.shape[1]
    smem = pl.BlockSpec(memory_space=pltpu.SMEM)
    return pl.pallas_call(
        functools.partial(triplet_kernel, s, slots, a_slots.shape[0], group),
        grid=(half // group,),
        in_specs=[
            smem,
            smem,
            smem,
            pl.BlockSpec((2, group, BLK, LANES), lambda n: (0, n, 0, 0)),
            pl.BlockSpec((4, group, BLK, LANES), lambda n: (0, n, 0, 0)),
        ],
        out_specs=pl.BlockSpec((group, BLK * BLK), lambda n: (n, 0)),
        out_shape=jax.ShapeDtypeStruct((half, BLK * BLK), BF16),
        scratch_shapes=[pltpu.VMEM((BLK * group, LANES), F32)],
        compiler_params=pltpu.CompilerParams(vmem_limit_bytes=VMEM_LIMIT),
        cost_estimate=pl.CostEstimate(
            flops=2 * half * BLK * 256 * LANES, bytes_accessed=7 * 1024 * 1024, transcendentals=0
        ),
        name="triplets",
    )(a_slots, b_slots, counts, lefts, rights)


def finish_kernel(piece, mine_ref, theirs_ref, gate_ref, w_ref, g_ref, *refs):
    out_ref = refs[-1]
    weight = own_lanes_first(w_ref[...])
    gain = gains_of(g_ref)
    for start in range(0, mine_ref.shape[-1], piece):
        to = slice(start, start + piece)
        normed = normed_of(mine_ref[:, to], theirs_ref[:, to], gain)
        projected = jnp.dot(weight, normed, preferred_element_type=F32)
        out_ref[:, to] = (gate_ref[:, to].astype(F32) * projected).astype(BF16)


def finish(s, mine, theirs, gate, weight, gain, chunk, piece, held=None):
    half, cells = mine.shape
    cut = pl.BlockSpec((half, chunk), lambda n: (0, n))
    cut_of_s = pl.BlockSpec((None, half, chunk), lambda n: (s, 0, n))
    operands = [mine, theirs, gate, weight, gain]
    in_specs = [
        cut,
        cut,
        cut_of_s,
        pl.BlockSpec(weight.shape, lambda n: (0, 0)),
        pl.BlockSpec(gain.shape, lambda n: (0, 0)),
    ]
    aliases = {}
    if held is not None:
        aliases = {len(operands): 0}
        operands.append(held)
        in_specs.append(pl.BlockSpec(memory_space=pl.ANY))
    return pl.pallas_call(
        functools.partial(finish_kernel, piece),
        grid=(cells // chunk,),
        in_specs=in_specs,
        out_specs=cut_of_s,
        out_shape=jax.ShapeDtypeStruct(gate.shape, BF16),
        input_output_aliases=aliases,
        compiler_params=pltpu.CompilerParams(vmem_limit_bytes=VMEM_LIMIT),
        cost_estimate=pl.CostEstimate(
            flops=2 * cells * 2 * half * half, bytes_accessed=4 * half * cells * 2, transcendentals=0
        ),
        name="finish",
    )(*operands)


def per_device(
    pair,
    ln_in_gain,
    a_weight,
    b_weight,
    ln_out_gain,
    out_gate_weight,
    out_weight,
    a_slots,
    b_slots,
    counts,
):
    slots, half, cells = pair.shape
    rows = lax.axis_size("row")
    swap = [(0, 1), (1, 0)]
    up = [(i, (i + 1) % rows) for i in range(rows)]
    down = [(i, (i - 1) % rows) for i in range(rows)]

    a_slots, b_slots = a_slots.T, b_slots.T
    a_weight, b_weight = jnp.swapaxes(a_weight, 1, 2), jnp.swapaxes(b_weight, 1, 2)
    weights = (a_weight, b_weight, out_gate_weight.T)
    gain, last_gain = ln_in_gain[:, None], ln_out_gain[:, None]

    pair_other = lax.ppermute(pair, "chan", swap)
    cuts = ((0, cells // 4 * 3), (cells // 4 * 3, cells // 4))
    chosen = select_blocks(pair, a_slots, b_slots, counts, cuts)
    arrived = [
        (lax.ppermute(chosen[2 * n], "row", up), lax.ppermute(chosen[2 * n + 1], "row", down))
        for n in range(len(cuts))
    ]
    lefts, rights, gate = project(
        [pair, pair_other, pair, pair_other], weights, gain, 1024, 256, True
    )
    for (start, size), (from_behind, from_ahead) in zip(cuts, arrived):
        from_behind, from_ahead, lefts = lax.optimization_barrier((from_behind, from_ahead, lefts))
        behind_other = lax.ppermute(from_behind, "chan", swap)
        ahead_other = lax.ppermute(from_ahead, "chan", swap)
        lefts, rights = project(
            [from_behind, behind_other, from_ahead, ahead_other],
            weights,
            gain,
            1024,
            256,
            False,
            [lefts, rights],
            start,
        )
    updates = []
    for s in range(slots):
        update = triplet_sum(s, lefts, rights, a_slots, b_slots, counts, slots, 16)
        updates.append((update, lax.ppermute(update, "chan", swap)))
        if s + 1 < slots:
            update, lefts = lax.optimization_barrier((update, lefts))
    out = None
    for s, (mine, theirs) in enumerate(updates):
        out = finish(s, mine, theirs, gate, out_weight.T, last_gain, 1024, 256, out)
    return out


def solution(mesh):
    in_specs = (
        P(("parts", "row", "col"), "chan", None),
        P(),
        P(None, None, "chan"),
        P(None, None, "chan"),
        P(),
        P(None, "chan"),
        P(None, "chan"),
        P("parts", None),
        P("parts", None),
        P("parts"),
    )
    out_specs = P(("parts", "row", "col"), "chan", None)
    return jax.shard_map(
        per_device, mesh=mesh, in_specs=in_specs, out_specs=out_specs, check_vma=False
    )
```

```python
import functools

import jax
import jax.numpy as jnp
from jax import lax
from jax.experimental import pallas as pl
from jax.experimental.pallas import tpu as pltpu
from jax.sharding import PartitionSpec as P

BLK = 64
LANES = 128
epsilon = 1e-05
VMEM_LIMIT = 24 * 1024 * 1024
F32 = jnp.float32
BF16 = jnp.bfloat16


def sigmoid(x):
    return 0.5 * jnp.tanh(0.5 * x) + 0.5


def tile_of(row, col):
    return row * lax.axis_size("col") + col


def neighbour_tiles():
    rows = lax.axis_size("row")
    row, col = lax.axis_index("row"), lax.axis_index("col")
    behind = lax.rem(row + rows - 1, rows)
    ahead = lax.rem(row + 1, rows)
    return tile_of(row, col), tile_of(behind, col), tile_of(ahead, col)


def select_kernel(slots, triplets, cuts, a_ref, b_ref, n_ref, pair_ref, *refs):
    me, behind, ahead = neighbour_tiles()
    out_refs, sems = refs[:-1], refs[-1]
    picks = []
    for target in (ahead, behind):
        pick = jnp.int32(0)
        for s in range(slots):
            count = n_ref[target * slots + s]
            for m in range(triplets):
                for ids in (a_ref, b_ref):
                    name = ids[m, target * slots + s] - me * slots
                    mine = jnp.logical_and(name >= 0, name < slots)
                    pick = jnp.where(jnp.logical_and(m < count, mine), name, pick)
        picks.append(pick)
    copies = []
    for at, (start, size) in enumerate(cuts):
        for which, pick in enumerate(picks):
            out = 2 * at + which
            copies.append(
                pltpu.make_async_copy(
                    pair_ref.at[pick, :, pl.ds(start, size)], out_refs[out], sems.at[out]
                )
            )
            copies[-1].start()
    for copy in copies:
        copy.wait()


def select_blocks(pair, a_slots, b_slots, counts, cuts):
    slots, channels, cells = pair.shape
    smem = pl.BlockSpec(memory_space=pltpu.SMEM)
    vmem = pl.BlockSpec(memory_space=pltpu.VMEM)
    out_shape = [
        pltpu.VMEM((channels, size), pair.dtype) for _, size in cuts for _ in range(2)
    ]
    return pl.pallas_call(
        functools.partial(select_kernel, slots, a_slots.shape[0], cuts),
        out_shape=out_shape,
        in_specs=[smem, smem, smem, pl.BlockSpec(memory_space=pltpu.HBM)],
        out_specs=[vmem] * len(out_shape),
        scratch_shapes=[pltpu.SemaphoreType.DMA((len(out_shape),))],
        name="select_blocks",
    )(a_slots, b_slots, counts, pair)


def own_lanes_first(weight):
    return jnp.where(
        lax.axis_index("chan") == 0, weight, pltpu.roll(weight, weight.shape[1] // 2, 1)
    )


def gains_of(g_ref):
    half = g_ref.shape[0] // 2
    chan = lax.axis_index("chan")
    mine = g_ref[pl.ds(pl.multiple_of(chan * half, half), half), :]
    theirs = g_ref[pl.ds(pl.multiple_of((1 - chan) * half, half), half), :]
    return mine, theirs


def normed_of(mine, theirs, gain):
    half = mine.shape[0]
    total = 2 * half
    mine = mine.astype(F32)
    theirs = theirs.astype(F32)
    mean = (jnp.sum(mine, axis=0, keepdims=True) + jnp.sum(theirs, axis=0, keepdims=True)) / total
    mine = mine - mean
    theirs = theirs - mean
    spread = (
        jnp.sum(mine * mine, axis=0, keepdims=True) + jnp.sum(theirs * theirs, axis=0, keepdims=True)
    ) / total
    scale = lax.rsqrt(spread + epsilon)
    return jnp.concatenate(
        [(mine * scale * gain[0]).astype(BF16), (theirs * scale * gain[1]).astype(BF16)],
        axis=0,
    )


def gated_rows(w_ref):
    gate, value = w_ref[0].astype(F32), w_ref[1].astype(F32)
    rows = []
    for at in range(0, gate.shape[0], 8):
        rows += [gate[at : at + 8], value[at : at + 8]]
    return [0.5 * row for row in rows]


def project_kernel(piece, chunk, offset, gated, *refs):
    if gated:
        m_ref, t_ref, a_ref, b_ref, g_ref, o_ref, l_ref, p_ref, gate_ref, sl, sp, sq = refs
        blocks = ((m_ref.at[0], t_ref.at[0]), (m_ref.at[1], t_ref.at[1]))
        rows = [0.5 * o_ref[...].astype(F32)]
        pair_of = 0
    else:
        m0, t0, m1, t1, a_ref, b_ref, g_ref, _, _, l_ref, p_ref, sl, sp, sq = refs
        blocks = ((m0, t0), (m1, t1))
        rows = []
        pair_of = 1
    half, cells = blocks[0][0].shape
    weight = jnp.concatenate(gated_rows(a_ref) + gated_rows(b_ref) + rows, axis=0)
    weight = own_lanes_first(weight).astype(BF16)
    gain = gains_of(g_ref)
    low = lax.broadcasted_iota(jnp.int32, (8, LANES), 1) < BLK
    high_rows = chunk // BLK

    @pl.loop(0, cells // chunk)
    def _(n):
        for start in range(0, chunk, piece):
            at = pl.ds(pl.multiple_of(n * chunk + start, piece), piece)
            results = []
            for x, (m, t) in enumerate(blocks):
                normed = normed_of(m[:, at], t[:, at], gain)
                y = jnp.dot(weight, normed, preferred_element_type=F32)
                results.append(y)
                if gated:
                    gate_ref[x, :, at] = (jnp.tanh(y[4 * half :]) + 1.0).astype(BF16)
            for row in range(0, half, 8):
                sides = []
                for side in range(2):
                    for y in results:
                        gate = y[2 * half * side + 2 * row : 2 * half * side + 2 * row + 8]
                        value = y[2 * half * side + 2 * row + 8 : 2 * half * side + 2 * row + 16]
                        sides.append((jnp.tanh(gate) + 1.0) * value)
                for sub in range(0, piece, LANES):
                    i = (start + sub) // BLK
                    even = slice(i * half + row, i * half + row + 8)
                    odd = slice((i + 1) * half + row, (i + 1) * half + row + 8)
                    l0, l1, r0, r1 = (v[:, sub : sub + LANES] for v in sides)
                    l0r, l1r, r0r, r1r = (pltpu.roll(v, BLK, 1) for v in (l0, l1, r0, r1))
                    sl[even, :] = jnp.where(low, l0, l1r)
                    sl[odd, :] = jnp.where(low, l0r, l1)
                    sp[even, :] = jnp.where(low, r0, r1r)
                    sp[odd, :] = jnp.where(low, r0r, r1)
                    sq[even, :] = jnp.where(low, r1, r0r)
                    sq[odd, :] = jnp.where(low, r1r, r0)

        to = pl.ds(pl.multiple_of(n * high_rows + offset // BLK, 16), high_rows)

        @pl.loop(0, half, unroll=8)
        def _(c):
            take = pl.ds(c, high_rows, stride=half)
            l_ref[pair_of, c, to, :] = sl[take, :].astype(BF16)
            p_ref[2 * pair_of, c, to, :] = sp[take, :].astype(BF16)
            p_ref[2 * pair_of + 1, c, to, :] = sq[take, :].astype(BF16)


def project(blocks, weights, gain, chunk, piece, gated, held=None, offset=0):
    half, cells = blocks[0].shape[-2:]
    operands = [*blocks, weights[0], weights[1], gain]
    out_shape = [
        pltpu.VMEM((2, half, BLK, LANES), BF16),
        pltpu.VMEM((4, half, BLK, LANES), BF16),
    ]
    aliases = {}
    if gated:
        operands.append(weights[2])
        out_shape.append(pltpu.VMEM((2, half, cells), BF16))
    else:
        aliases = {len(operands): 0, len(operands) + 1: 1}
        operands += [pltpu.with_memory_space_constraint(value, pltpu.VMEM) for value in held]
    vmem = pl.BlockSpec(memory_space=pltpu.VMEM)
    return pl.pallas_call(
        functools.partial(project_kernel, piece, chunk, offset, gated),
        in_specs=[vmem] * len(operands),
        out_specs=[vmem] * len(out_shape),
        out_shape=out_shape,
        scratch_shapes=[pltpu.VMEM((chunk // BLK * half, LANES), F32)] * 3,
        input_output_aliases=aliases,
        compiler_params=pltpu.CompilerParams(vmem_limit_bytes=VMEM_LIMIT),
        name="project_own" if gated else "project_fetched",
    )(*operands)


def triplet_kernel(s, slots, triplets, group, a_ref, b_ref, n_ref, l_ref, p_ref, out_ref, *accs):
    me, behind, ahead = neighbour_tiles()
    lane = lax.broadcasted_iota(jnp.int32, (1, LANES), 1)
    low = (lane < BLK).astype(F32)
    high = 1.0 - low
    block = me * slots + s
    count = n_ref[block]
    picks = []
    for pair_at in range(2):
        for part in range(2):
            chosen = jnp.int32(0)
            used = jnp.int32(0)
            for m in range(triplets):
                left = a_ref[m, block]
                if pair_at == 0:
                    hit = left == me * slots + part
                else:
                    first = (behind, ahead)[part] * slots
                    hit = jnp.logical_and(left >= first, left < first + slots)
                hit = jnp.logical_and(hit, m < count)
                place = b_ref[m, block] - me * slots
                from_me = jnp.logical_and(place >= 0, place < slots)
                right = b_ref[m, block] - behind * slots
                from_behind = jnp.logical_and(right >= 0, right < slots)
                place = jnp.where(from_me, place, jnp.where(from_behind, 2, 3))
                chosen = jnp.where(hit, place, chosen)
                used = jnp.where(hit, 1, used)
            if part == 1:
                chosen = chosen + 1 - 2 * (chosen & 1)
            picks.append((chosen, ((low, high)[part] * used.astype(F32)).astype(BF16)))

    take_low = lax.broadcasted_iota(jnp.int32, (group, LANES), 1) < BLK
    half = l_ref.shape[1]

    @pl.loop(0, half, step=group * len(accs))
    def _(base):
        for which, acc in enumerate(accs):
            for at in range(group):
                c = base + which * group + at
                lhs = jnp.concatenate([l_ref[0, c], l_ref[1, c]], axis=1)
                parts = [p_ref[pick, c] * mask for pick, mask in picks]
                rhs = jnp.concatenate([parts[0] + parts[1], parts[2] + parts[3]], axis=1)
                acc[pl.ds(at, BLK, stride=group), :] = lax.dot_general(
                    lhs,
                    jnp.concatenate([rhs, rhs], axis=0),
                    (((1,), (1,)), ((), ())),
                    preferred_element_type=F32,
                )
            rows = pl.ds(pl.multiple_of(base + which * group, group), group)
            for t in range(BLK // 2):
                even = acc[2 * t * group : (2 * t + 1) * group, :]
                odd = acc[(2 * t + 1) * group : (2 * t + 2) * group, :]
                out_ref[rows, t * LANES : (t + 1) * LANES] = jnp.where(
                    take_low, even, odd
                ).astype(BF16)


def triplet_sum(s, lefts, rights, a_slots, b_slots, counts, slots, group):
    half = lefts.shape[1]
    smem = pl.BlockSpec(memory_space=pltpu.SMEM)
    vmem = pl.BlockSpec(memory_space=pltpu.VMEM)
    lefts, rights = (
        pltpu.with_memory_space_constraint(value, pltpu.VMEM) for value in (lefts, rights)
    )
    return pl.pallas_call(
        functools.partial(triplet_kernel, s, slots, a_slots.shape[0], group),
        in_specs=[smem, smem, smem, vmem, vmem],
        out_specs=vmem,
        out_shape=pltpu.VMEM((half, BLK * BLK), BF16),
        scratch_shapes=[pltpu.VMEM((BLK * group, LANES), F32)] * 2,
        compiler_params=pltpu.CompilerParams(vmem_limit_bytes=VMEM_LIMIT),
        name="triplets",
    )(a_slots, b_slots, counts, lefts, rights)


def finish_kernel(s, piece, mine_ref, theirs_ref, gate_ref, w_ref, g_ref, *refs):
    out_ref, held, sems = refs[-3:]
    weight = own_lanes_first(0.5 * w_ref[...].astype(F32)).astype(BF16)
    gain = gains_of(g_ref)
    cells = mine_ref.shape[-1]
    steps = sems.shape[0]
    size = cells // steps

    def copy(n):
        to = pl.ds(pl.multiple_of(n * size, size), size)
        return pltpu.make_async_copy(held.at[:, to], out_ref.at[s, :, to], sems.at[n])

    @pl.loop(0, steps)
    def _(n):
        for start in range(0, size, piece):
            to = pl.ds(pl.multiple_of(n * size + start, piece), piece)
            normed = normed_of(mine_ref[:, to], theirs_ref[:, to], gain)
            projected = jnp.dot(weight, normed, preferred_element_type=F32)
            held[:, to] = (gate_ref[s, :, to].astype(F32) * projected).astype(BF16)
        copy(n).start()

    @pl.loop(0, steps)
    def _(n):
        copy(n).wait()


def finish(s, mine, theirs, gate, weight, gain, steps, piece, out=None):
    half, cells = mine.shape
    vmem = pl.BlockSpec(memory_space=pltpu.VMEM)
    operands = [mine, theirs, gate, weight, gain]
    in_specs = [vmem] * 5
    aliases = {}
    if out is not None:
        aliases = {len(operands): 0}
        operands.append(out)
        in_specs.append(pl.BlockSpec(memory_space=pltpu.HBM))
    return pl.pallas_call(
        functools.partial(finish_kernel, s, piece),
        in_specs=in_specs,
        out_specs=pl.BlockSpec(memory_space=pltpu.HBM),
        out_shape=jax.ShapeDtypeStruct(gate.shape, BF16),
        scratch_shapes=[pltpu.VMEM((half, cells), BF16), pltpu.SemaphoreType.DMA((steps,))],
        input_output_aliases=aliases,
        compiler_params=pltpu.CompilerParams(vmem_limit_bytes=VMEM_LIMIT),
        name="finish",
    )(*operands)


def per_device(
    pair,
    ln_in_gain,
    a_weight,
    b_weight,
    ln_out_gain,
    out_gate_weight,
    out_weight,
    a_slots,
    b_slots,
    counts,
):
    slots, half, cells = pair.shape
    rows = lax.axis_size("row")
    swap = [(0, 1), (1, 0)]
    up = [(i, (i + 1) % rows) for i in range(rows)]
    down = [(i, (i - 1) % rows) for i in range(rows)]

    a_slots, b_slots = a_slots.T, b_slots.T
    a_weight, b_weight = jnp.swapaxes(a_weight, 1, 2), jnp.swapaxes(b_weight, 1, 2)
    weights = (a_weight, b_weight, out_gate_weight.T)
    gain, last_gain = ln_in_gain[:, None], ln_out_gain[:, None]

    pair_other = lax.ppermute(pair, "chan", swap)
    cuts = ((0, cells // 4 * 3), (cells // 4 * 3, cells // 4))
    chosen = select_blocks(pair, a_slots, b_slots, counts, cuts)
    arrived = [
        (lax.ppermute(chosen[2 * n], "row", up), lax.ppermute(chosen[2 * n + 1], "row", down))
        for n in range(len(cuts))
    ]
    lefts, rights, gate = project(
        [pair, pair_other], weights, gain, 1024, 256, True
    )
    for (start, size), (from_behind, from_ahead) in zip(cuts, arrived):
        from_behind, from_ahead, lefts = lax.optimization_barrier((from_behind, from_ahead, lefts))
        behind_other = lax.ppermute(from_behind, "chan", swap)
        ahead_other = lax.ppermute(from_ahead, "chan", swap)
        lefts, rights = project(
            [from_behind, behind_other, from_ahead, ahead_other],
            weights,
            gain,
            1024,
            256,
            False,
            [lefts, rights],
            start,
        )
    updates = []
    for s in range(slots):
        update = triplet_sum(s, lefts, rights, a_slots, b_slots, counts, slots, 16)
        updates.append((update, lax.ppermute(update, "chan", swap)))
        if s + 1 < slots:
            update, lefts = lax.optimization_barrier((update, lefts))
    out = None
    for s, (mine, theirs) in enumerate(updates):
        out = finish(s, mine, theirs, gate, out_weight.T, last_gain, 4, 256, out)
    return out


def solution(mesh):
    in_specs = (
        P(("parts", "row", "col"), "chan", None),
        P(),
        P(None, None, "chan"),
        P(None, None, "chan"),
        P(),
        P(None, "chan"),
        P(None, "chan"),
        P("parts", None),
        P("parts", None),
        P("parts"),
    )
    out_specs = P(("parts", "row", "col"), "chan", None)
    return jax.shard_map(
        per_device, mesh=mesh, in_specs=in_specs, out_specs=out_specs, check_vma=False
    )
```

```python
import functools

import jax
import jax.numpy as jnp
from jax import lax
from jax.experimental import pallas as pl
from jax.experimental.pallas import tpu as pltpu
from jax.sharding import PartitionSpec as P

BLK = 64
LANES = 128
epsilon = 1e-05
VMEM_LIMIT = 24 * 1024 * 1024
F32 = jnp.float32
BF16 = jnp.bfloat16


def sigmoid(x):
    return 0.5 * jnp.tanh(0.5 * x) + 0.5


def tile_of(row, col):
    return row * lax.axis_size("col") + col


def neighbour_tiles():
    rows = lax.axis_size("row")
    row, col = lax.axis_index("row"), lax.axis_index("col")
    behind = lax.rem(row + rows - 1, rows)
    ahead = lax.rem(row + 1, rows)
    return tile_of(row, col), tile_of(behind, col), tile_of(ahead, col)


def select_kernel(slots, triplets, cuts, a_ref, b_ref, n_ref, pair_ref, *refs):
    me, behind, ahead = neighbour_tiles()
    out_refs, sems = refs[:-1], refs[-1]
    picks = []
    for target in (ahead, behind):
        pick = jnp.int32(0)
        for s in range(slots):
            count = n_ref[target * slots + s]
            for m in range(triplets):
                for ids in (a_ref, b_ref):
                    name = ids[m, target * slots + s] - me * slots
                    mine = jnp.logical_and(name >= 0, name < slots)
                    pick = jnp.where(jnp.logical_and(m < count, mine), name, pick)
        picks.append(pick)
    copies = []
    for at, (start, size) in enumerate(cuts):
        for which, pick in enumerate(picks):
            out = 2 * at + which
            copies.append(
                pltpu.make_async_copy(
                    pair_ref.at[pick, :, pl.ds(start, size)], out_refs[out], sems.at[out]
                )
            )
            copies[-1].start()
    for copy in copies:
        copy.wait()


def select_blocks(pair, a_slots, b_slots, counts, cuts):
    slots, channels, cells = pair.shape
    smem = pl.BlockSpec(memory_space=pltpu.SMEM)
    vmem = pl.BlockSpec(memory_space=pltpu.VMEM)
    out_shape = [
        pltpu.VMEM((channels, size), pair.dtype) for _, size in cuts for _ in range(2)
    ]
    return pl.pallas_call(
        functools.partial(select_kernel, slots, a_slots.shape[0], cuts),
        out_shape=out_shape,
        in_specs=[smem, smem, smem, pl.BlockSpec(memory_space=pltpu.HBM)],
        out_specs=[vmem] * len(out_shape),
        scratch_shapes=[pltpu.SemaphoreType.DMA((len(out_shape),))],
        name="select_blocks",
    )(a_slots, b_slots, counts, pair)


def own_lanes_first(weight):
    return jnp.where(
        lax.axis_index("chan") == 0, weight, pltpu.roll(weight, weight.shape[1] // 2, 1)
    )


def gains_of(g_ref):
    half = g_ref.shape[0] // 2
    chan = lax.axis_index("chan")
    mine = g_ref[pl.ds(pl.multiple_of(chan * half, half), half), :]
    theirs = g_ref[pl.ds(pl.multiple_of((1 - chan) * half, half), half), :]
    return mine, theirs


def normed_of(mine, theirs, gain):
    half = mine.shape[0]
    total = 2 * half
    mine = mine.astype(F32)
    theirs = theirs.astype(F32)
    mean = (jnp.sum(mine, axis=0, keepdims=True) + jnp.sum(theirs, axis=0, keepdims=True)) / total
    mine = mine - mean
    theirs = theirs - mean
    spread = (
        jnp.sum(mine * mine, axis=0, keepdims=True) + jnp.sum(theirs * theirs, axis=0, keepdims=True)
    ) / total
    scale = lax.rsqrt(spread + epsilon)
    return jnp.concatenate(
        [(mine * scale * gain[0]).astype(BF16), (theirs * scale * gain[1]).astype(BF16)],
        axis=0,
    )


def gated_rows(w_ref):
    gate, value = w_ref[0].astype(F32), w_ref[1].astype(F32)
    rows = []
    for at in range(0, gate.shape[0], 8):
        rows += [gate[at : at + 8], value[at : at + 8]]
    return [0.5 * row for row in rows]


def project_kernel(piece, chunk, offset, gated, *refs):
    if gated:
        m_ref, t_ref, a_ref, b_ref, g_ref, o_ref, l_ref, p_ref, gate_ref, sl, sp, sq = refs
        blocks = ((m_ref.at[0], t_ref.at[0]), (m_ref.at[1], t_ref.at[1]))
        rows = [0.5 * o_ref[...].astype(F32)]
        pair_of = 0
    else:
        m0, t0, m1, t1, a_ref, b_ref, g_ref, _, _, l_ref, p_ref, sl, sp, sq = refs
        blocks = ((m0, t0), (m1, t1))
        rows = []
        pair_of = 1
    half, cells = blocks[0][0].shape
    weight = jnp.concatenate(gated_rows(a_ref) + gated_rows(b_ref) + rows, axis=0)
    weight = own_lanes_first(weight).astype(BF16)
    gain = gains_of(g_ref)
    low = lax.broadcasted_iota(jnp.int32, (8, LANES), 1) < BLK
    high_rows = chunk // BLK

    @pl.loop(0, cells // chunk)
    def _(n):
        for start in range(0, chunk, piece):
            at = pl.ds(pl.multiple_of(n * chunk + start, piece), piece)
            results = []
            for x, (m, t) in enumerate(blocks):
                normed = normed_of(m[:, at], t[:, at], gain)
                y = jnp.dot(weight, normed, preferred_element_type=F32)
                results.append(y)
                if gated:
                    gate_ref[x, :, at] = (jnp.tanh(y[4 * half :]) + 1.0).astype(BF16)
            for row in range(0, half, 8):
                sides = []
                for side in range(2):
                    for y in results:
                        gate = y[2 * half * side + 2 * row : 2 * half * side + 2 * row + 8]
                        value = y[2 * half * side + 2 * row + 8 : 2 * half * side + 2 * row + 16]
                        sides.append((jnp.tanh(gate) + 1.0) * value)
                for sub in range(0, piece, LANES):
                    i = (start + sub) // BLK
                    even = slice(i * half + row, i * half + row + 8)
                    odd = slice((i + 1) * half + row, (i + 1) * half + row + 8)
                    l0, l1, r0, r1 = (v[:, sub : sub + LANES] for v in sides)
                    l0r, l1r, r0r, r1r = (pltpu.roll(v, BLK, 1) for v in (l0, l1, r0, r1))
                    sl[even, :] = jnp.where(low, l0, l1r)
                    sl[odd, :] = jnp.where(low, l0r, l1)
                    sp[even, :] = jnp.where(low, r0, r1r)
                    sp[odd, :] = jnp.where(low, r0r, r1)
                    sq[even, :] = jnp.where(low, r1, r0r)
                    sq[odd, :] = jnp.where(low, r1r, r0)

        to = pl.ds(pl.multiple_of(n * high_rows + offset // BLK, 16), high_rows)

        @pl.loop(0, half, unroll=8)
        def _(c):
            take = pl.ds(c, high_rows, stride=half)
            l_ref[pair_of, c, to, :] = sl[take, :].astype(BF16)
            p_ref[2 * pair_of, c, to, :] = sp[take, :].astype(BF16)
            p_ref[2 * pair_of + 1, c, to, :] = sq[take, :].astype(BF16)


def project(blocks, weights, gain, chunk, piece, gated, held=None, offset=0):
    half, cells = blocks[0].shape[-2:]
    operands = [*blocks, weights[0], weights[1], gain]
    out_shape = [
        pltpu.VMEM((2, half, BLK, LANES), BF16),
        pltpu.VMEM((4, half, BLK, LANES), BF16),
    ]
    aliases = {}
    if gated:
        operands.append(weights[2])
        out_shape.append(pltpu.VMEM((2, half, cells), BF16))
    else:
        aliases = {len(operands): 0, len(operands) + 1: 1}
        operands += [pltpu.with_memory_space_constraint(value, pltpu.VMEM) for value in held]
    vmem = pl.BlockSpec(memory_space=pltpu.VMEM)
    return pl.pallas_call(
        functools.partial(project_kernel, piece, chunk, offset, gated),
        in_specs=[vmem] * len(operands),
        out_specs=[vmem] * len(out_shape),
        out_shape=out_shape,
        scratch_shapes=[pltpu.VMEM((chunk // BLK * half, LANES), F32)] * 3,
        input_output_aliases=aliases,
        compiler_params=pltpu.CompilerParams(vmem_limit_bytes=VMEM_LIMIT),
        name="project_own" if gated else "project_fetched",
    )(*operands)


def triplet_kernel(s, slots, triplets, group, a_ref, b_ref, n_ref, l_ref, p_ref, out_ref, *accs):
    me, behind, ahead = neighbour_tiles()
    lane = lax.broadcasted_iota(jnp.int32, (1, LANES), 1)
    low = (lane < BLK).astype(F32)
    high = 1.0 - low
    block = me * slots + s
    count = n_ref[block]
    picks = []
    for pair_at in range(2):
        for part in range(2):
            chosen = jnp.int32(0)
            used = jnp.int32(0)
            for m in range(triplets):
                left = a_ref[m, block]
                if pair_at == 0:
                    hit = left == me * slots + part
                else:
                    first = (behind, ahead)[part] * slots
                    hit = jnp.logical_and(left >= first, left < first + slots)
                hit = jnp.logical_and(hit, m < count)
                place = b_ref[m, block] - me * slots
                from_me = jnp.logical_and(place >= 0, place < slots)
                right = b_ref[m, block] - behind * slots
                from_behind = jnp.logical_and(right >= 0, right < slots)
                place = jnp.where(from_me, place, jnp.where(from_behind, 2, 3))
                chosen = jnp.where(hit, place, chosen)
                used = jnp.where(hit, 1, used)
            if part == 1:
                chosen = chosen + 1 - 2 * (chosen & 1)
            picks.append((chosen, ((low, high)[part] * used.astype(F32)).astype(BF16)))

    take_low = lax.broadcasted_iota(jnp.int32, (group, LANES), 1) < BLK
    half = l_ref.shape[1]

    @pl.loop(0, half, step=group * len(accs))
    def _(base):
        for which, acc in enumerate(accs):
            for at in range(group):
                c = base + which * group + at
                lhs = jnp.concatenate([l_ref[0, c], l_ref[1, c]], axis=1)
                parts = [p_ref[pick, c] * mask for pick, mask in picks]
                rhs = jnp.concatenate([parts[0] + parts[1], parts[2] + parts[3]], axis=1)
                acc[pl.ds(at, BLK, stride=group), :] = lax.dot_general(
                    lhs,
                    jnp.concatenate([rhs, rhs], axis=0),
                    (((1,), (1,)), ((), ())),
                    preferred_element_type=F32,
                )
            rows = pl.ds(pl.multiple_of(base + which * group, group), group)
            for t in range(BLK // 2):
                even = acc[2 * t * group : (2 * t + 1) * group, :]
                odd = acc[(2 * t + 1) * group : (2 * t + 2) * group, :]
                out_ref[rows, t * LANES : (t + 1) * LANES] = jnp.where(
                    take_low, even, odd
                ).astype(BF16)


def triplet_sum(s, lefts, rights, a_slots, b_slots, counts, slots, group):
    half = lefts.shape[1]
    smem = pl.BlockSpec(memory_space=pltpu.SMEM)
    vmem = pl.BlockSpec(memory_space=pltpu.VMEM)
    lefts, rights = (
        pltpu.with_memory_space_constraint(value, pltpu.VMEM) for value in (lefts, rights)
    )
    return pl.pallas_call(
        functools.partial(triplet_kernel, s, slots, a_slots.shape[0], group),
        in_specs=[smem, smem, smem, vmem, vmem],
        out_specs=vmem,
        out_shape=pltpu.VMEM((half, BLK * BLK), BF16),
        scratch_shapes=[pltpu.VMEM((BLK * group, LANES), F32)] * 2,
        compiler_params=pltpu.CompilerParams(vmem_limit_bytes=VMEM_LIMIT),
        name="triplets",
    )(a_slots, b_slots, counts, lefts, rights)


def finish_kernel(s, piece, mine_ref, theirs_ref, gate_ref, w_ref, g_ref, *refs):
    out_ref, held, sems = refs[-3:]
    weight = own_lanes_first(0.5 * w_ref[...].astype(F32)).astype(BF16)
    gain = gains_of(g_ref)
    cells = mine_ref.shape[-1]
    steps = sems.shape[0]
    size = cells // steps

    def copy(n):
        to = pl.ds(pl.multiple_of(n * size, size), size)
        return pltpu.make_async_copy(held.at[:, to], out_ref.at[s, :, to], sems.at[n])

    @pl.loop(0, steps)
    def _(n):
        for start in range(0, size, piece):
            to = pl.ds(pl.multiple_of(n * size + start, piece), piece)
            normed = normed_of(mine_ref[:, to], theirs_ref[:, to], gain)
            projected = jnp.dot(weight, normed, preferred_element_type=F32)
            held[:, to] = (gate_ref[s, :, to].astype(F32) * projected).astype(BF16)
        copy(n).start()

    @pl.loop(0, steps)
    def _(n):
        copy(n).wait()


def finish(s, mine, theirs, gate, weight, gain, steps, piece, out=None):
    half, cells = mine.shape
    vmem = pl.BlockSpec(memory_space=pltpu.VMEM)
    operands = [mine, theirs, gate, weight, gain]
    in_specs = [vmem] * 5
    aliases = {}
    if out is not None:
        aliases = {len(operands): 0}
        operands.append(out)
        in_specs.append(pl.BlockSpec(memory_space=pltpu.HBM))
    return pl.pallas_call(
        functools.partial(finish_kernel, s, piece),
        in_specs=in_specs,
        out_specs=pl.BlockSpec(memory_space=pltpu.HBM),
        out_shape=jax.ShapeDtypeStruct(gate.shape, BF16),
        scratch_shapes=[pltpu.VMEM((half, cells), BF16), pltpu.SemaphoreType.DMA((steps,))],
        input_output_aliases=aliases,
        compiler_params=pltpu.CompilerParams(vmem_limit_bytes=VMEM_LIMIT),
        name="finish",
    )(*operands)


def per_device(
    pair,
    ln_in_gain,
    a_weight,
    b_weight,
    ln_out_gain,
    out_gate_weight,
    out_weight,
    a_slots,
    b_slots,
    counts,
):
    slots, half, cells = pair.shape
    rows = lax.axis_size("row")
    swap = [(0, 1), (1, 0)]
    up = [(i, (i + 1) % rows) for i in range(rows)]
    down = [(i, (i - 1) % rows) for i in range(rows)]

    a_slots, b_slots = a_slots.T, b_slots.T
    a_weight, b_weight = jnp.swapaxes(a_weight, 1, 2), jnp.swapaxes(b_weight, 1, 2)
    weights = (a_weight, b_weight, out_gate_weight.T)
    gain, last_gain = ln_in_gain[:, None], ln_out_gain[:, None]

    pair_other = lax.ppermute(pair, "chan", swap)
    cuts = ((0, cells // 4 * 3), (cells // 4 * 3, cells // 4))
    chosen = select_blocks(pair, a_slots, b_slots, counts, cuts)
    arrived = [
        (lax.ppermute(chosen[2 * n], "row", up), lax.ppermute(chosen[2 * n + 1], "row", down))
        for n in range(len(cuts))
    ]
    lefts, rights, gate = project(
        [pair, pair_other], weights, gain, 1024, 1024, True
    )
    for (start, size), (from_behind, from_ahead) in zip(cuts, arrived):
        from_behind, from_ahead, lefts = lax.optimization_barrier((from_behind, from_ahead, lefts))
        behind_other = lax.ppermute(from_behind, "chan", swap)
        ahead_other = lax.ppermute(from_ahead, "chan", swap)
        lefts, rights = project(
            [from_behind, behind_other, from_ahead, ahead_other],
            weights,
            gain,
            1024,
            512 if start == 0 else 128,
            False,
            [lefts, rights],
            start,
        )
    updates = []
    for s in range(slots):
        update = triplet_sum(s, lefts, rights, a_slots, b_slots, counts, slots, 16)
        updates.append((update, lax.ppermute(update, "chan", swap)))
        if s + 1 < slots:
            update, lefts = lax.optimization_barrier((update, lefts))
    out = None
    for s, (mine, theirs) in enumerate(updates):
        out = finish(s, mine, theirs, gate, out_weight.T, last_gain, 4, (1024, 512)[s % 2], out)
    return out


def solution(mesh):
    in_specs = (
        P(("parts", "row", "col"), "chan", None),
        P(),
        P(None, None, "chan"),
        P(None, None, "chan"),
        P(),
        P(None, "chan"),
        P(None, "chan"),
        P("parts", None),
        P("parts", None),
        P("parts"),
    )
    out_specs = P(("parts", "row", "col"), "chan", None)
    return jax.shard_map(
        per_device, mesh=mesh, in_specs=in_specs, out_specs=out_specs, check_vma=False
    )
```

```python
import functools

import jax
import jax.numpy as jnp
from jax import lax
from jax.experimental import pallas as pl
from jax.experimental.pallas import tpu as pltpu
from jax.sharding import PartitionSpec as P

BLK = 64
LANES = 128
epsilon = 1e-05
VMEM_LIMIT = 24 * 1024 * 1024
F32 = jnp.float32
BF16 = jnp.bfloat16


def sigmoid(x):
    return 0.5 * jnp.tanh(0.5 * x) + 0.5


def tile_of(row, col):
    return row * lax.axis_size("col") + col


def neighbour_tiles():
    rows = lax.axis_size("row")
    row, col = lax.axis_index("row"), lax.axis_index("col")
    behind = lax.rem(row + rows - 1, rows)
    ahead = lax.rem(row + 1, rows)
    return tile_of(row, col), tile_of(behind, col), tile_of(ahead, col)


def select_kernel(slots, triplets, cuts, a_ref, b_ref, n_ref, pair_ref, *refs):
    me, behind, ahead = neighbour_tiles()
    out_refs, sems = refs[:-1], refs[-1]
    picks = []
    for target in (ahead, behind):
        pick = jnp.int32(0)
        for s in range(slots):
            count = n_ref[target * slots + s]
            for m in range(triplets):
                for ids in (a_ref, b_ref):
                    name = ids[m, target * slots + s] - me * slots
                    mine = jnp.logical_and(name >= 0, name < slots)
                    pick = jnp.where(jnp.logical_and(m < count, mine), name, pick)
        picks.append(pick)
    copies = []
    for at, (start, size) in enumerate(cuts):
        for which, pick in enumerate(picks):
            out = 2 * at + which
            copies.append(
                pltpu.make_async_copy(
                    pair_ref.at[pick, :, pl.ds(start, size)], out_refs[out], sems.at[out]
                )
            )
            copies[-1].start()
    for copy in copies:
        copy.wait()


def select_blocks(pair, a_slots, b_slots, counts, cuts):
    slots, channels, cells = pair.shape
    smem = pl.BlockSpec(memory_space=pltpu.SMEM)
    vmem = pl.BlockSpec(memory_space=pltpu.VMEM)
    out_shape = [
        pltpu.VMEM((channels, size), pair.dtype) for _, size in cuts for _ in range(2)
    ]
    return pl.pallas_call(
        functools.partial(select_kernel, slots, a_slots.shape[0], cuts),
        out_shape=out_shape,
        in_specs=[smem, smem, smem, pl.BlockSpec(memory_space=pltpu.HBM)],
        out_specs=[vmem] * len(out_shape),
        scratch_shapes=[pltpu.SemaphoreType.DMA((len(out_shape),))],
        name="select_blocks",
    )(a_slots, b_slots, counts, pair)


def prepared(weight, gain):
    weight = weight * gain
    weight = weight - jnp.mean(weight, axis=1, keepdims=True)
    rolled = pltpu.roll(weight, weight.shape[1] // 2, 1)
    return jnp.where(lax.axis_index("chan") == 0, weight, rolled).astype(BF16)


def gated_rows(w_ref):
    gate, value = w_ref[0].astype(F32), w_ref[1].astype(F32)
    rows = []
    for at in range(0, gate.shape[0], 8):
        rows += [gate[at : at + 8], value[at : at + 8]]
    return [0.5 * row for row in rows]


def repeated(value, times):
    return jnp.concatenate([value] * times, axis=0)


def centred_of(mine, theirs):
    values = jnp.concatenate([mine, theirs], axis=0)
    channels = values.shape[0]
    ones = jnp.full((16, channels), 1.0 / channels, BF16)
    mean = jnp.dot(ones, values, preferred_element_type=F32)
    rounded = mean.astype(BF16)
    centred = values - repeated(rounded, channels // 16)
    square = jnp.dot(ones, centred * centred, preferred_element_type=F32)
    left = mean - rounded.astype(F32)
    spread = jnp.maximum(square - left * left, 0.0)
    return centred, lax.rsqrt(spread + epsilon)


def project_kernel(piece, chunk, offset, gated, *refs):
    if gated:
        m_ref, t_ref, a_ref, b_ref, o_ref, u_ref, g_ref, h_ref = refs[:8]
        l_ref, p_ref, gate_ref, w_ref, v_ref, sl, sp = refs[8:]
        blocks = ((m_ref.at[0], t_ref.at[0]), (m_ref.at[1], t_ref.at[1]))
        rows = gated_rows(a_ref) + gated_rows(b_ref) + [0.5 * o_ref[...].astype(F32)]
        weight = prepared(jnp.concatenate(rows, axis=0), g_ref[...])
        pair_of = 0
    else:
        m0, t0, m1, t1, w_ref, _, _, l_ref, p_ref, sl, sp = refs
        blocks = ((m0, t0), (m1, t1))
        weight = w_ref[...]
        pair_of = 1
    half, cells = blocks[0][0].shape
    if gated:
        w_ref[...] = weight[: 4 * half]
        v_ref[...] = prepared(0.5 * u_ref[...].astype(F32), h_ref[...])
    low = lax.broadcasted_iota(jnp.int32, (8, LANES), 1) < BLK
    high_rows = chunk // BLK

    @pl.loop(0, cells // chunk)
    def _(n):
        for start in range(0, chunk, piece):
            at = pl.ds(pl.multiple_of(n * chunk + start, piece), piece)
            results = []
            for x, (m, t) in enumerate(blocks):
                centred, scale = centred_of(m[:, at], t[:, at])
                normed = centred * repeated(scale.astype(BF16), 2 * half // 16)
                y = jnp.dot(weight, normed, preferred_element_type=F32)
                results.append(y)
                if gated:
                    gate_ref[x, :, at] = (jnp.tanh(y[4 * half :]) + 1.0).astype(BF16)
            for row in range(0, half, 8):
                sides = []
                for side in range(2):
                    for y in results:
                        gate = y[2 * half * side + 2 * row : 2 * half * side + 2 * row + 8]
                        value = y[2 * half * side + 2 * row + 8 : 2 * half * side + 2 * row + 16]
                        sides.append((jnp.tanh(gate) + 1.0) * value)
                for sub in range(0, piece, LANES):
                    i = (start + sub) // BLK
                    even = slice(i * half + row, i * half + row + 8)
                    odd = slice((i + 1) * half + row, (i + 1) * half + row + 8)
                    l0, l1, r0, r1 = (v[:, sub : sub + LANES] for v in sides)
                    l0r, l1r, r0r, r1r = (pltpu.roll(v, BLK, 1) for v in (l0, l1, r0, r1))
                    sl[even, :] = jnp.where(low, l0, l1r)
                    sl[odd, :] = jnp.where(low, l0r, l1)
                    sp[even, :] = jnp.where(low, r0, r1r)
                    sp[odd, :] = jnp.where(low, r0r, r1)

        to = pl.ds(pl.multiple_of(n * high_rows + offset // BLK, 16), high_rows)

        @pl.loop(0, half, unroll=8)
        def _(c):
            take = pl.ds(c, high_rows, stride=half)
            l_ref[pair_of, c, to, :] = sl[take, :].astype(BF16)
            right = sp[take, :].astype(BF16)
            p_ref[2 * pair_of, c, to, :] = right
            p_ref[2 * pair_of + 1, c, to, :] = pltpu.roll(right, BLK, 1)


def project(operands, half, cells, chunk, piece, gated, offset=0):
    out_shape = [
        pltpu.VMEM((2, half, BLK, LANES), BF16),
        pltpu.VMEM((4, half, BLK, LANES), BF16),
    ]
    aliases = {}
    if gated:
        out_shape += [
            pltpu.VMEM((2, half, cells), BF16),
            pltpu.VMEM((4 * half, 2 * half), BF16),
            pltpu.VMEM((half, 2 * half), BF16),
        ]
    else:
        aliases = {len(operands) - 2: 0, len(operands) - 1: 1}
        operands = operands[:-2] + [
            pltpu.with_memory_space_constraint(value, pltpu.VMEM) for value in operands[-2:]
        ]
    vmem = pl.BlockSpec(memory_space=pltpu.VMEM)
    return pl.pallas_call(
        functools.partial(project_kernel, piece, chunk, offset, gated),
        in_specs=[vmem] * len(operands),
        out_specs=[vmem] * len(out_shape),
        out_shape=out_shape,
        scratch_shapes=[pltpu.VMEM((chunk // BLK * half, LANES), F32)] * 2,
        input_output_aliases=aliases,
        compiler_params=pltpu.CompilerParams(vmem_limit_bytes=VMEM_LIMIT),
        name="project_own" if gated else "project_fetched",
    )(*operands)


def triplet_kernel(s, slots, triplets, group, a_ref, b_ref, n_ref, l_ref, p_ref, out_ref, *accs):
    me, behind, ahead = neighbour_tiles()
    lane = lax.broadcasted_iota(jnp.int32, (1, LANES), 1)
    low = (lane < BLK).astype(F32)
    high = 1.0 - low
    block = me * slots + s
    count = n_ref[block]
    picks = []
    for pair_at in range(2):
        for part in range(2):
            chosen = jnp.int32(0)
            used = jnp.int32(0)
            for m in range(triplets):
                left = a_ref[m, block]
                if pair_at == 0:
                    hit = left == me * slots + part
                else:
                    first = (behind, ahead)[part] * slots
                    hit = jnp.logical_and(left >= first, left < first + slots)
                hit = jnp.logical_and(hit, m < count)
                place = b_ref[m, block] - me * slots
                from_me = jnp.logical_and(place >= 0, place < slots)
                right = b_ref[m, block] - behind * slots
                from_behind = jnp.logical_and(right >= 0, right < slots)
                place = jnp.where(from_me, place, jnp.where(from_behind, 2, 3))
                chosen = jnp.where(hit, place, chosen)
                used = jnp.where(hit, 1, used)
            if part == 1:
                chosen = chosen + 1 - 2 * (chosen & 1)
            picks.append((chosen, ((low, high)[part] * used.astype(F32)).astype(BF16)))

    take_low = lax.broadcasted_iota(jnp.int32, (group, LANES), 1) < BLK
    half = l_ref.shape[1]

    @pl.loop(0, half, step=group * len(accs))
    def _(base):
        for which, acc in enumerate(accs):
            for at in range(group):
                c = base + which * group + at
                lhs = jnp.concatenate([l_ref[0, c], l_ref[1, c]], axis=1)
                parts = [p_ref[pick, c] * mask for pick, mask in picks]
                rhs = jnp.concatenate([parts[0] + parts[1], parts[2] + parts[3]], axis=1)
                acc[pl.ds(at, BLK, stride=group), :BLK] = lax.dot_general(
                    lhs, rhs, (((1,), (1,)), ((), ())), preferred_element_type=F32
                )
            rows = pl.ds(pl.multiple_of(base + which * group, group), group)
            for t in range(BLK // 2):
                even = acc[2 * t * group : (2 * t + 1) * group, :]
                odd = acc[(2 * t + 1) * group : (2 * t + 2) * group, :]
                out_ref[rows, t * LANES : (t + 1) * LANES] = jnp.where(
                    take_low, even, pltpu.roll(odd, BLK, 1)
                ).astype(BF16)


def triplet_sum(s, lefts, rights, a_slots, b_slots, counts, slots, group):
    half = lefts.shape[1]
    smem = pl.BlockSpec(memory_space=pltpu.SMEM)
    vmem = pl.BlockSpec(memory_space=pltpu.VMEM)
    lefts, rights = (
        pltpu.with_memory_space_constraint(value, pltpu.VMEM) for value in (lefts, rights)
    )
    return pl.pallas_call(
        functools.partial(triplet_kernel, s, slots, a_slots.shape[0], group),
        in_specs=[smem, smem, smem, vmem, vmem],
        out_specs=vmem,
        out_shape=pltpu.VMEM((half, BLK * BLK), BF16),
        scratch_shapes=[pltpu.VMEM((BLK * group, LANES), F32)] * 2,
        compiler_params=pltpu.CompilerParams(vmem_limit_bytes=VMEM_LIMIT),
        name="triplets",
    )(a_slots, b_slots, counts, lefts, rights)


def finish_kernel(s, piece, mine_ref, theirs_ref, gate_ref, w_ref, *refs):
    out_ref, held, sems = refs[-3:]
    weight = w_ref[...]
    cells = mine_ref.shape[-1]
    steps = sems.shape[0]
    size = cells // steps

    def copy(n):
        to = pl.ds(pl.multiple_of(n * size, size), size)
        return pltpu.make_async_copy(held.at[:, to], out_ref.at[s, :, to], sems.at[n])

    @pl.loop(0, steps)
    def _(n):
        for start in range(0, size, piece):
            to = pl.ds(pl.multiple_of(n * size + start, piece), piece)
            centred, scale = centred_of(mine_ref[:, to], theirs_ref[:, to])
            projected = jnp.dot(weight, centred, preferred_element_type=F32)
            scaled = projected * repeated(scale[:8], weight.shape[0] // 8)
            held[:, to] = (gate_ref[s, :, to].astype(F32) * scaled).astype(BF16)
        copy(n).start()

    @pl.loop(0, steps)
    def _(n):
        copy(n).wait()


def finish(s, mine, theirs, gate, weight, steps, piece, out=None):
    half, cells = mine.shape
    vmem = pl.BlockSpec(memory_space=pltpu.VMEM)
    operands = [mine, theirs, gate, weight]
    in_specs = [vmem] * 4
    aliases = {}
    if out is not None:
        aliases = {len(operands): 0}
        operands.append(out)
        in_specs.append(pl.BlockSpec(memory_space=pltpu.HBM))
    return pl.pallas_call(
        functools.partial(finish_kernel, s, piece),
        in_specs=in_specs,
        out_specs=pl.BlockSpec(memory_space=pltpu.HBM),
        out_shape=jax.ShapeDtypeStruct(gate.shape, BF16),
        scratch_shapes=[pltpu.VMEM((half, cells), BF16), pltpu.SemaphoreType.DMA((steps,))],
        input_output_aliases=aliases,
        compiler_params=pltpu.CompilerParams(vmem_limit_bytes=VMEM_LIMIT),
        name="finish",
    )(*operands)


def per_device(
    pair,
    ln_in_gain,
    a_weight,
    b_weight,
    ln_out_gain,
    out_gate_weight,
    out_weight,
    a_slots,
    b_slots,
    counts,
):
    slots, half, cells = pair.shape
    rows = lax.axis_size("row")
    swap = [(0, 1), (1, 0)]
    up = [(i, (i + 1) % rows) for i in range(rows)]
    down = [(i, (i - 1) % rows) for i in range(rows)]

    a_slots, b_slots = a_slots.T, b_slots.T
    weights = [
        jnp.swapaxes(a_weight, 1, 2),
        jnp.swapaxes(b_weight, 1, 2),
        out_gate_weight.T,
        out_weight.T,
        ln_in_gain[None, :],
        ln_out_gain[None, :],
    ]

    pair_other = lax.ppermute(pair, "chan", swap)
    cuts = ((0, cells // 4 * 3), (cells // 4 * 3, cells // 4))
    chosen = select_blocks(pair, a_slots, b_slots, counts, cuts)
    arrived = [
        (lax.ppermute(chosen[2 * n], "row", up), lax.ppermute(chosen[2 * n + 1], "row", down))
        for n in range(len(cuts))
    ]
    lefts, rights, gate, weight, last_weight = project(
        [pair, pair_other, *weights], half, cells, 1024, 256, True
    )
    for (start, size), (from_behind, from_ahead) in zip(cuts, arrived):
        from_behind, from_ahead, lefts = lax.optimization_barrier((from_behind, from_ahead, lefts))
        behind_other = lax.ppermute(from_behind, "chan", swap)
        ahead_other = lax.ppermute(from_ahead, "chan", swap)
        lefts, rights = project(
            [from_behind, behind_other, from_ahead, ahead_other, weight, lefts, rights],
            half,
            size,
            1024,
            256,
            False,
            start,
        )
    updates = []
    for s in range(slots):
        update = triplet_sum(s, lefts, rights, a_slots, b_slots, counts, slots, 16)
        updates.append((update, lax.ppermute(update, "chan", swap)))
        if s + 1 < slots:
            update, lefts = lax.optimization_barrier((update, lefts))
    out = None
    for s, (mine, theirs) in enumerate(updates):
        out = finish(s, mine, theirs, gate, last_weight, 4, 256, out)
    return out


def solution(mesh):
    in_specs = (
        P(("parts", "row", "col"), "chan", None),
        P(),
        P(None, None, "chan"),
        P(None, None, "chan"),
        P(),
        P(None, "chan"),
        P(None, "chan"),
        P("parts", None),
        P("parts", None),
        P("parts"),
    )
    out_specs = P(("parts", "row", "col"), "chan", None)
    return jax.shard_map(
        per_device, mesh=mesh, in_specs=in_specs, out_specs=out_specs, check_vma=False
    )
```

```python
import functools

import jax
import jax.numpy as jnp
from jax import lax
from jax.experimental import pallas as pl
from jax.experimental.pallas import tpu as pltpu
from jax.sharding import PartitionSpec as P

BLK = 64
LANES = 128
epsilon = 1e-05
VMEM_LIMIT = 24 * 1024 * 1024
F32 = jnp.float32
BF16 = jnp.bfloat16


def sigmoid(x):
    return 0.5 * jnp.tanh(0.5 * x) + 0.5


def tile_of(row, col):
    return row * lax.axis_size("col") + col


def neighbour_tiles():
    rows = lax.axis_size("row")
    row, col = lax.axis_index("row"), lax.axis_index("col")
    behind = lax.rem(row + rows - 1, rows)
    ahead = lax.rem(row + 1, rows)
    return tile_of(row, col), tile_of(behind, col), tile_of(ahead, col)


def select_kernel(slots, triplets, cuts, a_ref, b_ref, n_ref, pair_ref, *refs):
    me, behind, ahead = neighbour_tiles()
    out_refs, sems = refs[:-1], refs[-1]
    picks = []
    for target in (ahead, behind):
        pick = jnp.int32(0)
        for s in range(slots):
            count = n_ref[target * slots + s]
            for m in range(triplets):
                for ids in (a_ref, b_ref):
                    name = ids[m, target * slots + s] - me * slots
                    mine = jnp.logical_and(name >= 0, name < slots)
                    pick = jnp.where(jnp.logical_and(m < count, mine), name, pick)
        picks.append(pick)
    copies = []
    for at, (start, size) in enumerate(cuts):
        for which, pick in enumerate(picks):
            out = 2 * at + which
            copies.append(
                pltpu.make_async_copy(
                    pair_ref.at[pick, :, pl.ds(start, size)], out_refs[out], sems.at[out]
                )
            )
            copies[-1].start()
    for copy in copies:
        copy.wait()


def select_blocks(pair, a_slots, b_slots, counts, cuts):
    slots, channels, cells = pair.shape
    smem = pl.BlockSpec(memory_space=pltpu.SMEM)
    vmem = pl.BlockSpec(memory_space=pltpu.VMEM)
    out_shape = [
        pltpu.VMEM((channels, size), pair.dtype) for _, size in cuts for _ in range(2)
    ]
    return pl.pallas_call(
        functools.partial(select_kernel, slots, a_slots.shape[0], cuts),
        out_shape=out_shape,
        in_specs=[smem, smem, smem, pl.BlockSpec(memory_space=pltpu.HBM)],
        out_specs=[vmem] * len(out_shape),
        scratch_shapes=[pltpu.SemaphoreType.DMA((len(out_shape),))],
        name="select_blocks",
    )(a_slots, b_slots, counts, pair)


def prepared(weight, gain):
    weight = weight * gain
    rolled = pltpu.roll(weight, weight.shape[1] // 2, 1)
    return jnp.where(lax.axis_index("chan") == 0, weight, rolled).astype(BF16)


def gated_rows(w_ref):
    gate, value = w_ref[0].astype(F32), w_ref[1].astype(F32)
    rows = []
    for at in range(0, gate.shape[0], 8):
        rows += [gate[at : at + 8], value[at : at + 8]]
    return [0.5 * row for row in rows]


def normed_of(mine, theirs):
    total = 2 * mine.shape[0]
    mine = mine.astype(F32)
    theirs = theirs.astype(F32)
    mean = jnp.sum(mine + theirs, axis=0, keepdims=True) * (1.0 / total)
    mine = mine - mean
    theirs = theirs - mean
    spread = jnp.sum(mine * mine + theirs * theirs, axis=0, keepdims=True) * (1.0 / total)
    scale = lax.rsqrt(spread + epsilon)
    return jnp.concatenate([(mine * scale).astype(BF16), (theirs * scale).astype(BF16)], axis=0)


def project_kernel(piece, chunk, offset, gated, *refs):
    if gated:
        m_ref, t_ref, a_ref, b_ref, o_ref, u_ref, g_ref, h_ref = refs[:8]
        l_ref, p_ref, gate_ref, w_ref, v_ref, sl, sp = refs[8:]
        blocks = ((m_ref.at[0], t_ref.at[0]), (m_ref.at[1], t_ref.at[1]))
        rows = gated_rows(a_ref) + gated_rows(b_ref) + [0.5 * o_ref[...].astype(F32)]
        weight = prepared(jnp.concatenate(rows, axis=0), g_ref[...])
        pair_of = 0
    else:
        m0, t0, m1, t1, w_ref, _, _, l_ref, p_ref, sl, sp = refs
        blocks = ((m0, t0), (m1, t1))
        weight = w_ref[...]
        pair_of = 1
    half, cells = blocks[0][0].shape
    if gated:
        w_ref[...] = weight[: 4 * half]
        v_ref[...] = prepared(0.5 * u_ref[...].astype(F32), h_ref[...])

        @pl.loop(0, half)
        def _(c):
            p_ref[4, c] = jnp.zeros((BLK, LANES), BF16)

    low = lax.broadcasted_iota(jnp.int32, (8, LANES), 1) < BLK
    high_rows = chunk // BLK

    @pl.loop(0, cells // chunk)
    def _(n):
        for start in range(0, chunk, piece):
            at = pl.ds(pl.multiple_of(n * chunk + start, piece), piece)
            sides = []
            for x, (m, t) in enumerate(blocks):
                y = jnp.dot(weight, normed_of(m[:, at], t[:, at]), preferred_element_type=F32)
                if gated:
                    gate_ref[x, :, at] = (jnp.tanh(y[4 * half :]) + 1.0).astype(BF16)
                for side in range(2):
                    groups = []
                    for row in range(2 * half * side, 2 * half * (side + 1), 16):
                        groups.append((jnp.tanh(y[row : row + 8]) + 1.0) * y[row + 8 : row + 16])
                    sides.append(groups)
            for row in range(0, half, 8):
                l0, r0, l1, r1 = (groups[row // 8] for groups in sides)
                for sub in range(0, piece, LANES):
                    i = (start + sub) // BLK
                    even = slice(i * half + row, i * half + row + 8)
                    odd = slice((i + 1) * half + row, (i + 1) * half + row + 8)
                    cut = slice(sub, sub + LANES)
                    for held, v0, v1 in ((sl, l0[:, cut], l1[:, cut]), (sp, r0[:, cut], r1[:, cut])):
                        held[even, :] = jnp.where(low, v0, pltpu.roll(v1, BLK, 1))
                        held[odd, :] = jnp.where(low, pltpu.roll(v0, BLK, 1), v1)

        to = pl.ds(pl.multiple_of(n * high_rows + offset // BLK, 16), high_rows)

        @pl.loop(0, half, unroll=8)
        def _(c):
            take = pl.ds(c, high_rows, stride=half)
            l_ref[pair_of, c, to, :] = sl[take, :].astype(BF16)
            right = sp[take, :].astype(BF16)
            p_ref[2 * pair_of, c, to, :] = right
            p_ref[2 * pair_of + 1, c, to, :] = pltpu.roll(right, BLK, 1)


def project(operands, half, cells, chunk, piece, gated, offset=0):
    out_shape = [
        pltpu.VMEM((2, half, BLK, LANES), BF16),
        pltpu.VMEM((5, half, BLK, LANES), BF16),
    ]
    aliases = {}
    if gated:
        out_shape += [
            pltpu.VMEM((2, half, cells), BF16),
            pltpu.VMEM((4 * half, 2 * half), BF16),
            pltpu.VMEM((half, 2 * half), BF16),
        ]
    else:
        aliases = {len(operands) - 2: 0, len(operands) - 1: 1}
        operands = operands[:-2] + [
            pltpu.with_memory_space_constraint(value, pltpu.VMEM) for value in operands[-2:]
        ]
    vmem = pl.BlockSpec(memory_space=pltpu.VMEM)
    return pl.pallas_call(
        functools.partial(project_kernel, piece, chunk, offset, gated),
        in_specs=[vmem] * len(operands),
        out_specs=[vmem] * len(out_shape),
        out_shape=out_shape,
        scratch_shapes=[pltpu.VMEM((chunk // BLK * half, LANES), F32)] * 2,
        input_output_aliases=aliases,
        compiler_params=pltpu.CompilerParams(vmem_limit_bytes=VMEM_LIMIT),
        name="project_own" if gated else "project_fetched",
    )(*operands)


def triplet_kernel(s, slots, triplets, group, a_ref, b_ref, n_ref, l_ref, p_ref, out_ref, *accs):
    me, behind, ahead = neighbour_tiles()
    low = lax.broadcasted_iota(jnp.int32, (BLK, LANES), 1) < BLK
    block = me * slots + s
    count = n_ref[block]
    picks = []
    for pair_at in range(2):
        for part in range(2):
            chosen = jnp.int32(0)
            used = jnp.int32(0)
            for m in range(triplets):
                left = a_ref[m, block]
                if pair_at == 0:
                    hit = left == me * slots + part
                else:
                    first = (behind, ahead)[part] * slots
                    hit = jnp.logical_and(left >= first, left < first + slots)
                hit = jnp.logical_and(hit, m < count)
                place = b_ref[m, block] - me * slots
                from_me = jnp.logical_and(place >= 0, place < slots)
                right = b_ref[m, block] - behind * slots
                from_behind = jnp.logical_and(right >= 0, right < slots)
                place = jnp.where(from_me, place, jnp.where(from_behind, 2, 3))
                chosen = jnp.where(hit, place, chosen)
                used = jnp.where(hit, 1, used)
            if part == 1:
                chosen = chosen + 1 - 2 * (chosen & 1)
            picks.append(jnp.where(used == 1, chosen, 4))

    take_low = lax.broadcasted_iota(jnp.int32, (group, LANES), 1) < BLK
    half = l_ref.shape[1]

    @pl.loop(0, half, step=group * len(accs))
    def _(base):
        for which, acc in enumerate(accs):
            for at in range(group):
                c = base + which * group + at
                lhs = jnp.concatenate([l_ref[0, c], l_ref[1, c]], axis=1)
                parts = [p_ref[pick, c] for pick in picks]
                rhs = jnp.concatenate(
                    [jnp.where(low, parts[0], parts[1]), jnp.where(low, parts[2], parts[3])], axis=1
                )
                acc[pl.ds(at, BLK, stride=group), :BLK] = lax.dot_general(
                    lhs, rhs, (((1,), (1,)), ((), ())), preferred_element_type=F32
                )
            rows = pl.ds(pl.multiple_of(base + which * group, group), group)
            for t in range(BLK // 2):
                even = acc[2 * t * group : (2 * t + 1) * group, :]
                odd = acc[(2 * t + 1) * group : (2 * t + 2) * group, :]
                out_ref[rows, t * LANES : (t + 1) * LANES] = jnp.where(
                    take_low, even, pltpu.roll(odd, BLK, 1)
                ).astype(BF16)


def triplet_sum(s, lefts, rights, a_slots, b_slots, counts, slots, group):
    half = lefts.shape[1]
    smem = pl.BlockSpec(memory_space=pltpu.SMEM)
    vmem = pl.BlockSpec(memory_space=pltpu.VMEM)
    lefts, rights = (
        pltpu.with_memory_space_constraint(value, pltpu.VMEM) for value in (lefts, rights)
    )
    return pl.pallas_call(
        functools.partial(triplet_kernel, s, slots, a_slots.shape[0], group),
        in_specs=[smem, smem, smem, vmem, vmem],
        out_specs=vmem,
        out_shape=pltpu.VMEM((half, BLK * BLK), BF16),
        scratch_shapes=[pltpu.VMEM((BLK * group, LANES), F32)] * 2,
        compiler_params=pltpu.CompilerParams(vmem_limit_bytes=VMEM_LIMIT),
        name="triplets",
    )(a_slots, b_slots, counts, lefts, rights)


def finish_kernel(s, piece, mine_ref, theirs_ref, gate_ref, w_ref, *refs):
    out_ref, held, sems = refs[-3:]
    weight = w_ref[...]
    cells = mine_ref.shape[-1]
    steps = sems.shape[0]
    size = cells // steps

    def copy(n):
        to = pl.ds(pl.multiple_of(n * size, size), size)
        return pltpu.make_async_copy(held.at[:, to], out_ref.at[s, :, to], sems.at[n])

    @pl.loop(0, steps)
    def _(n):
        for start in range(0, size, piece):
            to = pl.ds(pl.multiple_of(n * size + start, piece), piece)
            normed = normed_of(mine_ref[:, to], theirs_ref[:, to])
            projected = jnp.dot(weight, normed, preferred_element_type=F32)
            held[:, to] = (gate_ref[s, :, to].astype(F32) * projected).astype(BF16)
        copy(n).start()

    @pl.loop(0, steps)
    def _(n):
        copy(n).wait()


def finish(s, mine, theirs, gate, weight, steps, piece, out=None):
    half, cells = mine.shape
    vmem = pl.BlockSpec(memory_space=pltpu.VMEM)
    operands = [mine, theirs, gate, weight]
    in_specs = [vmem] * 4
    aliases = {}
    if out is not None:
        aliases = {len(operands): 0}
        operands.append(out)
        in_specs.append(pl.BlockSpec(memory_space=pltpu.HBM))
    return pl.pallas_call(
        functools.partial(finish_kernel, s, piece),
        in_specs=in_specs,
        out_specs=pl.BlockSpec(memory_space=pltpu.HBM),
        out_shape=jax.ShapeDtypeStruct(gate.shape, BF16),
        scratch_shapes=[pltpu.VMEM((half, cells), BF16), pltpu.SemaphoreType.DMA((steps,))],
        input_output_aliases=aliases,
        compiler_params=pltpu.CompilerParams(vmem_limit_bytes=VMEM_LIMIT),
        name="finish",
    )(*operands)


def per_device(
    pair,
    ln_in_gain,
    a_weight,
    b_weight,
    ln_out_gain,
    out_gate_weight,
    out_weight,
    a_slots,
    b_slots,
    counts,
):
    slots, half, cells = pair.shape
    rows = lax.axis_size("row")
    swap = [(0, 1), (1, 0)]
    up = [(i, (i + 1) % rows) for i in range(rows)]
    down = [(i, (i - 1) % rows) for i in range(rows)]

    a_slots, b_slots = a_slots.T, b_slots.T
    weights = [
        jnp.swapaxes(a_weight, 1, 2),
        jnp.swapaxes(b_weight, 1, 2),
        out_gate_weight.T,
        out_weight.T,
        ln_in_gain[None, :],
        ln_out_gain[None, :],
    ]

    pair_other = lax.ppermute(pair, "chan", swap)
    cuts = ((0, cells // 4 * 3), (cells // 4 * 3, cells // 4))
    chosen = select_blocks(pair, a_slots, b_slots, counts, cuts)
    arrived = [
        (lax.ppermute(chosen[2 * n], "row", up), lax.ppermute(chosen[2 * n + 1], "row", down))
        for n in range(len(cuts))
    ]
    lefts, rights, gate, weight, last_weight = project(
        [pair, pair_other, *weights], half, cells, 1024, 128, True
    )
    for (start, size), (from_behind, from_ahead) in zip(cuts, arrived):
        from_behind, from_ahead, lefts = lax.optimization_barrier((from_behind, from_ahead, lefts))
        behind_other = lax.ppermute(from_behind, "chan", swap)
        ahead_other = lax.ppermute(from_ahead, "chan", swap)
        lefts, rights = project(
            [from_behind, behind_other, from_ahead, ahead_other, weight, lefts, rights],
            half,
            size,
            1024,
            128,
            False,
            start,
        )
    updates = []
    for s in range(slots):
        update = triplet_sum(s, lefts, rights, a_slots, b_slots, counts, slots, 16)
        updates.append((update, lax.ppermute(update, "chan", swap)))
        if s + 1 < slots:
            update, lefts = lax.optimization_barrier((update, lefts))
    out = None
    for s, (mine, theirs) in enumerate(updates):
        out = finish(s, mine, theirs, gate, last_weight, 4, 256, out)
    return out


def solution(mesh):
    in_specs = (
        P(("parts", "row", "col"), "chan", None),
        P(),
        P(None, None, "chan"),
        P(None, None, "chan"),
        P(),
        P(None, "chan"),
        P(None, "chan"),
        P("parts", None),
        P("parts", None),
        P("parts"),
    )
    out_specs = P(("parts", "row", "col"), "chan", None)
    return jax.shard_map(
        per_device, mesh=mesh, in_specs=in_specs, out_specs=out_specs, check_vma=False
    )
```

```python
import functools

import jax
import jax.numpy as jnp
from jax import lax
from jax.experimental import pallas as pl
from jax.experimental.pallas import tpu as pltpu
from jax.sharding import PartitionSpec as P

BLK = 64
LANES = 128
epsilon = 1e-05
VMEM_LIMIT = 24 * 1024 * 1024
F32 = jnp.float32
BF16 = jnp.bfloat16


def sigmoid(x):
    return 0.5 * jnp.tanh(0.5 * x) + 0.5


def tile_of(row, col):
    return row * lax.axis_size("col") + col


def neighbour_tiles():
    rows = lax.axis_size("row")
    row, col = lax.axis_index("row"), lax.axis_index("col")
    behind = lax.rem(row + rows - 1, rows)
    ahead = lax.rem(row + 1, rows)
    return tile_of(row, col), tile_of(behind, col), tile_of(ahead, col)


def select_kernel(slots, triplets, cuts, a_ref, b_ref, n_ref, pair_ref, *refs):
    me, behind, ahead = neighbour_tiles()
    out_refs, sems = refs[:-1], refs[-1]
    picks = []
    for target in (ahead, behind):
        pick = jnp.int32(0)
        for s in range(slots):
            count = n_ref[target * slots + s]
            for m in range(triplets):
                for ids in (a_ref, b_ref):
                    name = ids[m, target * slots + s] - me * slots
                    mine = jnp.logical_and(name >= 0, name < slots)
                    pick = jnp.where(jnp.logical_and(m < count, mine), name, pick)
        picks.append(pick)
    copies = []
    for at, (start, size) in enumerate(cuts):
        for which, pick in enumerate(picks):
            out = 2 * at + which
            copies.append(
                pltpu.make_async_copy(
                    pair_ref.at[pick, :, pl.ds(start, size)], out_refs[out], sems.at[out]
                )
            )
            copies[-1].start()
    for copy in copies:
        copy.wait()


def select_blocks(pair, a_slots, b_slots, counts, cuts):
    slots, channels, cells = pair.shape
    smem = pl.BlockSpec(memory_space=pltpu.SMEM)
    vmem = pl.BlockSpec(memory_space=pltpu.VMEM)
    out_shape = [
        pltpu.VMEM((channels, size), pair.dtype) for _, size in cuts for _ in range(2)
    ]
    return pl.pallas_call(
        functools.partial(select_kernel, slots, a_slots.shape[0], cuts),
        out_shape=out_shape,
        in_specs=[smem, smem, smem, pl.BlockSpec(memory_space=pltpu.HBM)],
        out_specs=[vmem] * len(out_shape),
        scratch_shapes=[pltpu.SemaphoreType.DMA((len(out_shape),))],
        name="select_blocks",
    )(a_slots, b_slots, counts, pair)


def prepared(weight, gain=None):
    if gain is not None:
        weight = weight * gain
    rolled = pltpu.roll(weight, weight.shape[1] // 2, 1)
    return jnp.where(lax.axis_index("chan") == 0, weight, rolled).astype(BF16)


def gated_rows(w_ref):
    gate, value = w_ref[0].astype(F32), w_ref[1].astype(F32)
    rows = []
    for at in range(0, gate.shape[0], 8):
        rows += [gate[at : at + 8], value[at : at + 8]]
    return [0.5 * row for row in rows]


def normed_of(mine, theirs, gain=None):
    total = 2 * mine.shape[0]
    mine = mine.astype(F32)
    theirs = theirs.astype(F32)
    mean = jnp.sum(mine + theirs, axis=0, keepdims=True) * (1.0 / total)
    mine = mine - mean
    theirs = theirs - mean
    spread = jnp.sum(mine * mine + theirs * theirs, axis=0, keepdims=True) * (1.0 / total)
    scale = lax.rsqrt(spread + epsilon)
    mine = mine * scale
    theirs = theirs * scale
    if gain is not None:
        half = mine.shape[0]
        mine = mine * gain[:half]
        theirs = theirs * gain[half:]
    return jnp.concatenate([mine.astype(BF16), theirs.astype(BF16)], axis=0)


def project_kernel(chunk, cuts, offset, gated, *refs):
    if gated:
        m_ref, t_ref, a_ref, b_ref, o_ref, u_ref, g_ref, h_ref = refs[:8]
        l_ref, p_ref, gate_ref, w_ref, v_ref, gain_ref, sl, sp = refs[8:]
        pieces = [((m_ref.at[0], t_ref.at[0]), (m_ref.at[1], t_ref.at[1]))]
        rows = gated_rows(a_ref) + gated_rows(b_ref) + [0.5 * o_ref[...].astype(F32)]
        weight = prepared(jnp.concatenate(rows, axis=0))
        pair_of = 0
    else:
        m0, m1 = refs[:2]
        theirs = refs[2 : 2 + 2 * len(cuts)]
        w_ref, gain_ref, _, _, l_ref, p_ref, sl, sp = refs[2 + 2 * len(cuts) :]
        pieces = []
        for at, (start, size) in enumerate(cuts):
            cut = pl.ds(start, size)
            t0, t1 = theirs[2 * at], theirs[2 * at + 1]
            pieces.append(((m0.at[:, cut], t0), (m1.at[:, cut], t1)))
        weight = w_ref[...]
        pair_of = 1
    half = l_ref.shape[1]
    if gated:
        w_ref[...] = weight[: 4 * half]
        mine = g_ref[pl.ds(pl.multiple_of(lax.axis_index("chan") * half, half), half), :]
        other = g_ref[pl.ds(pl.multiple_of((1 - lax.axis_index("chan")) * half, half), half), :]
        gain_ref[...] = jnp.broadcast_to(jnp.concatenate([mine, other], axis=0), gain_ref.shape)
        v_ref[...] = prepared(0.5 * u_ref[...].astype(F32), h_ref[...])

        @pl.loop(0, half)
        def _(c):
            p_ref[4, c] = jnp.zeros((BLK, LANES), BF16)

    low = lax.broadcasted_iota(jnp.int32, (8, LANES), 1) < BLK
    high_rows = chunk // BLK
    pitch = sl.shape[0] // high_rows

    def step(blocks, n, to):
        for start in range(0, chunk, LANES):
            at = pl.ds(pl.multiple_of(n * chunk + start, LANES), LANES)
            sides = []
            for x, (m, t) in enumerate(blocks):
                normed = normed_of(m[:, at], t[:, at], gain_ref[...])
                y = jnp.dot(weight, normed, preferred_element_type=F32)
                if gated:
                    gate_ref[x, :, at] = (jnp.tanh(y[4 * half :]) + 1.0).astype(BF16)
                for side in range(2):
                    groups = []
                    for row in range(2 * half * side, 2 * half * (side + 1), 16):
                        groups.append((jnp.tanh(y[row : row + 8]) + 1.0) * y[row + 8 : row + 16])
                    sides.append(groups)
            i = start // BLK
            for row in range(0, half, 8):
                l0, r0, l1, r1 = (groups[row // 8] for groups in sides)
                even = slice(i * pitch + row, i * pitch + row + 8)
                odd = slice((i + 1) * pitch + row, (i + 1) * pitch + row + 8)
                for held, v0, v1 in ((sl, l0, l1), (sp, r0, r1)):
                    held[even, :] = jnp.where(low, v0, pltpu.roll(v1, BLK, 1))
                    held[odd, :] = jnp.where(low, pltpu.roll(v0, BLK, 1), v1)

        @pl.loop(0, half, unroll=8)
        def _(c):
            take = pl.ds(c, high_rows, stride=pitch)
            l_ref[pair_of, c, to, :] = sl[take, :].astype(BF16)
            right = sp[take, :].astype(BF16)
            p_ref[2 * pair_of, c, to, :] = right
            p_ref[2 * pair_of + 1, c, to, :] = pltpu.roll(right, BLK, 1)

    for (start, size), blocks in zip(cuts, pieces):

        @pl.loop(0, size // chunk)
        def _(n):
            first = n * high_rows + (offset + start) // BLK
            step(blocks, n, pl.ds(pl.multiple_of(first, 16), high_rows))


def project(operands, half, cuts, chunk, gated, offset=0):
    out_shape = [
        pltpu.VMEM((2, half, BLK, LANES), BF16),
        pltpu.VMEM((5, half, BLK, LANES), BF16),
    ]
    aliases = {}
    if gated:
        out_shape += [
            pltpu.VMEM((2, half, BLK * BLK), BF16),
            pltpu.VMEM((4 * half, 2 * half), BF16),
            pltpu.VMEM((half, 2 * half), BF16),
            pltpu.VMEM((2 * half, LANES), F32),
        ]
    else:
        aliases = {len(operands) - 2: 0, len(operands) - 1: 1}
        operands = operands[:-2] + [
            pltpu.with_memory_space_constraint(value, pltpu.VMEM) for value in operands[-2:]
        ]
    vmem = pl.BlockSpec(memory_space=pltpu.VMEM)
    return pl.pallas_call(
        functools.partial(project_kernel, chunk, cuts, offset, gated),
        in_specs=[vmem] * len(operands),
        out_specs=[vmem] * len(out_shape),
        out_shape=out_shape,
        scratch_shapes=[pltpu.VMEM((chunk // BLK * (half + 8), LANES), F32)] * 2,
        input_output_aliases=aliases,
        compiler_params=pltpu.CompilerParams(vmem_limit_bytes=VMEM_LIMIT),
        name="project_own" if gated else "project_fetched",
    )(*operands)


def triplet_kernel(s, slots, triplets, group, a_ref, b_ref, n_ref, l_ref, p_ref, out_ref, *accs):
    me, behind, ahead = neighbour_tiles()
    low = lax.broadcasted_iota(jnp.int32, (BLK, LANES), 1) < BLK
    block = me * slots + s
    count = n_ref[block]
    picks = []
    for pair_at in range(2):
        for part in range(2):
            chosen = jnp.int32(0)
            used = jnp.int32(0)
            for m in range(triplets):
                left = a_ref[m, block]
                if pair_at == 0:
                    hit = left == me * slots + part
                else:
                    first = (behind, ahead)[part] * slots
                    hit = jnp.logical_and(left >= first, left < first + slots)
                hit = jnp.logical_and(hit, m < count)
                place = b_ref[m, block] - me * slots
                from_me = jnp.logical_and(place >= 0, place < slots)
                right = b_ref[m, block] - behind * slots
                from_behind = jnp.logical_and(right >= 0, right < slots)
                place = jnp.where(from_me, place, jnp.where(from_behind, 2, 3))
                chosen = jnp.where(hit, place, chosen)
                used = jnp.where(hit, 1, used)
            if part == 1:
                chosen = chosen + 1 - 2 * (chosen & 1)
            picks.append(jnp.where(used == 1, chosen, 4))

    take_low = lax.broadcasted_iota(jnp.int32, (group, LANES), 1) < BLK
    half = l_ref.shape[1]
    pitch = accs[0].shape[0] // BLK

    @pl.loop(0, half, step=group * len(accs))
    def _(base):
        for which, acc in enumerate(accs):
            for at in range(group):
                c = base + which * group + at
                lhs = jnp.concatenate([l_ref[0, c], l_ref[1, c]], axis=1)
                parts = [p_ref[pick, c] for pick in picks]
                rhs = jnp.concatenate(
                    [jnp.where(low, parts[0], parts[1]), jnp.where(low, parts[2], parts[3])], axis=1
                )
                acc[pl.ds(at, BLK, stride=pitch), :BLK] = lax.dot_general(
                    lhs, rhs, (((1,), (1,)), ((), ())), preferred_element_type=F32
                )
            rows = pl.ds(pl.multiple_of(base + which * group, group), group)
            for t in range(BLK // 2):
                even = acc[2 * t * pitch : 2 * t * pitch + group, :]
                odd = acc[(2 * t + 1) * pitch : (2 * t + 1) * pitch + group, :]
                out_ref[rows, t * LANES : (t + 1) * LANES] = jnp.where(
                    take_low, even, pltpu.roll(odd, BLK, 1)
                ).astype(BF16)


def triplet_sum(s, lefts, rights, a_slots, b_slots, counts, slots, group):
    half = lefts.shape[1]
    smem = pl.BlockSpec(memory_space=pltpu.SMEM)
    vmem = pl.BlockSpec(memory_space=pltpu.VMEM)
    lefts, rights = (
        pltpu.with_memory_space_constraint(value, pltpu.VMEM) for value in (lefts, rights)
    )
    return pl.pallas_call(
        functools.partial(triplet_kernel, s, slots, a_slots.shape[0], group),
        in_specs=[smem, smem, smem, vmem, vmem],
        out_specs=vmem,
        out_shape=pltpu.VMEM((half, BLK * BLK), BF16),
        scratch_shapes=[pltpu.VMEM((BLK * (group + 8), LANES), F32)] * 2,
        compiler_params=pltpu.CompilerParams(vmem_limit_bytes=VMEM_LIMIT),
        name="triplets",
    )(a_slots, b_slots, counts, lefts, rights)


def finish_kernel(s, mine_ref, theirs_ref, gate_ref, w_ref, *refs):
    weight = w_ref[...]
    cells = mine_ref.shape[-1]
    if s == 0:
        held = refs[0]
        steps = 4
    else:
        before_ref, out_ref, held, sems = refs
        steps = sems.shape[0] - 1
        before = pltpu.make_async_copy(before_ref, out_ref.at[0], sems.at[steps])
        before.start()
    size = cells // steps

    def copy(n):
        to = pl.ds(pl.multiple_of(n * size, size), size)
        return pltpu.make_async_copy(held.at[:, to], out_ref.at[1, :, to], sems.at[n])

    @pl.loop(0, steps)
    def _(n):
        for start in range(0, size, LANES):
            to = pl.ds(pl.multiple_of(n * size + start, LANES), LANES)
            normed = normed_of(mine_ref[:, to], theirs_ref[:, to])
            projected = jnp.dot(weight, normed, preferred_element_type=F32)
            held[:, to] = (gate_ref[s, :, to].astype(F32) * projected).astype(BF16)
        if s > 0:
            copy(n).start()

    if s > 0:

        @pl.loop(0, steps)
        def _(n):
            copy(n).wait()

        before.wait()


def finish(s, mine, theirs, gate, weight, before=None):
    vmem = pl.BlockSpec(memory_space=pltpu.VMEM)
    operands = [mine, theirs, gate, weight]
    if s == 0:
        out_shape, out_specs, scratch = pltpu.VMEM(mine.shape, BF16), vmem, []
    else:
        operands.append(before)
        out_shape = jax.ShapeDtypeStruct(gate.shape, BF16)
        out_specs = pl.BlockSpec(memory_space=pltpu.HBM)
        scratch = [pltpu.VMEM(mine.shape, BF16), pltpu.SemaphoreType.DMA((5,))]
    return pl.pallas_call(
        functools.partial(finish_kernel, s),
        in_specs=[vmem] * len(operands),
        out_specs=out_specs,
        out_shape=out_shape,
        scratch_shapes=scratch,
        compiler_params=pltpu.CompilerParams(vmem_limit_bytes=VMEM_LIMIT),
        name="finish",
    )(*operands)


def per_device(
    pair,
    ln_in_gain,
    a_weight,
    b_weight,
    ln_out_gain,
    out_gate_weight,
    out_weight,
    a_slots,
    b_slots,
    counts,
):
    slots, half, cells = pair.shape
    rows = lax.axis_size("row")
    swap = [(0, 1), (1, 0)]
    up = [(i, (i + 1) % rows) for i in range(rows)]
    down = [(i, (i - 1) % rows) for i in range(rows)]

    a_slots, b_slots = a_slots.T, b_slots.T
    weights = [
        jnp.swapaxes(a_weight, 1, 2),
        jnp.swapaxes(b_weight, 1, 2),
        out_gate_weight.T,
        out_weight.T,
        ln_in_gain[:, None],
        ln_out_gain[None, :],
    ]

    pair_other = lax.ppermute(pair, "chan", swap)
    cuts = ((0, cells // 2), (cells // 2, cells // 2))
    chosen = select_blocks(pair, a_slots, b_slots, counts, cuts)
    arrived = [
        (lax.ppermute(chosen[2 * n], "row", up), lax.ppermute(chosen[2 * n + 1], "row", down))
        for n in range(len(cuts))
    ]
    lefts, rights, gate, weight, last_weight, gain = project(
        [pair, pair_other, *weights], half, ((0, cells),), 1024, True
    )
    for (start, size), (from_behind, from_ahead) in zip(cuts, arrived):
        from_behind, from_ahead, lefts = lax.optimization_barrier((from_behind, from_ahead, lefts))
        parts = ((0, size),) if start else ((0, size // 2), (size // 2, size // 2))
        others = [
            lax.ppermute(lax.slice_in_dim(value, at, at + wide, axis=1), "chan", swap)
            for at, wide in parts
            for value in (from_behind, from_ahead)
        ]
        lefts, rights = project(
            [from_behind, from_ahead, *others, weight, gain, lefts, rights],
            half,
            parts,
            1024,
            False,
            start,
        )
    updates = []
    for s in range(slots):
        update = triplet_sum(s, lefts, rights, a_slots, b_slots, counts, slots, 16)
        updates.append((update, lax.ppermute(update, "chan", swap)))
        if s + 1 < slots:
            update, lefts = lax.optimization_barrier((update, lefts))
    out = None
    for s, (mine, theirs) in enumerate(updates):
        out = finish(s, mine, theirs, gate, last_weight, out)
    return out


def solution(mesh):
    in_specs = (
        P(("parts", "row", "col"), "chan", None),
        P(),
        P(None, None, "chan"),
        P(None, None, "chan"),
        P(),
        P(None, "chan"),
        P(None, "chan"),
        P("parts", None),
        P("parts", None),
        P("parts"),
    )
    out_specs = P(("parts", "row", "col"), "chan", None)
    return jax.shard_map(
        per_device, mesh=mesh, in_specs=in_specs, out_specs=out_specs, check_vma=False
    )
```

```python
import functools

import jax
import jax.numpy as jnp
from jax import lax
from jax.experimental import pallas as pl
from jax.experimental.pallas import tpu as pltpu
from jax.sharding import PartitionSpec as P

BLK = 64
LANES = 128
epsilon = 1e-05
VMEM_LIMIT = 24 * 1024 * 1024
F32 = jnp.float32
BF16 = jnp.bfloat16


def sigmoid(x):
    return 0.5 * jnp.tanh(0.5 * x) + 0.5


def tile_of(row, col):
    return row * lax.axis_size("col") + col


def neighbour_tiles():
    rows = lax.axis_size("row")
    row, col = lax.axis_index("row"), lax.axis_index("col")
    behind = lax.rem(row + rows - 1, rows)
    ahead = lax.rem(row + 1, rows)
    return tile_of(row, col), tile_of(behind, col), tile_of(ahead, col)


def select_kernel(slots, triplets, cuts, a_ref, b_ref, n_ref, pair_ref, *refs):
    me, behind, ahead = neighbour_tiles()
    out_refs, sems = refs[:-1], refs[-1]
    picks = []
    for target in (ahead, behind):
        pick = jnp.int32(0)
        for s in range(slots):
            count = n_ref[target * slots + s]
            for m in range(triplets):
                for ids in (a_ref, b_ref):
                    name = ids[m, target * slots + s] - me * slots
                    mine = jnp.logical_and(name >= 0, name < slots)
                    pick = jnp.where(jnp.logical_and(m < count, mine), name, pick)
        picks.append(pick)
    copies = []
    for at, (start, size) in enumerate(cuts):
        for which, pick in enumerate(picks):
            out = 2 * at + which
            copies.append(
                pltpu.make_async_copy(
                    pair_ref.at[pick, :, pl.ds(start, size)], out_refs[out], sems.at[out]
                )
            )
            copies[-1].start()
    for copy in copies:
        copy.wait()


def select_blocks(pair, a_slots, b_slots, counts, cuts):
    slots, channels, cells = pair.shape
    smem = pl.BlockSpec(memory_space=pltpu.SMEM)
    vmem = pl.BlockSpec(memory_space=pltpu.VMEM)
    out_shape = [
        pltpu.VMEM((channels, size), pair.dtype) for _, size in cuts for _ in range(2)
    ]
    return pl.pallas_call(
        functools.partial(select_kernel, slots, a_slots.shape[0], cuts),
        out_shape=out_shape,
        in_specs=[smem, smem, smem, pl.BlockSpec(memory_space=pltpu.HBM)],
        out_specs=[vmem] * len(out_shape),
        scratch_shapes=[pltpu.SemaphoreType.DMA((len(out_shape),))],
        name="select_blocks",
    )(a_slots, b_slots, counts, pair)


def prepared(weight, gain=None):
    if gain is not None:
        weight = weight * gain
    rolled = pltpu.roll(weight, weight.shape[1] // 2, 1)
    return jnp.where(lax.axis_index("chan") == 0, weight, rolled).astype(BF16)


def gated_rows(w_ref):
    gate, value = w_ref[0].astype(F32), w_ref[1].astype(F32)
    rows = []
    for at in range(0, gate.shape[0], 8):
        rows += [gate[at : at + 8], value[at : at + 8]]
    return [0.5 * row for row in rows]


def normed_of(mine, theirs, gain=None):
    total = 2 * mine.shape[0]
    mine = mine.astype(F32)
    theirs = theirs.astype(F32)
    mean = jnp.sum(mine + theirs, axis=0, keepdims=True) * (1.0 / total)
    mine = mine - mean
    theirs = theirs - mean
    spread = jnp.sum(mine * mine + theirs * theirs, axis=0, keepdims=True) * (1.0 / total)
    scale = lax.rsqrt(spread + epsilon)
    mine = mine * scale
    theirs = theirs * scale
    if gain is not None:
        half = mine.shape[0]
        mine = mine * gain[:half]
        theirs = theirs * gain[half:]
    return jnp.concatenate([mine.astype(BF16), theirs.astype(BF16)], axis=0)


def gated_sides(mine, theirs, weight, gain, half):
    y = jnp.dot(weight, normed_of(mine, theirs, gain), preferred_element_type=F32)
    sides = []
    for side in range(2):
        groups = []
        for row in range(2 * half * side, 2 * half * (side + 1), 16):
            groups.append((jnp.tanh(y[row : row + 8]) + 1.0) * y[row + 8 : row + 16])
        sides.append(groups)
    return sides, y[4 * half :]


def pair_chunk(sides_at, chunk, held, half):
    low = lax.broadcasted_iota(jnp.int32, (8, LANES), 1) < BLK
    pitch = held[0].shape[0] // (chunk // BLK)
    for start in range(0, chunk, LANES):
        first, second = sides_at(start)
        i = start // BLK
        for out, values0, values1 in zip(held, first, second):
            for at, (v0, v1) in enumerate(zip(values0, values1)):
                even = slice(i * pitch + 8 * at, i * pitch + 8 * at + 8)
                odd = slice((i + 1) * pitch + 8 * at, (i + 1) * pitch + 8 * at + 8)
                out[even, :] = jnp.where(low, v0, pltpu.roll(v1, BLK, 1))
                out[odd, :] = jnp.where(low, pltpu.roll(v0, BLK, 1), v1)
        yield


def spread_chunk(chunk, held, l_ref, p_ref, pair_of, first_row, half):
    rows = chunk // BLK
    pitch = held[0].shape[0] // rows
    to = pl.ds(pl.multiple_of(first_row, 16), rows)
    for c in range(half):
        take = pl.ds(c, rows, stride=pitch)
        l_ref[pair_of, c, to, :] = held[0][take, :].astype(BF16)
        right = held[1][take, :].astype(BF16)
        p_ref[2 * pair_of, c, to, :] = right
        p_ref[2 * pair_of + 1, c, to, :] = pltpu.roll(right, BLK, 1)
        if c % 8 == 7:
            yield


def two_chunks(sides_at, n, chunk, held, l_ref, p_ref, pair_of, first_row, half):
    rows = chunk // BLK
    steps = [
        pair_chunk(functools.partial(sides_at, 2 * n + k), chunk, held[2 * k : 2 * k + 2], half)
        for k in range(2)
    ]
    spreads = [
        spread_chunk(
            chunk, held[2 * k : 2 * k + 2], l_ref, p_ref, pair_of, first_row + (2 * n + k) * rows, half
        )
        for k in range(2)
    ]
    for _ in steps[0]:
        pass
    for _ in zip(steps[1], spreads[0]):
        pass
    for _ in spreads[0]:
        pass
    for _ in spreads[1]:
        pass


def cells_at(n, chunk, start):
    return pl.ds(pl.multiple_of(n * chunk + start, LANES), LANES)


def own_kernel(chunk, *refs):
    t_ref = refs[0]
    sources = refs[1:8]
    l_ref, p_ref, gate_ref, w_ref, v_ref, gain_ref = refs[8:14]
    targets = refs[14:21]
    held, sems = refs[21:25], refs[25]
    copies = [
        pltpu.make_async_copy(source, target, sems.at[at])
        for at, (source, target) in enumerate(zip(sources, targets))
    ]
    for copy in copies:
        copy.start()
    half = l_ref.shape[1]

    @pl.loop(0, half)
    def _(c):
        p_ref[4, c] = jnp.zeros((BLK, LANES), BF16)

    for copy in copies:
        copy.wait()
    m_ref, a_ref, b_ref, o_ref, u_ref, g_ref, h_ref = targets
    rows = gated_rows(a_ref) + gated_rows(b_ref) + [0.5 * o_ref[...].astype(F32)]
    weight = prepared(jnp.concatenate(rows, axis=0))
    w_ref[...] = weight[: 4 * half]
    v_ref[...] = prepared(0.5 * u_ref[...].astype(F32), h_ref[...])
    across = jnp.transpose(jnp.broadcast_to(g_ref[...], (2 * half, LANES)))
    in_order = lax.axis_index("chan") == 0
    gain_ref[:half] = jnp.where(in_order, across[:half], across[half:])
    gain_ref[half:] = jnp.where(in_order, across[half:], across[:half])

    def sides_at(n, start):
        at = cells_at(n, chunk, start)
        both = []
        for x in range(2):
            sides, rest = gated_sides(m_ref[x, :, at], t_ref[x, :, at], weight, gain_ref[...], half)
            gate_ref[x, :, at] = (jnp.tanh(rest) + 1.0).astype(BF16)
            both.append(sides)
        return both

    @pl.loop(0, m_ref.shape[-1] // chunk // 2)
    def _(n):
        two_chunks(sides_at, n, chunk, held, l_ref, p_ref, 0, 0, half)


def both_kernel(chunk, first_row, m0, m1, *refs):
    theirs = refs[:4]
    w_ref, gain_ref, _, _, l_ref, p_ref = refs[4:10]
    held = refs[10:]
    half = l_ref.shape[1]
    weight = w_ref[...]

    def sides_at(n, start):
        at = cells_at(n, chunk, start)
        within = pl.ds(start, LANES)
        return [
            gated_sides(m[:, at], theirs[2 * n + x][:, within], weight, gain_ref[...], half)[0]
            for x, m in enumerate((m0, m1))
        ]

    two_chunks(sides_at, 0, chunk, held, l_ref, p_ref, 1, first_row, half)


def early_kernel(chunk, m_ref, t0_ref, t1_ref, w_ref, gain_ref, l_ref, r_ref):
    weight = w_ref[...]
    half = m_ref.shape[0]
    for n, t_ref in enumerate((t0_ref, t1_ref)):

        @pl.loop(0, chunk, step=4 * LANES)
        def _(base):
            for start in range(0, 4 * LANES, LANES):
                within = pl.ds(pl.multiple_of(base + start, LANES), LANES)
                at = pl.ds(pl.multiple_of(n * chunk + base + start, LANES), LANES)
                sides, _ = gated_sides(m_ref[:, at], t_ref[:, within], weight, gain_ref[...], half)
                for out, groups in zip((l_ref, r_ref), sides):
                    for row, group in enumerate(groups):
                        out[8 * row : 8 * row + 8, at] = group


def late_kernel(chunk, first_row, m_ref, t_ref, l0_ref, r0_ref, w_ref, gain_ref, *refs):
    l_ref, p_ref = refs[2:4]
    held = refs[4:]
    half = l_ref.shape[1]
    weight = w_ref[...]

    def sides_at(n, start):
        at = cells_at(n, chunk, start)
        first = [[ref[row : row + 8, at] for row in range(0, half, 8)] for ref in (l0_ref, r0_ref)]
        return first, gated_sides(m_ref[:, at], t_ref[:, at], weight, gain_ref[...], half)[0]

    two_chunks(sides_at, 0, chunk, held, l_ref, p_ref, 1, first_row, half)


def call(kernel, name, operands, out_shape, scratch, aliased=0, hbm=0):
    vmem = pl.BlockSpec(memory_space=pltpu.VMEM)
    plain = len(operands) - aliased
    operands = operands[:plain] + [
        pltpu.with_memory_space_constraint(value, pltpu.VMEM) for value in operands[plain:]
    ]
    operands = operands[: len(operands) - hbm] + [
        pltpu.with_memory_space_constraint(value, pltpu.HBM)
        for value in operands[len(operands) - hbm :]
    ]
    specs = [vmem] * (len(operands) - hbm) + [pl.BlockSpec(memory_space=pltpu.HBM)] * hbm
    return pl.pallas_call(
        kernel,
        in_specs=specs,
        out_specs=[vmem] * len(out_shape),
        out_shape=out_shape,
        scratch_shapes=scratch,
        input_output_aliases={plain + at: at for at in range(aliased)},
        compiler_params=pltpu.CompilerParams(vmem_limit_bytes=VMEM_LIMIT),
        name=name,
    )(*operands)


def operand_shapes(half):
    return [pltpu.VMEM((2, half, BLK, LANES), BF16), pltpu.VMEM((5, half, BLK, LANES), BF16)]


def chunk_scratch(half, chunk):
    return [pltpu.VMEM((chunk // BLK * (half + 8), LANES), F32)] * 4


def triplet_kernel(s, slots, triplets, group, a_ref, b_ref, n_ref, l_ref, p_ref, out_ref, acc):
    me, behind, ahead = neighbour_tiles()
    low = lax.broadcasted_iota(jnp.int32, (BLK, LANES), 1) < BLK
    block = me * slots + s
    count = n_ref[block]
    picks = []
    for pair_at in range(2):
        for part in range(2):
            chosen = jnp.int32(0)
            used = jnp.int32(0)
            for m in range(triplets):
                left = a_ref[m, block]
                if pair_at == 0:
                    hit = left == me * slots + part
                else:
                    first = (behind, ahead)[part] * slots
                    hit = jnp.logical_and(left >= first, left < first + slots)
                hit = jnp.logical_and(hit, m < count)
                place = b_ref[m, block] - me * slots
                from_me = jnp.logical_and(place >= 0, place < slots)
                right = b_ref[m, block] - behind * slots
                from_behind = jnp.logical_and(right >= 0, right < slots)
                place = jnp.where(from_me, place, jnp.where(from_behind, 2, 3))
                chosen = jnp.where(hit, place, chosen)
                used = jnp.where(hit, 1, used)
            if part == 1:
                chosen = chosen + 1 - 2 * (chosen & 1)
            picks.append(jnp.where(used == 1, chosen, 4))

    take_low = lax.broadcasted_iota(jnp.int32, (group, LANES), 1) < BLK
    half = l_ref.shape[1]
    pitch = acc.shape[0] // BLK

    def update_of(c):
        lhs = jnp.concatenate([l_ref[0, c], l_ref[1, c]], axis=1)
        parts = [p_ref[pick, c] for pick in picks]
        rhs = jnp.concatenate(
            [jnp.where(low, parts[0], parts[1]), jnp.where(low, parts[2], parts[3])], axis=1
        )
        return lax.dot_general(lhs, rhs, (((1,), (1,)), ((), ())), preferred_element_type=F32)

    @pl.loop(0, half // 2, step=group)
    def _(base):
        for at in range(group):
            c = base + at
            acc[pl.ds(at, BLK, stride=pitch), :] = jnp.concatenate(
                [update_of(c), update_of(c + half // 2)], axis=1
            )
        rows = pl.ds(pl.multiple_of(base, group), group)
        upper = pl.ds(pl.multiple_of(base + half // 2, group), group)
        for t in range(BLK // 2):
            even = acc[2 * t * pitch : 2 * t * pitch + group, :]
            odd = acc[(2 * t + 1) * pitch : (2 * t + 1) * pitch + group, :]
            to = slice(t * LANES, (t + 1) * LANES)
            out_ref[rows, to] = jnp.where(take_low, even, pltpu.roll(odd, BLK, 1)).astype(BF16)
            out_ref[upper, to] = jnp.where(take_low, pltpu.roll(even, BLK, 1), odd).astype(BF16)


def triplet_sum(s, lefts, rights, a_slots, b_slots, counts, slots, group):
    half = lefts.shape[1]
    smem = pl.BlockSpec(memory_space=pltpu.SMEM)
    vmem = pl.BlockSpec(memory_space=pltpu.VMEM)
    lefts, rights = (
        pltpu.with_memory_space_constraint(value, pltpu.VMEM) for value in (lefts, rights)
    )
    return pl.pallas_call(
        functools.partial(triplet_kernel, s, slots, a_slots.shape[0], group),
        in_specs=[smem, smem, smem, vmem, vmem],
        out_specs=vmem,
        out_shape=pltpu.VMEM((half, BLK * BLK), BF16),
        scratch_shapes=[pltpu.VMEM((BLK * (group + 8), LANES), F32)],
        compiler_params=pltpu.CompilerParams(vmem_limit_bytes=VMEM_LIMIT),
        name="triplets",
    )(a_slots, b_slots, counts, lefts, rights)


def finish_kernel(s, mine_ref, theirs_ref, gate_ref, w_ref, *refs):
    weight = w_ref[...]
    cells = mine_ref.shape[-1]
    if s == 0:
        held = refs[0]
        steps = 4
    else:
        before_ref, out_ref, held, sems = refs
        steps = sems.shape[0] - 1
        before = pltpu.make_async_copy(before_ref, out_ref.at[0], sems.at[steps])
        before.start()
    size = cells // steps

    def copy(n):
        to = pl.ds(pl.multiple_of(n * size, size), size)
        return pltpu.make_async_copy(held.at[:, to], out_ref.at[1, :, to], sems.at[n])

    @pl.loop(0, steps)
    def _(n):
        for start in range(0, size, LANES):
            to = pl.ds(pl.multiple_of(n * size + start, LANES), LANES)
            normed = normed_of(mine_ref[:, to], theirs_ref[:, to])
            projected = jnp.dot(weight, normed, preferred_element_type=F32)
            held[:, to] = (gate_ref[s, :, to].astype(F32) * projected).astype(BF16)
        if s > 0:
            copy(n).start()

    if s > 0:

        @pl.loop(0, steps)
        def _(n):
            copy(n).wait()

        before.wait()


def finish(s, mine, theirs, gate, weight, before=None):
    vmem = pl.BlockSpec(memory_space=pltpu.VMEM)
    operands = [mine, theirs, gate, weight]
    if s == 0:
        out_shape, out_specs, scratch = pltpu.VMEM(mine.shape, BF16), vmem, []
    else:
        operands.append(before)
        out_shape = jax.ShapeDtypeStruct(gate.shape, BF16)
        out_specs = pl.BlockSpec(memory_space=pltpu.HBM)
        scratch = [pltpu.VMEM(mine.shape, BF16), pltpu.SemaphoreType.DMA((9,))]
    return pl.pallas_call(
        functools.partial(finish_kernel, s),
        in_specs=[vmem] * len(operands),
        out_specs=out_specs,
        out_shape=out_shape,
        scratch_shapes=scratch,
        compiler_params=pltpu.CompilerParams(vmem_limit_bytes=VMEM_LIMIT),
        name="finish",
    )(*operands)


def per_device(
    pair,
    ln_in_gain,
    a_weight,
    b_weight,
    ln_out_gain,
    out_gate_weight,
    out_weight,
    a_slots,
    b_slots,
    counts,
):
    slots, half, cells = pair.shape
    rows = lax.axis_size("row")
    swap = [(0, 1), (1, 0)]
    up = [(i, (i + 1) % rows) for i in range(rows)]
    down = [(i, (i - 1) % rows) for i in range(rows)]

    a_slots, b_slots = a_slots.T, b_slots.T
    weights = [
        jnp.swapaxes(a_weight, 1, 2),
        jnp.swapaxes(b_weight, 1, 2),
        out_gate_weight.T,
        out_weight.T,
        ln_in_gain[None, :],
        ln_out_gain[None, :],
    ]

    pair_other = lax.ppermute(pair, "chan", swap)
    cuts = ((0, cells // 2), (cells // 2, cells // 2))
    chosen = select_blocks(pair, a_slots, b_slots, counts, cuts)
    arrived = [
        (lax.ppermute(chosen[2 * n], "row", up), lax.ppermute(chosen[2 * n + 1], "row", down))
        for n in range(len(cuts))
    ]
    chunk = cells // 4
    sources = [pair, *weights]
    lefts, rights, gate, weight, last_weight, gain = call(
        functools.partial(own_kernel, chunk),
        "project_own",
        [pair_other, *sources],
        operand_shapes(half)
        + [
            pltpu.VMEM((slots, half, cells), BF16),
            pltpu.VMEM((4 * half, 2 * half), BF16),
            pltpu.VMEM((half, 2 * half), BF16),
            pltpu.VMEM((2 * half, LANES), F32),
        ],
        [pltpu.VMEM(value.shape, value.dtype) for value in sources]
        + chunk_scratch(half, chunk)
        + [pltpu.SemaphoreType.DMA((len(sources),))],
        hbm=len(sources),
    )
    from_behind, from_ahead, lefts = lax.optimization_barrier((*arrived[0], lefts))
    others = [
        lax.ppermute(lax.slice_in_dim(value, at, at + chunk, axis=1), "chan", swap)
        for at in (0, chunk)
        for value in (from_behind, from_ahead)
    ]
    lefts, rights = call(
        functools.partial(both_kernel, chunk, 0),
        "project_first",
        [from_behind, from_ahead, *others, weight, gain, lefts, rights],
        operand_shapes(half),
        chunk_scratch(half, chunk),
        aliased=2,
    )
    from_behind, lefts = lax.optimization_barrier((arrived[1][0], lefts))
    others = [
        lax.ppermute(lax.slice_in_dim(from_behind, at, at + chunk, axis=1), "chan", swap)
        for at in (0, chunk)
    ]
    early = call(
        functools.partial(early_kernel, chunk),
        "project_early",
        [from_behind, *others, weight, gain],
        [pltpu.VMEM((half, 2 * chunk), F32)] * 2,
        [],
    )
    from_ahead, early = lax.optimization_barrier((arrived[1][1], early))
    ahead_other = lax.ppermute(from_ahead, "chan", swap)
    lefts, rights = call(
        functools.partial(late_kernel, chunk, BLK // 2),
        "project_late",
        [from_ahead, ahead_other, *early, weight, gain, lefts, rights],
        operand_shapes(half),
        chunk_scratch(half, chunk),
        aliased=2,
    )
    updates = []
    for s in range(slots):
        update = triplet_sum(s, lefts, rights, a_slots, b_slots, counts, slots, 16)
        updates.append((update, lax.ppermute(update, "chan", swap)))
        if s + 1 < slots:
            update, lefts = lax.optimization_barrier((update, lefts))
    out = None
    for s, (mine, theirs) in enumerate(updates):
        out = finish(s, mine, theirs, gate, last_weight, out)
    return out


def solution(mesh):
    in_specs = (
        P(("parts", "row", "col"), "chan", None),
        P(),
        P(None, None, "chan"),
        P(None, None, "chan"),
        P(),
        P(None, "chan"),
        P(None, "chan"),
        P("parts", None),
        P("parts", None),
        P("parts"),
    )
    out_specs = P(("parts", "row", "col"), "chan", None)
    return jax.shard_map(
        per_device, mesh=mesh, in_specs=in_specs, out_specs=out_specs, check_vma=False
    )
```

```python
import functools

import jax
import jax.numpy as jnp
from jax import lax
from jax.experimental import pallas as pl
from jax.experimental.pallas import tpu as pltpu
from jax.sharding import PartitionSpec as P

BLK = 64
LANES = 128
epsilon = 1e-05
VMEM_LIMIT = 24 * 1024 * 1024
F32 = jnp.float32
BF16 = jnp.bfloat16


def sigmoid(x):
    return 0.5 * jnp.tanh(0.5 * x) + 0.5


def tile_of(row, col):
    return row * lax.axis_size("col") + col


def neighbour_tiles():
    rows = lax.axis_size("row")
    row, col = lax.axis_index("row"), lax.axis_index("col")
    behind = lax.rem(row + rows - 1, rows)
    ahead = lax.rem(row + 1, rows)
    return tile_of(row, col), tile_of(behind, col), tile_of(ahead, col)


def select_kernel(slots, triplets, cuts, a_ref, b_ref, n_ref, pair_ref, *refs):
    me, behind, ahead = neighbour_tiles()
    out_refs, sems = refs[:-1], refs[-1]
    picks = []
    for target in (ahead, behind):
        pick = jnp.int32(0)
        for s in range(slots):
            count = n_ref[target * slots + s]
            for m in range(triplets):
                for ids in (a_ref, b_ref):
                    name = ids[m, target * slots + s] - me * slots
                    mine = jnp.logical_and(name >= 0, name < slots)
                    pick = jnp.where(jnp.logical_and(m < count, mine), name, pick)
        picks.append(pick)
    copies = []
    for at, (start, size) in enumerate(cuts):
        for which, pick in enumerate(picks):
            out = 2 * at + which
            copies.append(
                pltpu.make_async_copy(
                    pair_ref.at[pick, :, pl.ds(start, size)], out_refs[out], sems.at[out]
                )
            )
            copies[-1].start()
    for copy in copies:
        copy.wait()


def select_blocks(pair, a_slots, b_slots, counts, cuts):
    slots, channels, cells = pair.shape
    smem = pl.BlockSpec(memory_space=pltpu.SMEM)
    vmem = pl.BlockSpec(memory_space=pltpu.VMEM)
    out_shape = [
        pltpu.VMEM((channels, size), pair.dtype) for _, size in cuts for _ in range(2)
    ]
    return pl.pallas_call(
        functools.partial(select_kernel, slots, a_slots.shape[0], cuts),
        out_shape=out_shape,
        in_specs=[smem, smem, smem, pl.BlockSpec(memory_space=pltpu.HBM)],
        out_specs=[vmem] * len(out_shape),
        scratch_shapes=[pltpu.SemaphoreType.DMA((len(out_shape),))],
        name="select_blocks",
    )(a_slots, b_slots, counts, pair)


def prepared(weight, gain=None):
    if gain is not None:
        weight = weight * gain
    rolled = pltpu.roll(weight, weight.shape[1] // 2, 1)
    return jnp.where(lax.axis_index("chan") == 0, weight, rolled).astype(BF16)


def gated_rows(w_ref):
    gate, value = w_ref[0].astype(F32), w_ref[1].astype(F32)
    rows = []
    for at in range(0, gate.shape[0], 8):
        rows += [gate[at : at + 8], value[at : at + 8]]
    return [0.5 * row for row in rows]


def normed_of(mine, theirs, gain=None):
    total = 2 * mine.shape[0]
    mine = mine.astype(F32)
    theirs = theirs.astype(F32)
    mean = jnp.sum(mine + theirs, axis=0, keepdims=True) * (1.0 / total)
    mine = mine - mean
    theirs = theirs - mean
    spread = jnp.sum(mine * mine + theirs * theirs, axis=0, keepdims=True) * (1.0 / total)
    scale = lax.rsqrt(spread + epsilon)
    mine = mine * scale
    theirs = theirs * scale
    if gain is not None:
        half = mine.shape[0]
        mine = mine * gain[:half]
        theirs = theirs * gain[half:]
    return jnp.concatenate([mine.astype(BF16), theirs.astype(BF16)], axis=0)


def gated_sides(mine, theirs, weight, gain, half):
    y = jnp.dot(weight, normed_of(mine, theirs, gain), preferred_element_type=F32)
    sides = []
    for side in range(2):
        groups = []
        for row in range(2 * half * side, 2 * half * (side + 1), 16):
            groups.append((jnp.tanh(y[row : row + 8]) + 1.0) * y[row + 8 : row + 16])
        sides.append(groups)
    return sides, y[4 * half :]


def pair_chunk(sides_at, chunk, held, half):
    low = lax.broadcasted_iota(jnp.int32, (8, LANES), 1) < BLK
    pitch = held[0].shape[0] // (chunk // BLK)
    for start in range(0, chunk, LANES):
        first, second = sides_at(start)
        i = start // BLK
        for out, values0, values1 in zip(held, first, second):
            for at, (v0, v1) in enumerate(zip(values0, values1)):
                even = slice(i * pitch + 8 * at, i * pitch + 8 * at + 8)
                odd = slice((i + 1) * pitch + 8 * at, (i + 1) * pitch + 8 * at + 8)
                out[even, :] = jnp.where(low, v0, pltpu.roll(v1, BLK, 1))
                out[odd, :] = jnp.where(low, pltpu.roll(v0, BLK, 1), v1)
        yield


def spread_chunk(chunk, held, l_ref, p_ref, pair_of, first_row, half):
    rows = chunk // BLK
    pitch = held[0].shape[0] // rows
    to = pl.ds(pl.multiple_of(first_row, 16), rows)
    for c in range(half):
        take = pl.ds(c, rows, stride=pitch)
        l_ref[pair_of, c, to, :] = held[0][take, :].astype(BF16)
        right = held[1][take, :].astype(BF16)
        p_ref[2 * pair_of, c, to, :] = right
        p_ref[2 * pair_of + 1, c, to, :] = pltpu.roll(right, BLK, 1)
        if c % 8 == 7:
            yield


def two_chunks(sides_at, n, chunk, held, l_ref, p_ref, pair_of, first_row, half):
    rows = chunk // BLK
    steps = [
        pair_chunk(functools.partial(sides_at, 2 * n + k), chunk, held[2 * k : 2 * k + 2], half)
        for k in range(2)
    ]
    spreads = [
        spread_chunk(
            chunk, held[2 * k : 2 * k + 2], l_ref, p_ref, pair_of, first_row + (2 * n + k) * rows, half
        )
        for k in range(2)
    ]
    for _ in steps[0]:
        pass
    for _ in zip(steps[1], spreads[0]):
        pass
    for _ in spreads[0]:
        pass
    for _ in spreads[1]:
        pass


def cells_at(n, chunk, start):
    return pl.ds(pl.multiple_of(n * chunk + start, LANES), LANES)


def own_kernel(chunk, *refs):
    t_ref = refs[0]
    sources = refs[1:8]
    l_ref, p_ref, gate_ref, w_ref, v_ref, gain_ref = refs[8:14]
    targets = refs[14:21]
    held, sems = refs[21:25], refs[25]
    copies = [
        pltpu.make_async_copy(source, target, sems.at[at])
        for at, (source, target) in enumerate(zip(sources, targets))
    ]
    for copy in copies:
        copy.start()
    half = l_ref.shape[1]

    @pl.loop(0, half)
    def _(c):
        p_ref[4, c] = jnp.zeros((BLK, LANES), BF16)

    for copy in copies:
        copy.wait()
    m_ref, a_ref, b_ref, o_ref, u_ref, g_ref, h_ref = targets
    rows = gated_rows(a_ref) + gated_rows(b_ref) + [0.5 * o_ref[...].astype(F32)]
    weight = prepared(jnp.concatenate(rows, axis=0))
    w_ref[...] = weight[: 4 * half]
    v_ref[...] = prepared(0.5 * u_ref[...].astype(F32), h_ref[...])
    across = jnp.transpose(jnp.broadcast_to(g_ref[...], (2 * half, LANES)))
    in_order = lax.axis_index("chan") == 0
    gain_ref[:half] = jnp.where(in_order, across[:half], across[half:])
    gain_ref[half:] = jnp.where(in_order, across[half:], across[:half])

    def sides_at(n, start):
        at = cells_at(n, chunk, start)
        both = []
        for x in range(2):
            sides, rest = gated_sides(m_ref[x, :, at], t_ref[x, :, at], weight, gain_ref[...], half)
            gate_ref[x, :, at] = (jnp.tanh(rest) + 1.0).astype(BF16)
            both.append(sides)
        return both

    @pl.loop(0, m_ref.shape[-1] // chunk // 2)
    def _(n):
        two_chunks(sides_at, n, chunk, held, l_ref, p_ref, 0, 0, half)


def both_kernel(chunk, first_row, m0, m1, *refs):
    theirs = refs[:-10]
    w_ref, gain_ref, _, _, l_ref, p_ref = refs[-10:-4]
    held = refs[-4:]
    half = l_ref.shape[1]
    weight = w_ref[...]
    wide = theirs[0].shape[1]

    def sides_at(n, start):
        at = n * chunk + start
        both = []
        for x, m in enumerate((m0, m1)):
            other = theirs[2 * (at // wide) + x][:, at % wide : at % wide + LANES]
            both.append(
                gated_sides(m[:, at : at + LANES], other, weight, gain_ref[...], half)[0]
            )
        return both

    two_chunks(sides_at, 0, chunk, held, l_ref, p_ref, 1, first_row, half)


def operand_shapes(half):
    return [pltpu.VMEM((2, half, BLK, LANES), BF16), pltpu.VMEM((5, half, BLK, LANES), BF16)]


def chunk_scratch(half, chunk):
    return [pltpu.VMEM((chunk // BLK * (half + 8), LANES), F32)] * 4


def call(kernel, name, operands, out_shape, scratch, aliased=0, hbm=0):
    vmem = pl.BlockSpec(memory_space=pltpu.VMEM)
    plain = len(operands) - aliased
    operands = operands[:plain] + [
        pltpu.with_memory_space_constraint(value, pltpu.VMEM) for value in operands[plain:]
    ]
    operands = operands[: len(operands) - hbm] + [
        pltpu.with_memory_space_constraint(value, pltpu.HBM)
        for value in operands[len(operands) - hbm :]
    ]
    specs = [vmem] * (len(operands) - hbm) + [pl.BlockSpec(memory_space=pltpu.HBM)] * hbm
    return pl.pallas_call(
        kernel,
        in_specs=specs,
        out_specs=[vmem] * len(out_shape),
        out_shape=out_shape,
        scratch_shapes=scratch,
        input_output_aliases={plain + at: at for at in range(aliased)},
        compiler_params=pltpu.CompilerParams(vmem_limit_bytes=VMEM_LIMIT),
        name=name,
    )(*operands)


def triplet_kernel(slots, triplets, group, first, a_ref, b_ref, n_ref, l_ref, p_ref, *refs):
    outs, acc = blocks_of(refs[:-1]), refs[-1]
    me, behind, ahead = neighbour_tiles()
    low = lax.broadcasted_iota(jnp.int32, (BLK, LANES), 1) < BLK
    picks = []
    for s in range(slots):
        block = me * slots + s
        count = n_ref[block]
        for pair_at in range(2):
            for part in range(2):
                chosen = jnp.int32(0)
                used = jnp.int32(0)
                for m in range(triplets):
                    left = a_ref[m, block]
                    if pair_at == 0:
                        hit = left == me * slots + part
                    else:
                        base = (behind, ahead)[part] * slots
                        hit = jnp.logical_and(left >= base, left < base + slots)
                    hit = jnp.logical_and(hit, m < count)
                    place = b_ref[m, block] - me * slots
                    from_me = jnp.logical_and(place >= 0, place < slots)
                    right = b_ref[m, block] - behind * slots
                    from_behind = jnp.logical_and(right >= 0, right < slots)
                    place = jnp.where(from_me, place, jnp.where(from_behind, 2, 3))
                    chosen = jnp.where(hit, place, chosen)
                    used = jnp.where(hit, 1, used)
                if part == 1:
                    chosen = chosen + 1 - 2 * (chosen & 1)
                picks.append(jnp.where(used == 1, chosen, 4))

    take_low = lax.broadcasted_iota(jnp.int32, (group, LANES), 1) < BLK
    pitch = acc.shape[0] // BLK

    @pl.loop(0, outs[0].shape[0], step=group)
    def _(base):
        for at in range(group):
            c = first + base + at
            lhs = jnp.concatenate([l_ref[0, c], l_ref[1, c]], axis=1)
            parts = [p_ref[pick, c] for pick in picks]
            tiles = [jnp.where(low, parts[k], parts[k + 1]) for k in range(0, len(parts), 2)]
            rhs = jnp.concatenate(
                [jnp.concatenate(tiles[k : k + 2], axis=1) for k in range(0, len(tiles), 2)], axis=0
            )
            acc[pl.ds(at, BLK, stride=pitch), :] = lax.dot_general(
                lhs, rhs, (((1,), (1,)), ((), ())), preferred_element_type=F32
            )
        rows = pl.ds(pl.multiple_of(base, group), group)
        for t in range(BLK // 2):
            even = acc[2 * t * pitch : 2 * t * pitch + group, :]
            odd = acc[(2 * t + 1) * pitch : (2 * t + 1) * pitch + group, :]
            to = slice(t * LANES, (t + 1) * LANES)
            outs[0][rows, to] = jnp.where(take_low, even, pltpu.roll(odd, BLK, 1)).astype(BF16)
            outs[1][rows, to] = jnp.where(take_low, pltpu.roll(even, BLK, 1), odd).astype(BF16)


def blocks_of(refs):
    return [refs[0].at[0], refs[0].at[1]] if len(refs) == 1 else list(refs)


def triplet_sum(first, out_shape, lefts, rights, a_slots, b_slots, counts, slots, group):
    smem = pl.BlockSpec(memory_space=pltpu.SMEM)
    vmem = pl.BlockSpec(memory_space=pltpu.VMEM)
    lefts, rights = (
        pltpu.with_memory_space_constraint(value, pltpu.VMEM) for value in (lefts, rights)
    )
    return pl.pallas_call(
        functools.partial(triplet_kernel, slots, a_slots.shape[0], group, first),
        in_specs=[smem, smem, smem, vmem, vmem],
        out_specs=[vmem] * len(out_shape),
        out_shape=out_shape,
        scratch_shapes=[pltpu.VMEM((BLK * (group + 8), LANES), F32)],
        compiler_params=pltpu.CompilerParams(vmem_limit_bytes=VMEM_LIMIT),
        name="triplets",
    )(a_slots, b_slots, counts, lefts, rights)


def finish_kernel(steps, *refs):
    sides = [[blocks_of(refs[at : at + 1]), blocks_of(refs[at + 1 : at + 3])] for at in (0, 3)]
    gate_ref, w_ref, out_ref, held, sems = refs[6:]
    weight = w_ref[...]
    slots, half, cells = gate_ref.shape
    size = cells // steps

    def copy(s, n):
        to = pl.ds(pl.multiple_of(n * size, size), size)
        return pltpu.make_async_copy(held.at[s, :, to], out_ref.at[s, :, to], sems.at[s, n])

    for s in range(slots):

        @pl.loop(0, steps)
        def _(n):
            for start in range(0, size, LANES):
                to = pl.ds(pl.multiple_of(n * size + start, LANES), LANES)
                mine, theirs = (
                    jnp.concatenate([blocks[s][:, to] for blocks in side], axis=0) for side in sides
                )
                projected = jnp.dot(
                    weight, normed_of(mine, theirs), preferred_element_type=F32
                )
                held[s, :, to] = (gate_ref[s, :, to].astype(F32) * projected).astype(BF16)
            copy(s, n).start()

    for s in range(slots):

        @pl.loop(0, steps)
        def _(n):
            copy(s, n).wait()


def finish(mine, theirs, gate, weight, steps):
    vmem = pl.BlockSpec(memory_space=pltpu.VMEM)
    operands = [*mine, *theirs, gate, weight]
    return pl.pallas_call(
        functools.partial(finish_kernel, steps),
        in_specs=[vmem] * len(operands),
        out_specs=pl.BlockSpec(memory_space=pltpu.HBM),
        out_shape=jax.ShapeDtypeStruct(gate.shape, BF16),
        scratch_shapes=[
            pltpu.VMEM(gate.shape, BF16),
            pltpu.SemaphoreType.DMA((gate.shape[0], steps)),
        ],
        compiler_params=pltpu.CompilerParams(vmem_limit_bytes=VMEM_LIMIT),
        name="finish",
    )(*operands)


def per_device(
    pair,
    ln_in_gain,
    a_weight,
    b_weight,
    ln_out_gain,
    out_gate_weight,
    out_weight,
    a_slots,
    b_slots,
    counts,
):
    slots, half, cells = pair.shape
    rows = lax.axis_size("row")
    swap = [(0, 1), (1, 0)]
    up = [(i, (i + 1) % rows) for i in range(rows)]
    down = [(i, (i - 1) % rows) for i in range(rows)]

    a_slots, b_slots = a_slots.T, b_slots.T
    weights = [
        jnp.swapaxes(a_weight, 1, 2),
        jnp.swapaxes(b_weight, 1, 2),
        out_gate_weight.T,
        out_weight.T,
        ln_in_gain[None, :],
        ln_out_gain[None, :],
    ]

    pair_other = lax.ppermute(pair, "chan", swap)
    cuts = ((0, cells // 2), (cells // 2, cells // 2))
    chosen = select_blocks(pair, a_slots, b_slots, counts, cuts)
    arrived = [
        (lax.ppermute(chosen[2 * n], "row", up), lax.ppermute(chosen[2 * n + 1], "row", down))
        for n in range(len(cuts))
    ]
    chunk = cells // 4
    sources = [pair, *weights]
    lefts, rights, gate, weight, last_weight, gain = call(
        functools.partial(own_kernel, chunk),
        "project_own",
        [pair_other, *sources],
        operand_shapes(half)
        + [
            pltpu.VMEM((slots, half, cells), BF16),
            pltpu.VMEM((4 * half, 2 * half), BF16),
            pltpu.VMEM((half, 2 * half), BF16),
            pltpu.VMEM((2 * half, LANES), F32),
        ],
        [pltpu.VMEM(value.shape, value.dtype) for value in sources]
        + chunk_scratch(half, chunk)
        + [pltpu.SemaphoreType.DMA((len(sources),))],
        hbm=len(sources),
    )
    for (start, size), behind_ahead in zip(cuts, arrived):
        *behind_ahead, lefts = lax.optimization_barrier((*behind_ahead, lefts))
        wide = chunk if start == 0 else size
        others = [
            lax.ppermute(lax.slice_in_dim(value, at, at + wide, axis=1), "chan", swap)
            for at in range(0, size, wide)
            for value in behind_ahead
        ]
        lefts, rights = call(
            functools.partial(both_kernel, chunk, start // BLK),
            "project_fetched",
            [*behind_ahead, *others, weight, gain, lefts, rights],
            operand_shapes(half),
            chunk_scratch(half, chunk),
            aliased=2,
        )
    mine, theirs = [], []
    wide = half // 2
    for first, out_shape in (
        (0, [pltpu.VMEM((slots, wide, cells), BF16)]),
        (wide, [pltpu.VMEM((wide, cells), BF16)] * slots),
    ):
        update, *rest = triplet_sum(
            first, out_shape, lefts, rights, a_slots, b_slots, counts, slots, 16
        )
        mine += [update, *rest]
        theirs += [lax.ppermute(value, "chan", swap) for value in (update, *rest)]
        update, lefts = lax.optimization_barrier((update, lefts))
    return finish(mine, theirs, gate, last_weight, 4)


def solution(mesh):
    in_specs = (
        P(("parts", "row", "col"), "chan", None),
        P(),
        P(None, None, "chan"),
        P(None, None, "chan"),
        P(),
        P(None, "chan"),
        P(None, "chan"),
        P("parts", None),
        P("parts", None),
        P("parts"),
    )
    out_specs = P(("parts", "row", "col"), "chan", None)
    return jax.shard_map(
        per_device, mesh=mesh, in_specs=in_specs, out_specs=out_specs, check_vma=False
    )
```

```python
import functools

import jax
import jax.numpy as jnp
from jax import lax
from jax.experimental import pallas as pl
from jax.experimental.pallas import tpu as pltpu
from jax.sharding import PartitionSpec as P

BLK = 64
LANES = 128
epsilon = 1e-05
VMEM_LIMIT = 24 * 1024 * 1024
F32 = jnp.float32
BF16 = jnp.bfloat16


def sigmoid(x):
    return 0.5 * jnp.tanh(0.5 * x) + 0.5


def tile_of(row, col):
    return row * lax.axis_size("col") + col


def neighbour_tiles():
    rows = lax.axis_size("row")
    row, col = lax.axis_index("row"), lax.axis_index("col")
    behind = lax.rem(row + rows - 1, rows)
    ahead = lax.rem(row + 1, rows)
    return tile_of(row, col), tile_of(behind, col), tile_of(ahead, col)


def select_kernel(slots, triplets, cuts, a_hbm, b_hbm, n_hbm, pair_hbm, *refs):
    pair_ref, *out_refs = refs[: 1 + 2 * len(cuts)]
    a_ref, b_ref, n_ref, sems = refs[1 + 2 * len(cuts) :]
    me, behind, ahead = neighbour_tiles()
    whole = pltpu.make_async_copy(pair_hbm, pair_ref, sems.at[0])
    tables = [
        pltpu.make_async_copy(source, target, sems.at[1 + at])
        for at, (source, target) in enumerate(((a_hbm, a_ref), (b_hbm, b_ref), (n_hbm, n_ref)))
    ]
    for copy in (*tables, whole):
        copy.start()
    for copy in tables:
        copy.wait()
    picks = []
    for target in (ahead, behind):
        pick = jnp.int32(0)
        for s in range(slots):
            count = n_ref[target * slots + s]
            for m in range(triplets):
                for ids in (a_ref, b_ref):
                    name = ids[m, target * slots + s] - me * slots
                    mine = jnp.logical_and(name >= 0, name < slots)
                    pick = jnp.where(jnp.logical_and(m < count, mine), name, pick)
        picks.append(pick)
    whole.wait()
    for at, (start, size) in enumerate(cuts):
        for which, pick in enumerate(picks):
            out_refs[2 * at + which][...] = pair_ref[pick, :, start : start + size]


def select_blocks(pair, a_slots, b_slots, counts, cuts):
    slots, channels, cells = pair.shape
    hbm = pl.BlockSpec(memory_space=pltpu.HBM)
    vmem = pl.BlockSpec(memory_space=pltpu.VMEM)
    out_shape = [pltpu.VMEM(pair.shape, pair.dtype)] + [
        pltpu.VMEM((channels, size), pair.dtype) for _, size in cuts for _ in range(2)
    ]
    operands = [
        pltpu.with_memory_space_constraint(value, pltpu.HBM)
        for value in (a_slots, b_slots, counts, pair)
    ]
    return pl.pallas_call(
        functools.partial(select_kernel, slots, a_slots.shape[0], cuts),
        out_shape=out_shape,
        in_specs=[hbm] * 4,
        out_specs=[vmem] * len(out_shape),
        scratch_shapes=[pltpu.SMEM(value.shape, value.dtype) for value in operands[:3]]
        + [pltpu.SemaphoreType.DMA((4,))],
        name="select_blocks",
    )(*operands)


def prepared(weight, gain=None):
    if gain is not None:
        weight = weight * gain
    rolled = pltpu.roll(weight, weight.shape[1] // 2, 1)
    return jnp.where(lax.axis_index("chan") == 0, weight, rolled).astype(BF16)


def gated_rows(w_ref):
    gate, value = w_ref[0].astype(F32), w_ref[1].astype(F32)
    rows = []
    for at in range(0, gate.shape[0], 8):
        rows += [gate[at : at + 8], value[at : at + 8]]
    return [0.5 * row for row in rows]


def normed_of(mine, theirs, gain=None):
    total = 2 * mine.shape[0]
    mine = mine.astype(F32)
    theirs = theirs.astype(F32)
    mean = jnp.sum(mine + theirs, axis=0, keepdims=True) * (1.0 / total)
    mine = mine - mean
    theirs = theirs - mean
    spread = jnp.sum(mine * mine + theirs * theirs, axis=0, keepdims=True) * (1.0 / total)
    scale = lax.rsqrt(spread + epsilon)
    mine = mine * scale
    theirs = theirs * scale
    if gain is not None:
        half = mine.shape[0]
        mine = mine * gain[:half]
        theirs = theirs * gain[half:]
    return jnp.concatenate([mine.astype(BF16), theirs.astype(BF16)], axis=0)


def gated_sides(mine, theirs, weight, gain, half):
    y = jnp.dot(weight, normed_of(mine, theirs, gain), preferred_element_type=F32)
    sides = []
    for side in range(2):
        groups = []
        for row in range(2 * half * side, 2 * half * (side + 1), 16):
            groups.append((jnp.tanh(y[row : row + 8]) + 1.0) * y[row + 8 : row + 16])
        sides.append(groups)
    return sides, y[4 * half :]


def pair_chunk(sides_at, chunk, held):
    low = lax.broadcasted_iota(jnp.int32, (8, LANES), 1) < BLK
    pitch = held[0].shape[0] // (chunk // BLK)
    for start in range(0, chunk, LANES):
        first, second = sides_at(start)
        i = start // BLK
        for out, values0, values1 in zip(held, first, second):
            for at, (v0, v1) in enumerate(zip(values0, values1)):
                even = slice(i * pitch + 8 * at, i * pitch + 8 * at + 8)
                odd = slice((i + 1) * pitch + 8 * at, (i + 1) * pitch + 8 * at + 8)
                out[even, :] = jnp.where(low, v0, pltpu.roll(v1, BLK, 1))
                out[odd, :] = jnp.where(low, pltpu.roll(v0, BLK, 1), v1)
        yield


def spread_chunk(rows, held, l_ref, pair_of, l_row, p_ref, p_row, before, turned_ref, half):
    pitch = held[0].shape[0] // rows
    to = pl.ds(pl.multiple_of(l_row, 16), rows)
    for c in range(half):
        take = pl.ds(c, rows, stride=pitch)
        l_ref[pair_of, c, to, :] = held[0][take, :].astype(BF16)
        right = held[1][take, :]
        if turned_ref is None:
            p_ref[c, pl.ds(pl.multiple_of(p_row, 16), rows), :] = right.astype(BF16)
        else:
            whole = jnp.concatenate([ref[c, :size].astype(F32) for ref, size in before] + [right])
            turned = jnp.transpose(whole).astype(BF16)
            turned_ref[2 * pair_of, c] = turned[:BLK]
            turned_ref[2 * pair_of + 1, c] = turned[BLK:]
        if c % 8 == 7:
            yield


def two_chunks(sides_at, n, chunk, held, spread):
    steps = [
        pair_chunk(functools.partial(sides_at, n + k), chunk, held[2 * k : 2 * k + 2])
        for k in range(2)
    ]
    spreads = [spread(n + k, held[2 * k : 2 * k + 2], k) for k in range(2)]
    for _ in steps[0]:
        pass
    for _ in zip(steps[1], spreads[0]):
        pass
    for _ in spreads[0]:
        pass
    for _ in spreads[1]:
        pass


def cells_at(n, chunk, start):
    return pl.ds(pl.multiple_of(n * chunk + start, LANES), LANES)


def own_kernel(chunk, *refs):
    m_ref, t_ref = refs[:2]
    sources = refs[2:8]
    l_ref, turned_ref, gate_ref, w_ref, v_ref, gain_ref = refs[8:14]
    targets = refs[14:20]
    p_ref, held, sems = refs[20], refs[21:25], refs[25]
    copies = [
        pltpu.make_async_copy(source, target, sems.at[at])
        for at, (source, target) in enumerate(zip(sources, targets))
    ]
    for copy in copies:
        copy.start()
    half = l_ref.shape[1]

    @pl.loop(0, half)
    def _(c):
        turned_ref[4, c] = jnp.zeros((BLK, BLK), BF16)

    for copy in copies:
        copy.wait()
    a_ref, b_ref, o_ref, u_ref, g_ref, h_ref = targets
    rows = gated_rows(a_ref) + gated_rows(b_ref) + [0.5 * o_ref[...].astype(F32)]
    weight = prepared(jnp.concatenate(rows, axis=0))
    w_ref[...] = weight[: 4 * half]
    v_ref[...] = prepared(0.5 * u_ref[...].astype(F32), h_ref[...])
    across = jnp.transpose(jnp.broadcast_to(g_ref[...], (2 * half, LANES)))
    in_order = lax.axis_index("chan") == 0
    gain_ref[:half] = jnp.where(in_order, across[:half], across[half:])
    gain_ref[half:] = jnp.where(in_order, across[half:], across[:half])
    chunks = m_ref.shape[-1] // chunk
    rows = chunk // BLK

    def sides_at(n, start):
        at = cells_at(n, chunk, start)
        both = []
        for x in range(2):
            sides, rest = gated_sides(m_ref[x, :, at], t_ref[x, :, at], weight, gain_ref[...], half)
            gate_ref[x, :, at] = (jnp.tanh(rest) + 1.0).astype(BF16)
            both.append(sides)
        return both

    def spread(last, n, held, k):
        before, turned = ([(p_ref, (chunks - 1) * rows)], turned_ref) if last and k else (None, None)
        return spread_chunk(rows, held, l_ref, 0, n * rows, p_ref, n * rows, before, turned, half)

    @pl.loop(0, chunks - 2, step=2)
    def _(n):
        two_chunks(sides_at, n, chunk, held, functools.partial(spread, False))

    two_chunks(sides_at, chunks - 2, chunk, held, functools.partial(spread, True))


def fetched_kernel(chunk, first_row, last, m0, m1, *refs):
    if last:
        *theirs, p0_ref, w_ref, gain_ref, _, _, l_ref, turned_ref, p_ref = refs[:-4]
        before = [(p0_ref, p0_ref.shape[1]), (p_ref, p_ref.shape[1])]
    else:
        *theirs, w_ref, gain_ref, _, l_ref, p_ref = refs[:-4]
    held = refs[-4:]
    half = l_ref.shape[1]
    weight = w_ref[...]
    wide = theirs[0].shape[1]
    rows = chunk // BLK

    def sides_at(n, start):
        at = n * chunk + start
        both = []
        for x, m in enumerate((m0, m1)):
            other = theirs[2 * (at // wide) + x][:, at % wide : at % wide + LANES]
            both.append(
                gated_sides(m[:, at : at + LANES], other, weight, gain_ref[...], half)[0]
            )
        return both

    def spread(n, held, k):
        done = (before, turned_ref) if last and k else (None, None)
        return spread_chunk(rows, held, l_ref, 1, first_row + n * rows, p_ref, n * rows, *done, half)

    two_chunks(sides_at, 0, chunk, held, spread)


def chunk_scratch(half, chunk):
    return [pltpu.VMEM((chunk // BLK * (half + 8), LANES), F32)] * 4


def call(kernel, name, operands, out_shape, scratch, aliased=0, hbm=0):
    vmem = pl.BlockSpec(memory_space=pltpu.VMEM)
    plain = len(operands) - aliased
    operands = operands[:plain] + [
        pltpu.with_memory_space_constraint(value, pltpu.VMEM) for value in operands[plain:]
    ]
    operands = operands[: len(operands) - hbm] + [
        pltpu.with_memory_space_constraint(value, pltpu.HBM)
        for value in operands[len(operands) - hbm :]
    ]
    specs = [vmem] * (len(operands) - hbm) + [pl.BlockSpec(memory_space=pltpu.HBM)] * hbm
    return pl.pallas_call(
        kernel,
        in_specs=specs,
        out_specs=[vmem] * len(out_shape),
        out_shape=out_shape,
        scratch_shapes=scratch,
        input_output_aliases={plain + at: at for at in range(aliased)},
        compiler_params=pltpu.CompilerParams(vmem_limit_bytes=VMEM_LIMIT),
        name=name,
    )(*operands)


def triplet_kernel(s, slots, triplets, group, a_ref, b_ref, n_ref, l_ref, turned_ref, out_ref, *accs):
    me, behind, ahead = neighbour_tiles()
    block = me * slots + s
    count = n_ref[block]
    picks = []
    for pair_at in range(2):
        for part in range(2):
            chosen = jnp.int32(0)
            used = jnp.int32(0)
            for m in range(triplets):
                left = a_ref[m, block]
                if pair_at == 0:
                    hit = left == me * slots + part
                else:
                    first = (behind, ahead)[part] * slots
                    hit = jnp.logical_and(left >= first, left < first + slots)
                hit = jnp.logical_and(hit, m < count)
                place = b_ref[m, block] - me * slots
                from_me = jnp.logical_and(place >= 0, place < slots)
                right = b_ref[m, block] - behind * slots
                from_behind = jnp.logical_and(right >= 0, right < slots)
                place = jnp.where(from_me, place, jnp.where(from_behind, 2, 3))
                chosen = jnp.where(hit, place, chosen)
                used = jnp.where(hit, 1, used)
            picks.append(jnp.where(used == 1, chosen, 4))

    take_low = lax.broadcasted_iota(jnp.int32, (group, LANES), 1) < BLK
    half = l_ref.shape[1]
    pitch = accs[0].shape[0] // BLK

    @pl.loop(0, half, step=group * len(accs))
    def _(base):
        for which, acc in enumerate(accs):
            for at in range(group):
                c = base + which * group + at
                lhs = jnp.concatenate([l_ref[0, c], l_ref[1, c]], axis=1)
                rhs = jnp.concatenate([turned_ref[pick, c] for pick in picks], axis=0)
                acc[pl.ds(at, BLK, stride=pitch), :BLK] = jnp.dot(
                    lhs, rhs, preferred_element_type=F32
                )
            rows = pl.ds(pl.multiple_of(base + which * group, group), group)
            for t in range(BLK // 2):
                even = acc[2 * t * pitch : 2 * t * pitch + group, :]
                odd = acc[(2 * t + 1) * pitch : (2 * t + 1) * pitch + group, :]
                out_ref[rows, t * LANES : (t + 1) * LANES] = jnp.where(
                    take_low, even, pltpu.roll(odd, BLK, 1)
                ).astype(BF16)


def triplet_sum(s, lefts, rights, a_slots, b_slots, counts, slots, group):
    half = lefts.shape[1]
    smem = pl.BlockSpec(memory_space=pltpu.SMEM)
    vmem = pl.BlockSpec(memory_space=pltpu.VMEM)
    lefts, rights = (
        pltpu.with_memory_space_constraint(value, pltpu.VMEM) for value in (lefts, rights)
    )
    return pl.pallas_call(
        functools.partial(triplet_kernel, s, slots, a_slots.shape[0], group),
        in_specs=[smem, smem, smem, vmem, vmem],
        out_specs=vmem,
        out_shape=pltpu.VMEM((half, BLK * BLK), BF16),
        scratch_shapes=[pltpu.VMEM((BLK * (group + 8), LANES), F32)] * 2,
        compiler_params=pltpu.CompilerParams(vmem_limit_bytes=VMEM_LIMIT),
        name="triplets",
    )(a_slots, b_slots, counts, lefts, rights)


def finish_kernel(s, mine_ref, theirs_ref, gate_ref, w_ref, *refs):
    weight = w_ref[...]
    cells = mine_ref.shape[-1]
    if s == 0:
        held = refs[0]
        steps = 4
    else:
        before_ref, out_ref, held, sems = refs
        steps = sems.shape[0] - 1
        before = pltpu.make_async_copy(before_ref, out_ref.at[0], sems.at[steps])
        before.start()
    size = cells // steps

    def copy(n):
        to = pl.ds(pl.multiple_of(n * size, size), size)
        return pltpu.make_async_copy(held.at[:, to], out_ref.at[1, :, to], sems.at[n])

    @pl.loop(0, steps)
    def _(n):
        for start in range(0, size, LANES):
            to = pl.ds(pl.multiple_of(n * size + start, LANES), LANES)
            normed = normed_of(mine_ref[:, to], theirs_ref[:, to])
            projected = jnp.dot(weight, normed, preferred_element_type=F32)
            held[:, to] = (gate_ref[s, :, to].astype(F32) * projected).astype(BF16)
        if s > 0:
            copy(n).start()

    if s > 0:

        @pl.loop(0, steps)
        def _(n):
            copy(n).wait()

        before.wait()


def finish(s, mine, theirs, gate, weight, before=None):
    vmem = pl.BlockSpec(memory_space=pltpu.VMEM)
    operands = [mine, theirs, gate, weight]
    if s == 0:
        out_shape, out_specs, scratch = pltpu.VMEM(mine.shape, BF16), vmem, []
    else:
        operands.append(before)
        out_shape = jax.ShapeDtypeStruct(gate.shape, BF16)
        out_specs = pl.BlockSpec(memory_space=pltpu.HBM)
        scratch = [pltpu.VMEM(mine.shape, BF16), pltpu.SemaphoreType.DMA((5,))]
    return pl.pallas_call(
        functools.partial(finish_kernel, s),
        in_specs=[vmem] * len(operands),
        out_specs=out_specs,
        out_shape=out_shape,
        scratch_shapes=scratch,
        compiler_params=pltpu.CompilerParams(vmem_limit_bytes=VMEM_LIMIT),
        name="finish",
    )(*operands)


def per_device(
    pair,
    ln_in_gain,
    a_weight,
    b_weight,
    ln_out_gain,
    out_gate_weight,
    out_weight,
    a_slots,
    b_slots,
    counts,
):
    slots, half, cells = pair.shape
    rows = lax.axis_size("row")
    swap = [(0, 1), (1, 0)]
    up = [(i, (i + 1) % rows) for i in range(rows)]
    down = [(i, (i - 1) % rows) for i in range(rows)]

    a_slots, b_slots = a_slots.T, b_slots.T
    weights = [
        jnp.swapaxes(a_weight, 1, 2),
        jnp.swapaxes(b_weight, 1, 2),
        out_gate_weight.T,
        out_weight.T,
        ln_in_gain[None, :],
        ln_out_gain[None, :],
    ]

    chunk = cells // 4
    cuts = ((0, 2 * chunk), (2 * chunk, 2 * chunk))
    pair, *chosen = select_blocks(pair, a_slots, b_slots, counts, cuts)
    arrived = [
        (lax.ppermute(chosen[2 * n], "row", up), lax.ppermute(chosen[2 * n + 1], "row", down))
        for n in range(len(cuts))
    ]
    pair_other = lax.ppermute(pair, "chan", swap)
    left_shape = pltpu.VMEM((2, half, BLK, LANES), BF16)
    right_shape = pltpu.VMEM((5, half, BLK, BLK), BF16)
    lefts, rights, gate, weight, last_weight, gain = call(
        functools.partial(own_kernel, chunk),
        "project_own",
        [pair, pair_other, *weights],
        [
            left_shape,
            right_shape,
            pltpu.VMEM((slots, half, cells), BF16),
            pltpu.VMEM((4 * half, 2 * half), BF16),
            pltpu.VMEM((half, 2 * half), BF16),
            pltpu.VMEM((2 * half, LANES), F32),
        ],
        [pltpu.VMEM(value.shape, value.dtype) for value in weights]
        + [pltpu.VMEM((half, BLK, LANES), BF16)]
        + chunk_scratch(half, chunk)
        + [pltpu.SemaphoreType.DMA((len(weights),))],
        hbm=len(weights),
    )
    for (start, size), behind_ahead in zip(cuts, arrived):
        *behind_ahead, lefts = lax.optimization_barrier((*behind_ahead, lefts))
        wide = chunk if start == 0 else size
        others = [
            lax.ppermute(lax.slice_in_dim(value, at, at + wide, axis=1), "chan", swap)
            for at in range(0, size, wide)
            for value in behind_ahead
        ]
        paired = pltpu.VMEM((half, size // BLK, LANES), BF16)
        if start == 0:
            lefts, rights_first = call(
                functools.partial(fetched_kernel, chunk, 0, False),
                "project_first",
                [*behind_ahead, *others, weight, gain, lefts],
                [left_shape, paired],
                chunk_scratch(half, chunk),
                aliased=1,
            )
        else:
            lefts, rights = call(
                functools.partial(fetched_kernel, chunk, start // BLK, True),
                "project_last",
                [*behind_ahead, *others, rights_first, weight, gain, lefts, rights],
                [left_shape, right_shape],
                [pltpu.VMEM((half, chunk // BLK, LANES), BF16)] + chunk_scratch(half, chunk),
                aliased=2,
            )
    updates = []
    for s in range(slots):
        update = triplet_sum(s, lefts, rights, a_slots, b_slots, counts, slots, 16)
        updates.append((update, lax.ppermute(update, "chan", swap)))
        if s + 1 < slots:
            update, lefts = lax.optimization_barrier((update, lefts))
    out = None
    for s, (mine, theirs) in enumerate(updates):
        out = finish(s, mine, theirs, gate, last_weight, out)
    return out


def solution(mesh):
    in_specs = (
        P(("parts", "row", "col"), "chan", None),
        P(),
        P(None, None, "chan"),
        P(None, None, "chan"),
        P(),
        P(None, "chan"),
        P(None, "chan"),
        P("parts", None),
        P("parts", None),
        P("parts"),
    )
    out_specs = P(("parts", "row", "col"), "chan", None)
    return jax.shard_map(
        per_device, mesh=mesh, in_specs=in_specs, out_specs=out_specs, check_vma=False
    )
```

```python
import functools

import jax
import jax.numpy as jnp
from jax import lax
from jax.experimental import pallas as pl
from jax.experimental.pallas import tpu as pltpu
from jax.sharding import PartitionSpec as P

BLK = 64
LANES = 128
epsilon = 1e-05
VMEM_LIMIT = 24 * 1024 * 1024
F32 = jnp.float32
BF16 = jnp.bfloat16


def sigmoid(x):
    return 0.5 * jnp.tanh(0.5 * x) + 0.5


def tile_of(row, col):
    return row * lax.axis_size("col") + col


def neighbour_tiles():
    rows = lax.axis_size("row")
    row, col = lax.axis_index("row"), lax.axis_index("col")
    behind = lax.rem(row + rows - 1, rows)
    ahead = lax.rem(row + 1, rows)
    return tile_of(row, col), tile_of(behind, col), tile_of(ahead, col)


def used_picks(s, slots, triplets, a_ref, b_ref, n_ref):
    me, behind, ahead = neighbour_tiles()
    block = me * slots + s
    count = n_ref[block]
    picks = []
    for left_at in range(4):
        pick = jnp.int32(4)
        for m in range(triplets):
            left = a_ref[m, block]
            if left_at < 2:
                hit = left == me * slots + left_at
            else:
                base = (behind, ahead)[left_at - 2] * slots
                hit = jnp.logical_and(left >= base, left < base + slots)
            hit = jnp.logical_and(hit, m < count)
            place = b_ref[m, block] - me * slots
            from_me = jnp.logical_and(place >= 0, place < slots)
            right = b_ref[m, block] - behind * slots
            from_behind = jnp.logical_and(right >= 0, right < slots)
            place = jnp.where(from_me, place, jnp.where(from_behind, 2, 3))
            pick = jnp.where(hit, place, pick)
        picks.append(pick)
    return picks


def select_kernel(slots, triplets, cuts, a_hbm, b_hbm, n_hbm, pair_hbm, *refs):
    picks_ref, pair_ref, *out_refs = refs[: 2 + 3 * len(cuts)]
    a_ref, b_ref, n_ref, sems = refs[2 + 3 * len(cuts) :]
    me, behind, ahead = neighbour_tiles()
    whole = pltpu.make_async_copy(pair_hbm, pair_ref, sems.at[0])
    tables = [
        pltpu.make_async_copy(source, target, sems.at[1 + at])
        for at, (source, target) in enumerate(((a_hbm, a_ref), (b_hbm, b_ref), (n_hbm, n_ref)))
    ]
    for copy in (*tables, whole):
        copy.start()
    for copy in tables:
        copy.wait()
    chosen = []
    for target in (ahead, behind):
        pick = jnp.int32(0)
        for s in range(slots):
            count = n_ref[target * slots + s]
            for m in range(triplets):
                for ids in (a_ref, b_ref):
                    name = ids[m, target * slots + s] - me * slots
                    mine = jnp.logical_and(name >= 0, name < slots)
                    pick = jnp.where(jnp.logical_and(m < count, mine), name, pick)
        chosen.append(pick)
    chosen.append(jnp.where(lax.axis_index("row") == 0, chosen[1], chosen[0]))
    for s in range(slots):
        for at, pick in enumerate(used_picks(s, slots, triplets, a_ref, b_ref, n_ref)):
            picks_ref[4 * s + at] = pick
    whole.wait()
    for at, (start, size) in enumerate(cuts):
        for which, pick in enumerate(chosen):
            out_refs[3 * at + which][...] = pair_ref[pick, :, start : start + size]


def select_blocks(pair, a_slots, b_slots, counts, cuts):
    slots, channels, cells = pair.shape
    hbm = pl.BlockSpec(memory_space=pltpu.HBM)
    vmem = pl.BlockSpec(memory_space=pltpu.VMEM)
    out_shape = [pltpu.SMEM((4 * slots,), jnp.int32), pltpu.VMEM(pair.shape, pair.dtype)] + [
        pltpu.VMEM((channels, size), pair.dtype) for _, size in cuts for _ in range(3)
    ]
    operands = [
        pltpu.with_memory_space_constraint(value, pltpu.HBM)
        for value in (a_slots, b_slots, counts, pair)
    ]
    return pl.pallas_call(
        functools.partial(select_kernel, slots, a_slots.shape[0], cuts),
        out_shape=out_shape,
        in_specs=[hbm] * 4,
        out_specs=[pl.BlockSpec(memory_space=pltpu.SMEM)] + [vmem] * (len(out_shape) - 1),
        scratch_shapes=[pltpu.SMEM(value.shape, value.dtype) for value in operands[:3]]
        + [pltpu.SemaphoreType.DMA((4,))],
        name="select_blocks",
    )(*operands)


def prepared(weight, gain=None):
    if gain is not None:
        weight = weight * gain
    rolled = pltpu.roll(weight, weight.shape[1] // 2, 1)
    return jnp.where(lax.axis_index("chan") == 0, weight, rolled).astype(BF16)


def gated_rows(w_ref):
    gate, value = w_ref[0].astype(F32), w_ref[1].astype(F32)
    rows = []
    for at in range(0, gate.shape[0], 8):
        rows += [gate[at : at + 8], value[at : at + 8]]
    return [0.5 * row for row in rows]


def normed_of(mine, theirs, gain=None):
    total = 2 * mine.shape[0]
    mine = mine.astype(F32)
    theirs = theirs.astype(F32)
    mean = jnp.sum(mine + theirs, axis=0, keepdims=True) * (1.0 / total)
    mine = mine - mean
    theirs = theirs - mean
    spread = jnp.sum(mine * mine + theirs * theirs, axis=0, keepdims=True) * (1.0 / total)
    scale = lax.rsqrt(spread + epsilon)
    mine = mine * scale
    theirs = theirs * scale
    if gain is not None:
        half = mine.shape[0]
        mine = mine * gain[:half]
        theirs = theirs * gain[half:]
    return jnp.concatenate([mine.astype(BF16), theirs.astype(BF16)], axis=0)


def gated_sides(mine, theirs, weight, gain, half):
    y = jnp.dot(weight, normed_of(mine, theirs, gain), preferred_element_type=F32)
    sides = []
    for side in range(2):
        groups = []
        for row in range(2 * half * side, 2 * half * (side + 1), 16):
            groups.append((jnp.tanh(y[row : row + 8]) + 1.0) * y[row + 8 : row + 16])
        sides.append(groups)
    return sides, y[4 * half :]


def pair_chunk(sides_at, chunk, held):
    low = lax.broadcasted_iota(jnp.int32, (8, LANES), 1) < BLK
    pitch = held[0].shape[0] // (chunk // BLK)
    for start in range(0, chunk, LANES):
        first, second = sides_at(start)
        i = start // BLK
        for out, values0, values1 in zip(held, first, second):
            for at, (v0, v1) in enumerate(zip(values0, values1)):
                even = slice(i * pitch + 8 * at, i * pitch + 8 * at + 8)
                odd = slice((i + 1) * pitch + 8 * at, (i + 1) * pitch + 8 * at + 8)
                out[even, :] = jnp.where(low, v0, pltpu.roll(v1, BLK, 1))
                out[odd, :] = jnp.where(low, pltpu.roll(v0, BLK, 1), v1)
        yield


def spread_chunk(rows, held, l_ref, pair_of, l_row, p_ref, p_row, before, turned_ref, half):
    pitch = held[0].shape[0] // rows
    to = pl.ds(pl.multiple_of(l_row, 16), rows)
    for c in range(half):
        take = pl.ds(c, rows, stride=pitch)
        l_ref[pair_of, c, to, :] = held[0][take, :].astype(BF16)
        right = held[1][take, :]
        if turned_ref is None:
            p_ref[c, pl.ds(pl.multiple_of(p_row, 16), rows), :] = right.astype(BF16)
        else:
            whole = jnp.concatenate([ref[c, :size].astype(F32) for ref, size in before] + [right])
            turned = jnp.transpose(whole).astype(BF16)
            turned_ref[2 * pair_of, c] = turned[:BLK]
            turned_ref[2 * pair_of + 1, c] = turned[BLK:]
        if c % 8 == 7:
            yield


def two_chunks(sides_at, n, chunk, held, spread):
    steps = [
        pair_chunk(functools.partial(sides_at, n + k), chunk, held[2 * k : 2 * k + 2])
        for k in range(2)
    ]
    spreads = [spread(n + k, held[2 * k : 2 * k + 2], k) for k in range(2)]
    for _ in steps[0]:
        pass
    for _ in zip(steps[1], spreads[0]):
        pass
    for _ in spreads[0]:
        pass
    for _ in spreads[1]:
        pass


def cells_at(n, chunk, start):
    return pl.ds(pl.multiple_of(n * chunk + start, LANES), LANES)


def own_kernel(chunk, *refs):
    m_ref, t_ref = refs[:2]
    sources = refs[2:8]
    l_ref, turned_ref, gate_ref, w_ref, v_ref, gain_ref = refs[8:14]
    targets = refs[14:20]
    p_ref, held, sems = refs[20], refs[21:25], refs[25]
    copies = [
        pltpu.make_async_copy(source, target, sems.at[at])
        for at, (source, target) in enumerate(zip(sources, targets))
    ]
    for copy in copies:
        copy.start()
    half = l_ref.shape[1]

    @pl.loop(0, half)
    def _(c):
        turned_ref[4, c] = jnp.zeros((BLK, BLK), BF16)

    for copy in copies:
        copy.wait()
    a_ref, b_ref, o_ref, u_ref, g_ref, h_ref = targets
    rows = gated_rows(a_ref) + gated_rows(b_ref) + [0.5 * o_ref[...].astype(F32)]
    weight = prepared(jnp.concatenate(rows, axis=0))
    w_ref[...] = weight[: 4 * half]
    v_ref[...] = prepared(0.5 * u_ref[...].astype(F32), h_ref[...])
    across = jnp.transpose(jnp.broadcast_to(g_ref[...], (2 * half, LANES)))
    in_order = lax.axis_index("chan") == 0
    gain_ref[:half] = jnp.where(in_order, across[:half], across[half:])
    gain_ref[half:] = jnp.where(in_order, across[half:], across[:half])
    chunks = m_ref.shape[-1] // chunk
    rows = chunk // BLK

    def sides_at(n, start):
        at = cells_at(n, chunk, start)
        both = []
        for x in range(2):
            sides, rest = gated_sides(m_ref[x, :, at], t_ref[x, :, at], weight, gain_ref[...], half)
            gate_ref[x, :, at] = (jnp.tanh(rest) + 1.0).astype(BF16)
            both.append(sides)
        return both

    def spread(last, n, held, k):
        before, turned = ([(p_ref, (chunks - 1) * rows)], turned_ref) if last and k else (None, None)
        return spread_chunk(rows, held, l_ref, 0, n * rows, p_ref, n * rows, before, turned, half)

    @pl.loop(0, chunks - 2, step=2)
    def _(n):
        two_chunks(sides_at, n, chunk, held, functools.partial(spread, False))

    two_chunks(sides_at, chunks - 2, chunk, held, functools.partial(spread, True))


def fetched_kernel(chunk, first_row, last, m0, m1, *refs):
    if last:
        *theirs, p0_ref, w_ref, gain_ref, _, _, l_ref, turned_ref, p_ref = refs[:-4]
        before = [(p0_ref, p0_ref.shape[1]), (p_ref, p_ref.shape[1])]
    else:
        *theirs, w_ref, gain_ref, _, l_ref, p_ref = refs[:-4]
    held = refs[-4:]
    half = l_ref.shape[1]
    weight = w_ref[...]
    wide = theirs[0].shape[1]
    rows = chunk // BLK

    def sides_at(n, start):
        at = n * chunk + start
        both = []
        for x, m in enumerate((m0, m1)):
            other = theirs[2 * (at // wide) + x][:, at % wide : at % wide + LANES]
            both.append(
                gated_sides(m[:, at : at + LANES], other, weight, gain_ref[...], half)[0]
            )
        return both

    def spread(n, held, k):
        done = (before, turned_ref) if last and k else (None, None)
        return spread_chunk(rows, held, l_ref, 1, first_row + n * rows, p_ref, n * rows, *done, half)

    two_chunks(sides_at, 0, chunk, held, spread)


def chunk_scratch(half, chunk):
    return [pltpu.VMEM((chunk // BLK * (half + 8), LANES), F32)] * 4


def call(kernel, name, operands, out_shape, scratch, aliased=0, hbm=0):
    vmem = pl.BlockSpec(memory_space=pltpu.VMEM)
    plain = len(operands) - aliased
    operands = operands[:plain] + [
        pltpu.with_memory_space_constraint(value, pltpu.VMEM) for value in operands[plain:]
    ]
    operands = operands[: len(operands) - hbm] + [
        pltpu.with_memory_space_constraint(value, pltpu.HBM)
        for value in operands[len(operands) - hbm :]
    ]
    specs = [vmem] * (len(operands) - hbm) + [pl.BlockSpec(memory_space=pltpu.HBM)] * hbm
    return pl.pallas_call(
        kernel,
        in_specs=specs,
        out_specs=[vmem] * len(out_shape),
        out_shape=out_shape,
        scratch_shapes=scratch,
        input_output_aliases={plain + at: at for at in range(aliased)},
        compiler_params=pltpu.CompilerParams(vmem_limit_bytes=VMEM_LIMIT),
        name=name,
    )(*operands)


def triplet_kernel(s, group, picks_ref, l_ref, turned_ref, out_ref, *accs):
    picks = [picks_ref[4 * s + at] for at in range(4)]
    take_low = lax.broadcasted_iota(jnp.int32, (group, LANES), 1) < BLK
    half = l_ref.shape[1]
    pitch = accs[0].shape[0] // BLK

    @pl.loop(0, half, step=group * len(accs))
    def _(base):
        for which, acc in enumerate(accs):
            for at in range(group):
                c = base + which * group + at
                lhs = jnp.concatenate([l_ref[0, c], l_ref[1, c]], axis=1)
                rhs = jnp.concatenate([turned_ref[pick, c] for pick in picks], axis=0)
                acc[pl.ds(at, BLK, stride=pitch), :BLK] = jnp.dot(
                    lhs, rhs, preferred_element_type=F32
                )
            rows = pl.ds(pl.multiple_of(base + which * group, group), group)
            for t in range(BLK // 2):
                even = acc[2 * t * pitch : 2 * t * pitch + group, :]
                odd = acc[(2 * t + 1) * pitch : (2 * t + 1) * pitch + group, :]
                out_ref[rows, t * LANES : (t + 1) * LANES] = jnp.where(
                    take_low, even, pltpu.roll(odd, BLK, 1)
                ).astype(BF16)


def triplet_sum(s, picks, lefts, rights, group):
    half = lefts.shape[1]
    vmem = pl.BlockSpec(memory_space=pltpu.VMEM)
    picks = pltpu.with_memory_space_constraint(picks, pltpu.SMEM)
    lefts, rights = (
        pltpu.with_memory_space_constraint(value, pltpu.VMEM) for value in (lefts, rights)
    )
    return pl.pallas_call(
        functools.partial(triplet_kernel, s, group),
        in_specs=[pl.BlockSpec(memory_space=pltpu.SMEM), vmem, vmem],
        out_specs=vmem,
        out_shape=pltpu.VMEM((half, BLK * BLK), BF16),
        scratch_shapes=[pltpu.VMEM((BLK * (group + 8), LANES), F32)] * 2,
        compiler_params=pltpu.CompilerParams(vmem_limit_bytes=VMEM_LIMIT),
        name="triplets",
    )(picks, lefts, rights)


def finish_kernel(s, mine_ref, theirs_ref, gate_ref, w_ref, *refs):
    weight = w_ref[...]
    cells = mine_ref.shape[-1]
    if s == 0:
        held = refs[0]
        steps = 4
    else:
        before_ref, out_ref, held, sems = refs
        steps = sems.shape[0] - 1
        before = pltpu.make_async_copy(before_ref, out_ref.at[0], sems.at[steps])
        before.start()
    size = cells // steps

    def copy(n):
        to = pl.ds(pl.multiple_of(n * size, size), size)
        return pltpu.make_async_copy(held.at[:, to], out_ref.at[1, :, to], sems.at[n])

    @pl.loop(0, steps)
    def _(n):
        for start in range(0, size, LANES):
            to = pl.ds(pl.multiple_of(n * size + start, LANES), LANES)
            normed = normed_of(mine_ref[:, to], theirs_ref[:, to])
            projected = jnp.dot(weight, normed, preferred_element_type=F32)
            held[:, to] = (gate_ref[s, :, to].astype(F32) * projected).astype(BF16)
        if s > 0:
            copy(n).start()

    if s > 0:

        @pl.loop(0, steps)
        def _(n):
            copy(n).wait()

        before.wait()


def finish(s, mine, theirs, gate, weight, before=None):
    vmem = pl.BlockSpec(memory_space=pltpu.VMEM)
    operands = [mine, theirs, gate, weight]
    if s == 0:
        out_shape, out_specs, scratch = pltpu.VMEM(mine.shape, BF16), vmem, []
    else:
        operands.append(before)
        out_shape = jax.ShapeDtypeStruct(gate.shape, BF16)
        out_specs = pl.BlockSpec(memory_space=pltpu.HBM)
        scratch = [pltpu.VMEM(mine.shape, BF16), pltpu.SemaphoreType.DMA((5,))]
    return pl.pallas_call(
        functools.partial(finish_kernel, s),
        in_specs=[vmem] * len(operands),
        out_specs=out_specs,
        out_shape=out_shape,
        scratch_shapes=scratch,
        compiler_params=pltpu.CompilerParams(vmem_limit_bytes=VMEM_LIMIT),
        name="finish",
    )(*operands)


def per_device(
    pair,
    ln_in_gain,
    a_weight,
    b_weight,
    ln_out_gain,
    out_gate_weight,
    out_weight,
    a_slots,
    b_slots,
    counts,
):
    slots, half, cells = pair.shape
    rows = lax.axis_size("row")
    swap = [(0, 1), (1, 0)]
    up = [(i, (i + 1) % rows) for i in range(rows)]
    down = [(i, (i - 1) % rows) for i in range(rows)]

    a_slots, b_slots = a_slots.T, b_slots.T
    weights = [
        jnp.swapaxes(a_weight, 1, 2),
        jnp.swapaxes(b_weight, 1, 2),
        out_gate_weight.T,
        out_weight.T,
        ln_in_gain[None, :],
        ln_out_gain[None, :],
    ]

    chunk = cells // 4
    cuts = ((0, 2 * chunk), (2 * chunk, 2 * chunk))
    picks, pair, *chosen = select_blocks(pair, a_slots, b_slots, counts, cuts)
    ends = [(0, rows - 1), (rows - 1, 0)]
    row = lax.axis_index("row")
    arrived = [
        tuple(
            lax.ppermute(chosen[3 * n + which], "row", pairs)
            for which, pairs in ((2, ends), (0, up[:-1]), (1, down[1:]))
        )
        for n in range(len(cuts))
    ]
    pair_other = lax.ppermute(pair, "chan", swap)
    left_shape = pltpu.VMEM((2, half, BLK, LANES), BF16)
    right_shape = pltpu.VMEM((5, half, BLK, BLK), BF16)
    lefts, rights, gate, weight, last_weight, gain = call(
        functools.partial(own_kernel, chunk),
        "project_own",
        [pair, pair_other, *weights],
        [
            left_shape,
            right_shape,
            pltpu.VMEM((slots, half, cells), BF16),
            pltpu.VMEM((4 * half, 2 * half), BF16),
            pltpu.VMEM((half, 2 * half), BF16),
            pltpu.VMEM((2 * half, LANES), F32),
        ],
        [pltpu.VMEM(value.shape, value.dtype) for value in weights]
        + [pltpu.VMEM((half, BLK, LANES), BF16)]
        + chunk_scratch(half, chunk)
        + [pltpu.SemaphoreType.DMA((len(weights),))],
        hbm=len(weights),
    )
    for (start, size), behind_ahead in zip(cuts, arrived):
        far, near_behind, near_ahead, lefts = lax.optimization_barrier((*behind_ahead, lefts))
        behind_ahead = [
            jnp.where(row == 0, far, near_behind),
            jnp.where(row == rows - 1, far, near_ahead),
        ]
        wide = chunk if start == 0 else size
        others = [
            lax.ppermute(lax.slice_in_dim(value, at, at + wide, axis=1), "chan", swap)
            for at in range(0, size, wide)
            for value in behind_ahead
        ]
        paired = pltpu.VMEM((half, size // BLK, LANES), BF16)
        if start == 0:
            lefts, rights_first = call(
                functools.partial(fetched_kernel, chunk, 0, False),
                "project_first",
                [*behind_ahead, *others, weight, gain, lefts],
                [left_shape, paired],
                chunk_scratch(half, chunk),
                aliased=1,
            )
        else:
            lefts, rights = call(
                functools.partial(fetched_kernel, chunk, start // BLK, True),
                "project_last",
                [*behind_ahead, *others, rights_first, weight, gain, lefts, rights],
                [left_shape, right_shape],
                [pltpu.VMEM((half, chunk // BLK, LANES), BF16)] + chunk_scratch(half, chunk),
                aliased=2,
            )
    updates = []
    for s in range(slots):
        update = triplet_sum(s, picks, lefts, rights, 16)
        updates.append((update, lax.ppermute(update, "chan", swap)))
        if s + 1 < slots:
            update, lefts = lax.optimization_barrier((update, lefts))
    out = None
    for s, (mine, theirs) in enumerate(updates):
        out = finish(s, mine, theirs, gate, last_weight, out)
    return out


def solution(mesh):
    in_specs = (
        P(("parts", "row", "col"), "chan", None),
        P(),
        P(None, None, "chan"),
        P(None, None, "chan"),
        P(),
        P(None, "chan"),
        P(None, "chan"),
        P("parts", None),
        P("parts", None),
        P("parts"),
    )
    out_specs = P(("parts", "row", "col"), "chan", None)
    return jax.shard_map(
        per_device, mesh=mesh, in_specs=in_specs, out_specs=out_specs, check_vma=False
    )
```

```python
import functools

import jax
import jax.numpy as jnp
from jax import lax
from jax.experimental import pallas as pl
from jax.experimental.pallas import tpu as pltpu
from jax.sharding import PartitionSpec as P

BLK = 64
LANES = 128
epsilon = 1e-05
VMEM_LIMIT = 24 * 1024 * 1024
F32 = jnp.float32
BF16 = jnp.bfloat16


def sigmoid(x):
    return 0.5 * jnp.tanh(0.5 * x) + 0.5


def tile_of(row, col):
    return row * lax.axis_size("col") + col


def neighbour_tiles():
    rows = lax.axis_size("row")
    row, col = lax.axis_index("row"), lax.axis_index("col")
    behind = lax.rem(row + rows - 1, rows)
    ahead = lax.rem(row + 1, rows)
    return tile_of(row, col), tile_of(behind, col), tile_of(ahead, col)


def used_picks(s, slots, triplets, a_ref, b_ref, n_ref):
    me, behind, ahead = neighbour_tiles()
    block = me * slots + s
    count = n_ref[block]
    picks = []
    for left_at in range(4):
        pick = jnp.int32(4)
        for m in range(triplets):
            left = a_ref[m, block]
            if left_at < 2:
                hit = left == me * slots + left_at
            else:
                base = (behind, ahead)[left_at - 2] * slots
                hit = jnp.logical_and(left >= base, left < base + slots)
            hit = jnp.logical_and(hit, m < count)
            place = b_ref[m, block] - me * slots
            from_me = jnp.logical_and(place >= 0, place < slots)
            right = b_ref[m, block] - behind * slots
            from_behind = jnp.logical_and(right >= 0, right < slots)
            place = jnp.where(from_me, place, jnp.where(from_behind, 2, 3))
            pick = jnp.where(hit, place, pick)
        picks.append(pick)
    return picks


def select_kernel(slots, triplets, cuts, a_hbm, b_hbm, n_hbm, pair_hbm, *refs):
    picks_ref, pair_ref, *out_refs = refs[: 2 + 2 * len(cuts)]
    a_ref, b_ref, n_ref, sems = refs[2 + 2 * len(cuts) :]
    me, behind, ahead = neighbour_tiles()
    whole = pltpu.make_async_copy(pair_hbm, pair_ref, sems.at[0])
    tables = [
        pltpu.make_async_copy(source, target, sems.at[1 + at])
        for at, (source, target) in enumerate(((a_hbm, a_ref), (b_hbm, b_ref), (n_hbm, n_ref)))
    ]
    for copy in (*tables, whole):
        copy.start()
    for copy in tables:
        copy.wait()
    chosen = []
    for target in (ahead, behind):
        pick = jnp.int32(0)
        for s in range(slots):
            count = n_ref[target * slots + s]
            for m in range(triplets):
                for ids in (a_ref, b_ref):
                    name = ids[m, target * slots + s] - me * slots
                    mine = jnp.logical_and(name >= 0, name < slots)
                    pick = jnp.where(jnp.logical_and(m < count, mine), name, pick)
        chosen.append(pick)
    for s in range(slots):
        for at, pick in enumerate(used_picks(s, slots, triplets, a_ref, b_ref, n_ref)):
            picks_ref[4 * s + at] = pick
    whole.wait()
    for at, (start, size) in enumerate(cuts):
        for which, pick in enumerate(chosen):
            out_refs[2 * at + which][...] = pair_ref[pick, :, start : start + size]


def select_blocks(pair, a_slots, b_slots, counts, cuts):
    slots, channels, cells = pair.shape
    hbm = pl.BlockSpec(memory_space=pltpu.HBM)
    vmem = pl.BlockSpec(memory_space=pltpu.VMEM)
    out_shape = [pltpu.SMEM((4 * slots,), jnp.int32), pltpu.VMEM(pair.shape, pair.dtype)] + [
        pltpu.VMEM((channels, size), pair.dtype) for _, size in cuts for _ in range(2)
    ]
    operands = [
        pltpu.with_memory_space_constraint(value, pltpu.HBM)
        for value in (a_slots, b_slots, counts, pair)
    ]
    return pl.pallas_call(
        functools.partial(select_kernel, slots, a_slots.shape[0], cuts),
        out_shape=out_shape,
        in_specs=[hbm] * 4,
        out_specs=[pl.BlockSpec(memory_space=pltpu.SMEM)] + [vmem] * (len(out_shape) - 1),
        scratch_shapes=[pltpu.SMEM(value.shape, value.dtype) for value in operands[:3]]
        + [pltpu.SemaphoreType.DMA((4,))],
        name="select_blocks",
    )(*operands)


def prepared(weight, gain=None):
    if gain is not None:
        weight = weight * gain
    rolled = pltpu.roll(weight, weight.shape[1] // 2, 1)
    return jnp.where(lax.axis_index("chan") == 0, weight, rolled).astype(BF16)


def gated_rows(w_ref):
    gate, value = w_ref[0].astype(F32), w_ref[1].astype(F32)
    rows = []
    for at in range(0, gate.shape[0], 8):
        rows += [gate[at : at + 8], value[at : at + 8]]
    return [0.5 * row for row in rows]


def normed_of(mine, theirs, gain=None):
    total = 2 * mine.shape[0]
    mine = mine.astype(F32)
    theirs = theirs.astype(F32)
    mean = jnp.sum(mine + theirs, axis=0, keepdims=True) * (1.0 / total)
    mine = mine - mean
    theirs = theirs - mean
    spread = jnp.sum(mine * mine + theirs * theirs, axis=0, keepdims=True) * (1.0 / total)
    scale = lax.rsqrt(spread + epsilon)
    mine = mine * scale
    theirs = theirs * scale
    if gain is not None:
        half = mine.shape[0]
        mine = mine * gain[:half]
        theirs = theirs * gain[half:]
    return jnp.concatenate([mine.astype(BF16), theirs.astype(BF16)], axis=0)


def gated_sides(mine, theirs, weight, gain, half):
    y = jnp.dot(weight, normed_of(mine, theirs, gain), preferred_element_type=F32)
    sides = []
    for side in range(2):
        groups = []
        for row in range(2 * half * side, 2 * half * (side + 1), 16):
            groups.append((jnp.tanh(y[row : row + 8]) + 1.0) * y[row + 8 : row + 16])
        sides.append(groups)
    return sides, y[4 * half :]


def pair_chunk(sides_at, chunk, held):
    low = lax.broadcasted_iota(jnp.int32, (8, LANES), 1) < BLK
    pitch = held[0].shape[0] // (chunk // BLK)
    for start in range(0, chunk, LANES):
        first, second = sides_at(start)
        i = start // BLK
        for out, values0, values1 in zip(held, first, second):
            for at, (v0, v1) in enumerate(zip(values0, values1)):
                even = slice(i * pitch + 8 * at, i * pitch + 8 * at + 8)
                odd = slice((i + 1) * pitch + 8 * at, (i + 1) * pitch + 8 * at + 8)
                out[even, :] = jnp.where(low, v0, pltpu.roll(v1, BLK, 1))
                out[odd, :] = jnp.where(low, pltpu.roll(v0, BLK, 1), v1)
        yield


def spread_chunk(rows, held, l_ref, pair_of, l_row, p_ref, p_row, before, turned_ref, half):
    pitch = held[0].shape[0] // rows
    to = pl.ds(pl.multiple_of(l_row, 16), rows)
    for c in range(half):
        take = pl.ds(c, rows, stride=pitch)
        l_ref[pair_of, c, to, :] = held[0][take, :].astype(BF16)
        right = held[1][take, :]
        if turned_ref is None:
            p_ref[c, pl.ds(pl.multiple_of(p_row, 16), rows), :] = right.astype(BF16)
        else:
            whole = jnp.concatenate([ref[c, :size].astype(F32) for ref, size in before] + [right])
            turned = jnp.transpose(whole).astype(BF16)
            turned_ref[2 * pair_of, c] = turned[:BLK]
            turned_ref[2 * pair_of + 1, c] = turned[BLK:]
        if c % 8 == 7:
            yield


def two_chunks(sides_at, n, chunk, held, spread, after=()):
    steps = [
        pair_chunk(functools.partial(sides_at, n + k), chunk, held[2 * k : 2 * k + 2])
        for k in range(2)
    ]
    spreads = [spread(n + k, held[2 * k : 2 * k + 2], k) for k in range(2)]
    for _ in steps[0]:
        pass
    for _ in zip(steps[1], spreads[0]):
        pass
    for _ in spreads[0]:
        pass
    for at, _ in enumerate(spreads[1]):
        if at > 0:
            next(iter(after), None)
    for _ in after:
        pass


def cells_at(n, chunk, start):
    return pl.ds(pl.multiple_of(n * chunk + start, LANES), LANES)


def own_kernel(chunk, *refs):
    m_ref, t_ref = refs[:2]
    sources = refs[2:8]
    l_ref, turned_ref, gate_ref, w_ref, v_ref, gain_ref = refs[8:14]
    targets = refs[14:20]
    p_ref, held, sems = refs[20], refs[21:25], refs[25]
    copies = [
        pltpu.make_async_copy(source, target, sems.at[at])
        for at, (source, target) in enumerate(zip(sources, targets))
    ]
    for copy in copies:
        copy.start()
    half = l_ref.shape[1]

    @pl.loop(0, half)
    def _(c):
        turned_ref[4, c] = jnp.zeros((BLK, BLK), BF16)

    for copy in copies:
        copy.wait()
    a_ref, b_ref, o_ref, u_ref, g_ref, h_ref = targets
    rows = gated_rows(a_ref) + gated_rows(b_ref) + [0.5 * o_ref[...].astype(F32)]
    weight = prepared(jnp.concatenate(rows, axis=0))
    w_ref[...] = weight[: 4 * half]
    v_ref[...] = prepared(0.5 * u_ref[...].astype(F32), h_ref[...])
    across = jnp.transpose(jnp.broadcast_to(g_ref[...], (2 * half, LANES)))
    in_order = lax.axis_index("chan") == 0
    gain_ref[:half] = jnp.where(in_order, across[:half], across[half:])
    gain_ref[half:] = jnp.where(in_order, across[half:], across[:half])
    chunks = m_ref.shape[-1] // chunk
    rows = chunk // BLK

    def sides_at(n, start):
        at = cells_at(n, chunk, start)
        both = []
        for x in range(2):
            sides, rest = gated_sides(m_ref[x, :, at], t_ref[x, :, at], weight, gain_ref[...], half)
            gate_ref[x, :, at] = (jnp.tanh(rest) + 1.0).astype(BF16)
            both.append(sides)
        return both

    def spread(last, n, held, k):
        before, turned = ([(p_ref, (chunks - 1) * rows)], turned_ref) if last and k else (None, None)
        return spread_chunk(rows, held, l_ref, 0, n * rows, p_ref, n * rows, before, turned, half)

    @pl.loop(0, chunks - 2, step=2)
    def _(n):
        two_chunks(sides_at, n, chunk, held, functools.partial(spread, False))

    two_chunks(sides_at, chunks - 2, chunk, held, functools.partial(spread, True))


def fetched_sides(chunk, ours, theirs, weight, gain_ref, half):
    wide = theirs[0].shape[1]

    def sides_at(n, start):
        at = n * chunk + start
        both = []
        for x, m in enumerate(ours):
            other = theirs[2 * (at // wide) + x][:, at % wide : at % wide + LANES]
            both.append(
                gated_sides(m[:, at : at + LANES], other, weight, gain_ref[...], half)[0]
            )
        return both

    return sides_at


def first_kernel(chunk, *refs):
    *ours_theirs, w_ref, gain_ref, _, l_ref, p_ref = refs[:-4]
    held = refs[-4:]
    half = l_ref.shape[1]
    rows = chunk // BLK
    sides_at = fetched_sides(
        chunk, ours_theirs[:2], ours_theirs[2:], w_ref[...], gain_ref, half
    )

    def spread(n, held, k):
        return spread_chunk(rows, held, l_ref, 1, n * rows, p_ref, n * rows, None, None, half)

    two_chunks(sides_at, 0, chunk, held, spread)


def last_kernel(chunk, first_row, group, picks_ref, *refs):
    *ours_theirs, p0_ref, w_ref, gain_ref, _, _, l_ref, turned_ref, out_ref, p_ref = refs[:-6]
    held, accs = refs[-6:-2], refs[-2:]
    before = [(p0_ref, p0_ref.shape[1]), (p_ref, p_ref.shape[1])]
    half = l_ref.shape[1]
    rows = chunk // BLK
    sides_at = fetched_sides(
        chunk, ours_theirs[:2], ours_theirs[2:], w_ref[...], gain_ref, half
    )

    def spread(n, held, k):
        done = (before, turned_ref) if k else (None, None)
        return spread_chunk(rows, held, l_ref, 1, first_row + n * rows, p_ref, n * rows, *done, half)

    products = triplet_steps(0, group, picks_ref, l_ref, turned_ref, out_ref, accs)
    two_chunks(sides_at, 0, chunk, held, spread, products)


def triplet_steps(s, group, picks_ref, l_ref, turned_ref, out_ref, accs):
    picks = [picks_ref[4 * s + at] for at in range(4)]
    take_low = lax.broadcasted_iota(jnp.int32, (group, LANES), 1) < BLK
    pitch = accs[0].shape[0] // BLK
    for first in range(0, l_ref.shape[1], group):
        acc = accs[first // group % len(accs)]
        for at in range(group):
            c = first + at
            lhs = jnp.concatenate([l_ref[0, c], l_ref[1, c]], axis=1)
            rhs = jnp.concatenate([turned_ref[pick, c] for pick in picks], axis=0)
            acc[pl.ds(at, BLK, stride=pitch), :BLK] = jnp.dot(
                lhs, rhs, preferred_element_type=F32
            )
            if at % 8 == 7 and at + 1 < group:
                yield
        for t in range(BLK // 2):
            even = acc[2 * t * pitch : 2 * t * pitch + group, :]
            odd = acc[(2 * t + 1) * pitch : (2 * t + 1) * pitch + group, :]
            out_ref[first : first + group, t * LANES : (t + 1) * LANES] = jnp.where(
                take_low, even, pltpu.roll(odd, BLK, 1)
            ).astype(BF16)
        yield


def triplet_kernel(s, group, picks_ref, l_ref, turned_ref, out_ref, *accs):
    for _ in triplet_steps(s, group, picks_ref, l_ref, turned_ref, out_ref, accs):
        pass


def acc_scratch(group):
    return [pltpu.VMEM((BLK * (group + 8), LANES), F32)] * 2


def chunk_scratch(half, chunk):
    return [pltpu.VMEM((chunk // BLK * (half + 8), LANES), F32)] * 4


def call(kernel, name, operands, out_shape, scratch, aliased=0, hbm=0, smem=0):
    spaces = [pltpu.SMEM] * smem + [pltpu.VMEM] * (len(operands) - smem - hbm) + [pltpu.HBM] * hbm
    plain = len(operands) - aliased
    operands = [
        value
        if space == pltpu.VMEM and at < plain
        else pltpu.with_memory_space_constraint(value, space)
        for at, (value, space) in enumerate(zip(operands, spaces))
    ]
    return pl.pallas_call(
        kernel,
        in_specs=[pl.BlockSpec(memory_space=space) for space in spaces],
        out_specs=[pl.BlockSpec(memory_space=pltpu.VMEM)] * len(out_shape),
        out_shape=out_shape,
        scratch_shapes=scratch,
        input_output_aliases={plain + at: at for at in range(aliased)},
        compiler_params=pltpu.CompilerParams(vmem_limit_bytes=VMEM_LIMIT),
        name=name,
    )(*operands)


def finish_kernel(s, run, pieces, mine_ref, theirs_ref, gate_ref, w_ref, *refs):
    weight = w_ref[...]
    cells = mine_ref.shape[-1]
    if s == 0:
        held = refs[0]
    else:
        before_ref, out_ref, held, sems = refs
        before = pltpu.make_async_copy(before_ref, out_ref.at[0], sems.at[pieces])
        before.start()
    size = cells // pieces

    def copy(n):
        to = pl.ds(pl.multiple_of(n * size, size), size)
        return pltpu.make_async_copy(held.at[:, to], out_ref.at[1, :, to], sems.at[n])

    @pl.loop(0, cells // run)
    def _(n):
        for start in range(0, run, LANES):
            to = cells_at(n, run, start)
            normed = normed_of(mine_ref[:, to], theirs_ref[:, to])
            projected = jnp.dot(weight, normed, preferred_element_type=F32)
            held[:, to] = (gate_ref[s, :, to].astype(F32) * projected).astype(BF16)
            done = start + LANES
            if s > 0 and done % size == 0:
                copy(n * (run // size) + done // size - 1).start()

    if s > 0:
        for n in range(pieces):
            copy(n).wait()
        before.wait()


def finish(s, mine, theirs, gate, weight, before=None):
    vmem = pl.BlockSpec(memory_space=pltpu.VMEM)
    operands = [mine, theirs, gate, weight]
    if s == 0:
        out_shape, out_specs, scratch = pltpu.VMEM(mine.shape, BF16), vmem, []
    else:
        operands.append(before)
        out_shape = jax.ShapeDtypeStruct(gate.shape, BF16)
        out_specs = pl.BlockSpec(memory_space=pltpu.HBM)
        scratch = [pltpu.VMEM(mine.shape, BF16), pltpu.SemaphoreType.DMA((5,))]
    return pl.pallas_call(
        functools.partial(finish_kernel, s, mine.shape[1] // 2, 4),
        in_specs=[vmem] * len(operands),
        out_specs=out_specs,
        out_shape=out_shape,
        scratch_shapes=scratch,
        compiler_params=pltpu.CompilerParams(vmem_limit_bytes=VMEM_LIMIT),
        name="finish",
    )(*operands)


def per_device(
    pair,
    ln_in_gain,
    a_weight,
    b_weight,
    ln_out_gain,
    out_gate_weight,
    out_weight,
    a_slots,
    b_slots,
    counts,
):
    slots, half, cells = pair.shape
    rows = lax.axis_size("row")
    swap = [(0, 1), (1, 0)]
    up = [(i, (i + 1) % rows) for i in range(rows)]
    down = [(i, (i - 1) % rows) for i in range(rows)]

    a_slots, b_slots = a_slots.T, b_slots.T
    weights = [
        jnp.swapaxes(a_weight, 1, 2),
        jnp.swapaxes(b_weight, 1, 2),
        out_gate_weight.T,
        out_weight.T,
        ln_in_gain[None, :],
        ln_out_gain[None, :],
    ]

    chunk = cells // 4
    cuts = ((0, 2 * chunk), (2 * chunk, 2 * chunk))
    picks, pair, *chosen = select_blocks(pair, a_slots, b_slots, counts, cuts)
    arrived = [
        (lax.ppermute(chosen[2 * n], "row", up), lax.ppermute(chosen[2 * n + 1], "row", down))
        for n in range(len(cuts))
    ]
    pair_other = lax.ppermute(pair, "chan", swap)
    left_shape = pltpu.VMEM((2, half, BLK, LANES), BF16)
    right_shape = pltpu.VMEM((5, half, BLK, BLK), BF16)
    lefts, rights, gate, weight, last_weight, gain = call(
        functools.partial(own_kernel, chunk),
        "project_own",
        [pair, pair_other, *weights],
        [
            left_shape,
            right_shape,
            pltpu.VMEM((slots, half, cells), BF16),
            pltpu.VMEM((4 * half, 2 * half), BF16),
            pltpu.VMEM((half, 2 * half), BF16),
            pltpu.VMEM((2 * half, LANES), F32),
        ],
        [pltpu.VMEM(value.shape, value.dtype) for value in weights]
        + [pltpu.VMEM((half, BLK, LANES), BF16)]
        + chunk_scratch(half, chunk)
        + [pltpu.SemaphoreType.DMA((len(weights),))],
        hbm=len(weights),
    )
    for (start, size), behind_ahead in zip(cuts, arrived):
        *behind_ahead, lefts = lax.optimization_barrier((*behind_ahead, lefts))
        wide = chunk if start == 0 else size
        others = [
            lax.ppermute(lax.slice_in_dim(value, at, at + wide, axis=1), "chan", swap)
            for at in range(0, size, wide)
            for value in behind_ahead
        ]
        paired = pltpu.VMEM((half, size // BLK, LANES), BF16)
        if start == 0:
            lefts, rights_first = call(
                functools.partial(first_kernel, chunk),
                "project_first",
                [*behind_ahead, *others, weight, gain, lefts],
                [left_shape, paired],
                chunk_scratch(half, chunk),
                aliased=1,
            )
        else:
            lefts, rights, update = call(
                functools.partial(last_kernel, chunk, start // BLK, 16),
                "project_last",
                [picks, *behind_ahead, *others, rights_first, weight, gain, lefts, rights],
                [left_shape, right_shape, pltpu.VMEM((half, cells), BF16)],
                [pltpu.VMEM((half, chunk // BLK, LANES), BF16)]
                + chunk_scratch(half, chunk)
                + acc_scratch(16),
                aliased=2,
                smem=1,
            )
    updates = [(update, lax.ppermute(update, "chan", swap))]
    update, lefts = lax.optimization_barrier((update, lefts))
    for s in range(1, slots):
        (update,) = call(
            functools.partial(triplet_kernel, s, 16),
            "triplets",
            [picks, lefts, rights],
            [pltpu.VMEM((half, cells), BF16)],
            acc_scratch(16),
            smem=1,
        )
        updates.append((update, lax.ppermute(update, "chan", swap)))
    out = None
    for s, (mine, theirs) in enumerate(updates):
        out = finish(s, mine, theirs, gate, last_weight, out)
    return out


def solution(mesh):
    in_specs = (
        P(("parts", "row", "col"), "chan", None),
        P(),
        P(None, None, "chan"),
        P(None, None, "chan"),
        P(),
        P(None, "chan"),
        P(None, "chan"),
        P("parts", None),
        P("parts", None),
        P("parts"),
    )
    out_specs = P(("parts", "row", "col"), "chan", None)
    return jax.shard_map(
        per_device, mesh=mesh, in_specs=in_specs, out_specs=out_specs, check_vma=False
    )
```

```python
import functools

import jax
import jax.numpy as jnp
from jax import lax
from jax.experimental import pallas as pl
from jax.experimental.pallas import tpu as pltpu
from jax.sharding import PartitionSpec as P

BLK = 64
LANES = 128
epsilon = 1e-05
VMEM_LIMIT = 24 * 1024 * 1024
F32 = jnp.float32
BF16 = jnp.bfloat16


def sigmoid(x):
    return 0.5 * jnp.tanh(0.5 * x) + 0.5


def tile_of(row, col):
    return row * lax.axis_size("col") + col


def neighbour_tiles():
    rows = lax.axis_size("row")
    row, col = lax.axis_index("row"), lax.axis_index("col")
    behind = lax.rem(row + rows - 1, rows)
    ahead = lax.rem(row + 1, rows)
    return tile_of(row, col), tile_of(behind, col), tile_of(ahead, col)


def used_picks(s, slots, triplets, a_ref, b_ref, n_ref):
    me, behind, ahead = neighbour_tiles()
    block = me * slots + s
    count = n_ref[block]
    picks = []
    for left_at in range(4):
        pick = jnp.int32(4)
        for m in range(triplets):
            left = a_ref[m, block]
            if left_at < 2:
                hit = left == me * slots + left_at
            else:
                base = (behind, ahead)[left_at - 2] * slots
                hit = jnp.logical_and(left >= base, left < base + slots)
            hit = jnp.logical_and(hit, m < count)
            place = b_ref[m, block] - me * slots
            from_me = jnp.logical_and(place >= 0, place < slots)
            right = b_ref[m, block] - behind * slots
            from_behind = jnp.logical_and(right >= 0, right < slots)
            place = jnp.where(from_me, place, jnp.where(from_behind, 2, 3))
            pick = jnp.where(hit, place, pick)
        picks.append(pick)
    return picks


def select_kernel(slots, triplets, cuts, a_hbm, b_hbm, n_hbm, pair_hbm, *refs):
    picks_ref, pair_ref, *out_refs = refs[: 2 + 2 * len(cuts)]
    a_ref, b_ref, n_ref, sems = refs[2 + 2 * len(cuts) :]
    me, behind, ahead = neighbour_tiles()
    whole = pltpu.make_async_copy(pair_hbm, pair_ref, sems.at[0])
    tables = [
        pltpu.make_async_copy(source, target, sems.at[1 + at])
        for at, (source, target) in enumerate(((a_hbm, a_ref), (b_hbm, b_ref), (n_hbm, n_ref)))
    ]
    for copy in (*tables, whole):
        copy.start()
    for copy in tables:
        copy.wait()
    chosen = []
    for target in (ahead, behind):
        pick = jnp.int32(0)
        for s in range(slots):
            count = n_ref[target * slots + s]
            for m in range(triplets):
                for ids in (a_ref, b_ref):
                    name = ids[m, target * slots + s] - me * slots
                    mine = jnp.logical_and(name >= 0, name < slots)
                    pick = jnp.where(jnp.logical_and(m < count, mine), name, pick)
        chosen.append(pick)
    for s in range(slots):
        for at, pick in enumerate(used_picks(s, slots, triplets, a_ref, b_ref, n_ref)):
            picks_ref[4 * s + at] = pick
    whole.wait()
    for at, (start, size) in enumerate(cuts):
        for which, pick in enumerate(chosen):
            out_refs[2 * at + which][...] = pair_ref[pick, :, start : start + size]


def select_blocks(pair, a_slots, b_slots, counts, cuts):
    slots, channels, cells = pair.shape
    hbm = pl.BlockSpec(memory_space=pltpu.HBM)
    vmem = pl.BlockSpec(memory_space=pltpu.VMEM)
    out_shape = [pltpu.SMEM((4 * slots,), jnp.int32), pltpu.VMEM(pair.shape, pair.dtype)] + [
        pltpu.VMEM((channels, size), pair.dtype) for _, size in cuts for _ in range(2)
    ]
    operands = [
        pltpu.with_memory_space_constraint(value, pltpu.HBM)
        for value in (a_slots, b_slots, counts, pair)
    ]
    return pl.pallas_call(
        functools.partial(select_kernel, slots, a_slots.shape[0], cuts),
        out_shape=out_shape,
        in_specs=[hbm] * 4,
        out_specs=[pl.BlockSpec(memory_space=pltpu.SMEM)] + [vmem] * (len(out_shape) - 1),
        scratch_shapes=[pltpu.SMEM(value.shape, value.dtype) for value in operands[:3]]
        + [pltpu.SemaphoreType.DMA((4,))],
        name="select_blocks",
    )(*operands)


def prepared(weight, gain=None):
    if gain is not None:
        weight = weight * gain
    rolled = pltpu.roll(weight, weight.shape[1] // 2, 1)
    return jnp.where(lax.axis_index("chan") == 0, weight, rolled).astype(BF16)


def gated_rows(w_ref):
    gate, value = w_ref[0].astype(F32), w_ref[1].astype(F32)
    rows = []
    for at in range(0, gate.shape[0], 8):
        rows += [gate[at : at + 8], value[at : at + 8]]
    return [0.5 * row for row in rows]


def normed_of(mine, theirs, gain=None):
    total = 2 * mine.shape[0]
    mine = mine.astype(F32)
    theirs = theirs.astype(F32)
    mean = jnp.sum(mine + theirs, axis=0, keepdims=True) * (1.0 / total)
    mine = mine - mean
    theirs = theirs - mean
    spread = jnp.sum(mine * mine + theirs * theirs, axis=0, keepdims=True) * (1.0 / total)
    scale = lax.rsqrt(spread + epsilon)
    mine = mine * scale
    theirs = theirs * scale
    if gain is not None:
        half = mine.shape[0]
        mine = mine * gain[:half]
        theirs = theirs * gain[half:]
    return jnp.concatenate([mine.astype(BF16), theirs.astype(BF16)], axis=0)


def gated_sides(mine, theirs, weight, gain, half):
    y = jnp.dot(weight, normed_of(mine, theirs, gain), preferred_element_type=F32)
    sides = []
    for side in range(2):
        groups = []
        for row in range(2 * half * side, 2 * half * (side + 1), 16):
            groups.append((jnp.tanh(y[row : row + 8]) + 1.0) * y[row + 8 : row + 16])
        sides.append(groups)
    return sides, y[4 * half :]


def pair_chunk(sides_at, chunk, held):
    low = lax.broadcasted_iota(jnp.int32, (8, LANES), 1) < BLK
    pitch = held[0].shape[0] // (chunk // BLK)
    for start in range(0, chunk, LANES):
        first, second = sides_at(start)
        i = start // BLK
        for out, values0, values1 in zip(held, first, second):
            for at, (v0, v1) in enumerate(zip(values0, values1)):
                even = slice(i * pitch + 8 * at, i * pitch + 8 * at + 8)
                odd = slice((i + 1) * pitch + 8 * at, (i + 1) * pitch + 8 * at + 8)
                out[even, :] = jnp.where(low, v0, pltpu.roll(v1, BLK, 1))
                out[odd, :] = jnp.where(low, pltpu.roll(v0, BLK, 1), v1)
        yield


def spread_chunk(rows, held, l_ref, pair_of, l_row, p_ref, p_row, before, turned_ref, half):
    pitch = held[0].shape[0] // rows
    to = pl.ds(pl.multiple_of(l_row, 16), rows)
    for c in range(half):
        take = pl.ds(c, rows, stride=pitch)
        l_ref[pair_of, c, to, :] = held[0][take, :].astype(BF16)
        right = held[1][take, :]
        if turned_ref is None:
            p_ref[c, pl.ds(pl.multiple_of(p_row, 16), rows), :] = right.astype(BF16)
        else:
            whole = jnp.concatenate([ref[c, :size].astype(F32) for ref, size in before] + [right])
            turned = jnp.transpose(whole).astype(BF16)
            turned_ref[2 * pair_of, c] = turned[:BLK]
            turned_ref[2 * pair_of + 1, c] = turned[BLK:]
        if c % 8 == 7:
            yield


def in_turn(sides_at, chunks, chunk, held, spread, after=(), pending=()):
    for k, n in enumerate(chunks):
        scratch = held[2 * (k % 2) : 2 * (k % 2) + 2]
        for _ in pair_chunk(functools.partial(sides_at, n), chunk, scratch):
            next(iter(pending), None)
        for _ in pending:
            pass
        pending = spread(n, scratch, k + 1 == len(chunks))
    for at, _ in enumerate(pending):
        if at > 0:
            next(iter(after), None)
    for _ in after:
        pass


def cells_at(n, chunk, start):
    return pl.ds(pl.multiple_of(n * chunk + start, LANES), LANES)


def own_kernel(chunk, *refs):
    m_ref, t_ref = refs[:2]
    sources = refs[2:8]
    l_ref, turned_ref, gate_ref, w_ref, v_ref, gain_ref = refs[8:14]
    targets = refs[14:20]
    p_ref, held, sems = refs[20], refs[21:25], refs[25]
    copies = [
        pltpu.make_async_copy(source, target, sems.at[at])
        for at, (source, target) in enumerate(zip(sources, targets))
    ]
    for copy in copies:
        copy.start()
    half = l_ref.shape[1]

    @pl.loop(0, half)
    def _(c):
        turned_ref[4, c] = jnp.zeros((BLK, BLK), BF16)

    for copy in copies:
        copy.wait()
    a_ref, b_ref, o_ref, u_ref, g_ref, h_ref = targets
    rows = gated_rows(a_ref) + gated_rows(b_ref) + [0.5 * o_ref[...].astype(F32)]
    weight = prepared(jnp.concatenate(rows, axis=0))
    w_ref[...] = weight[: 4 * half]
    v_ref[...] = prepared(0.5 * u_ref[...].astype(F32), h_ref[...])
    across = jnp.transpose(jnp.broadcast_to(g_ref[...], (2 * half, LANES)))
    in_order = lax.axis_index("chan") == 0
    gain_ref[:half] = jnp.where(in_order, across[:half], across[half:])
    gain_ref[half:] = jnp.where(in_order, across[half:], across[:half])
    chunks = m_ref.shape[-1] // chunk
    rows = chunk // BLK

    def sides_at(n, start):
        at = cells_at(n, chunk, start)
        both = []
        for x in range(2):
            sides, rest = gated_sides(m_ref[x, :, at], t_ref[x, :, at], weight, gain_ref[...], half)
            gate_ref[x, :, at] = (jnp.tanh(rest) + 1.0).astype(BF16)
            both.append(sides)
        return both

    def spread(last, n, held, k):
        before, turned = ([(p_ref, (chunks - 1) * rows)], turned_ref) if last and k else (None, None)
        return spread_chunk(rows, held, l_ref, 0, n * rows, p_ref, n * rows, before, turned, half)

    @pl.loop(0, chunks - 2, step=2)
    def _(n):
        in_turn(sides_at, (n, n + 1), chunk, held, functools.partial(spread, False))

    in_turn(sides_at, (chunks - 2, chunks - 1), chunk, held, functools.partial(spread, True))


def fetched_sides(chunk, ours, theirs, weight, gain_ref, half):
    def sides_at(n, start):
        at = n * chunk + start
        return [
            gated_sides(
                m[:, at : at + LANES], theirs[n][x, :, start : start + LANES], weight, gain_ref[...], half
            )[0]
            for x, m in enumerate(ours)
        ]

    return sides_at


def first_kernel(chunk, m0, m1, *refs):
    *theirs, w_ref, gain_ref, _, l_ref, p_ref = refs[:-4]
    held = refs[-4:]
    half = l_ref.shape[1]
    rows = chunk // BLK
    weight = w_ref[...]

    def sides_at(n, start):
        at = n * chunk + start
        return [
            gated_sides(
                m[:, at : at + LANES],
                theirs[2 * n + x][:, start : start + LANES],
                weight,
                gain_ref[...],
                half,
            )[0]
            for x, m in enumerate((m0, m1))
        ]

    def spread(n, held, last):
        return spread_chunk(rows, held, l_ref, 1, n * rows, p_ref, n * rows, None, None, half)

    in_turn(sides_at, range(2), chunk, held, spread)


def half_kernel(chunk, m0, m1, t_ref, w_ref, gain_ref, *held):
    half = m0.shape[0]
    sides_at = fetched_sides(chunk, (m0, m1), (t_ref,), w_ref[...], gain_ref, half)
    for _ in pair_chunk(functools.partial(sides_at, 0), chunk, held):
        pass


def last_kernel(chunk, first_row, group, picks_ref, m0, m1, t_ref, *refs):
    earlier_ref, *done, w_ref, gain_ref, _, _, l_ref, turned_ref, out_ref, p_ref = refs[:-4]
    held, accs = refs[-4:-2], refs[-2:]
    half = l_ref.shape[1]
    rows = chunk // BLK
    before = [(earlier_ref, earlier_ref.shape[1]), (p_ref, rows)]
    sides_at = fetched_sides(chunk, (m0, m1), (None, t_ref), w_ref[...], gain_ref, half)

    def spread(n, held, last):
        row = first_row + n * rows
        whole = (before, turned_ref) if last else (None, None)
        return spread_chunk(rows, held, l_ref, 1, row, p_ref, n * rows, *whole, half)

    products = triplet_steps(0, group, picks_ref, l_ref, turned_ref, out_ref, accs)
    in_turn(sides_at, (1,), chunk, held, spread, products, spread(0, done, False))


def triplet_steps(s, group, picks_ref, l_ref, turned_ref, out_ref, accs):
    picks = [picks_ref[4 * s + at] for at in range(4)]
    take_low = lax.broadcasted_iota(jnp.int32, (group, LANES), 1) < BLK
    pitch = accs[0].shape[0] // BLK
    for first in range(0, l_ref.shape[1], group):
        acc = accs[first // group % len(accs)]
        for at in range(group):
            c = first + at
            lhs = jnp.concatenate([l_ref[0, c], l_ref[1, c]], axis=1)
            rhs = jnp.concatenate([turned_ref[pick, c] for pick in picks], axis=0)
            acc[pl.ds(at, BLK, stride=pitch), :BLK] = jnp.dot(
                lhs, rhs, preferred_element_type=F32
            )
            if at % 8 == 7 and at + 1 < group:
                yield
        for t in range(BLK // 2):
            even = acc[2 * t * pitch : 2 * t * pitch + group, :]
            odd = acc[(2 * t + 1) * pitch : (2 * t + 1) * pitch + group, :]
            out_ref[first : first + group, t * LANES : (t + 1) * LANES] = jnp.where(
                take_low, even, pltpu.roll(odd, BLK, 1)
            ).astype(BF16)
        yield


def triplet_kernel(s, group, picks_ref, l_ref, turned_ref, out_ref, *accs):
    for _ in triplet_steps(s, group, picks_ref, l_ref, turned_ref, out_ref, accs):
        pass


def acc_scratch(group):
    return [pltpu.VMEM((BLK * (group + 8), LANES), F32)] * 2


def chunk_scratch(half, chunk):
    return [pltpu.VMEM((chunk // BLK * (half + 8), LANES), F32)] * 4


def call(kernel, name, operands, out_shape, scratch, aliased=0, hbm=0, smem=0):
    spaces = [pltpu.SMEM] * smem + [pltpu.VMEM] * (len(operands) - smem - hbm) + [pltpu.HBM] * hbm
    plain = len(operands) - aliased
    operands = [
        value
        if space == pltpu.VMEM and at < plain
        else pltpu.with_memory_space_constraint(value, space)
        for at, (value, space) in enumerate(zip(operands, spaces))
    ]
    return pl.pallas_call(
        kernel,
        in_specs=[pl.BlockSpec(memory_space=space) for space in spaces],
        out_specs=[pl.BlockSpec(memory_space=pltpu.VMEM)] * len(out_shape),
        out_shape=out_shape,
        scratch_shapes=scratch,
        input_output_aliases={plain + at: at for at in range(aliased)},
        compiler_params=pltpu.CompilerParams(vmem_limit_bytes=VMEM_LIMIT),
        name=name,
    )(*operands)


def finish_kernel(s, run, pieces, mine_ref, theirs_ref, gate_ref, w_ref, *refs):
    weight = w_ref[...]
    cells = mine_ref.shape[-1]
    if s == 0:
        held = refs[0]
    else:
        before_ref, out_ref, held, sems = refs
        before = pltpu.make_async_copy(before_ref, out_ref.at[0], sems.at[pieces])
        before.start()
    size = cells // pieces

    def copy(n):
        to = pl.ds(pl.multiple_of(n * size, size), size)
        return pltpu.make_async_copy(held.at[:, to], out_ref.at[1, :, to], sems.at[n])

    @pl.loop(0, cells // run)
    def _(n):
        for start in range(0, run, LANES):
            to = cells_at(n, run, start)
            normed = normed_of(mine_ref[:, to], theirs_ref[:, to])
            projected = jnp.dot(weight, normed, preferred_element_type=F32)
            held[:, to] = (gate_ref[s, :, to].astype(F32) * projected).astype(BF16)
            done = start + LANES
            if s > 0 and done % size == 0:
                copy(n * (run // size) + done // size - 1).start()

    if s > 0:
        for n in range(pieces):
            copy(n).wait()
        before.wait()


def finish(s, mine, theirs, gate, weight, before=None):
    vmem = pl.BlockSpec(memory_space=pltpu.VMEM)
    operands = [mine, theirs, gate, weight]
    if s == 0:
        out_shape, out_specs, scratch = pltpu.VMEM(mine.shape, BF16), vmem, []
    else:
        operands.append(before)
        out_shape = jax.ShapeDtypeStruct(gate.shape, BF16)
        out_specs = pl.BlockSpec(memory_space=pltpu.HBM)
        scratch = [pltpu.VMEM(mine.shape, BF16), pltpu.SemaphoreType.DMA((5,))]
    return pl.pallas_call(
        functools.partial(finish_kernel, s, mine.shape[1] // 2, 4),
        in_specs=[vmem] * len(operands),
        out_specs=out_specs,
        out_shape=out_shape,
        scratch_shapes=scratch,
        compiler_params=pltpu.CompilerParams(vmem_limit_bytes=VMEM_LIMIT),
        name="finish",
    )(*operands)


def per_device(
    pair,
    ln_in_gain,
    a_weight,
    b_weight,
    ln_out_gain,
    out_gate_weight,
    out_weight,
    a_slots,
    b_slots,
    counts,
):
    slots, half, cells = pair.shape
    rows = lax.axis_size("row")
    swap = [(0, 1), (1, 0)]
    up = [(i, (i + 1) % rows) for i in range(rows)]
    down = [(i, (i - 1) % rows) for i in range(rows)]

    a_slots, b_slots = a_slots.T, b_slots.T
    weights = [
        jnp.swapaxes(a_weight, 1, 2),
        jnp.swapaxes(b_weight, 1, 2),
        out_gate_weight.T,
        out_weight.T,
        ln_in_gain[None, :],
        ln_out_gain[None, :],
    ]

    chunk = cells // 4
    cuts = ((0, 2 * chunk), (2 * chunk, 2 * chunk))
    picks, pair, *chosen = select_blocks(pair, a_slots, b_slots, counts, cuts)
    arrived = [
        (lax.ppermute(chosen[2 * n], "row", up), lax.ppermute(chosen[2 * n + 1], "row", down))
        for n in range(len(cuts))
    ]
    pair_other = lax.ppermute(pair, "chan", swap)
    left_shape = pltpu.VMEM((2, half, BLK, LANES), BF16)
    right_shape = pltpu.VMEM((5, half, BLK, BLK), BF16)
    lefts, rights, gate, weight, last_weight, gain = call(
        functools.partial(own_kernel, chunk),
        "project_own",
        [pair, pair_other, *weights],
        [
            left_shape,
            right_shape,
            pltpu.VMEM((slots, half, cells), BF16),
            pltpu.VMEM((4 * half, 2 * half), BF16),
            pltpu.VMEM((half, 2 * half), BF16),
            pltpu.VMEM((2 * half, LANES), F32),
        ],
        [pltpu.VMEM(value.shape, value.dtype) for value in weights]
        + [pltpu.VMEM((half, BLK, LANES), BF16)]
        + chunk_scratch(half, chunk)
        + [pltpu.SemaphoreType.DMA((len(weights),))],
        hbm=len(weights),
    )
    for (start, size), behind_ahead in zip(cuts, arrived):
        *behind_ahead, lefts = lax.optimization_barrier((*behind_ahead, lefts))
        if start == 0:
            others = [
                lax.ppermute(lax.slice_in_dim(value, at, at + chunk, axis=1), "chan", swap)
                for at in (0, chunk)
                for value in behind_ahead
            ]
            lefts, earlier = call(
                functools.partial(first_kernel, chunk),
                "project_first",
                [*behind_ahead, *others, weight, gain, lefts],
                [left_shape, pltpu.VMEM((half, size // BLK, LANES), BF16)],
                chunk_scratch(half, chunk),
                aliased=1,
            )
        else:
            others = [
                lax.ppermute(
                    jnp.stack([value[:, at : at + chunk] for value in behind_ahead]), "chan", swap
                )
                for at in (0, chunk)
            ]
            done = call(
                functools.partial(half_kernel, chunk),
                "project_half",
                [*behind_ahead, others[0], weight, gain],
                chunk_scratch(half, chunk)[:2],
                [],
            )
            lefts, rights, update = call(
                functools.partial(last_kernel, chunk, start // BLK, 16),
                "project_last",
                [picks, *behind_ahead, others[1], earlier, *done, weight, gain, lefts, rights],
                [left_shape, right_shape, pltpu.VMEM((half, cells), BF16)],
                [pltpu.VMEM((half, chunk // BLK, LANES), BF16)]
                + chunk_scratch(half, chunk)[:2]
                + acc_scratch(16),
                aliased=2,
                smem=1,
            )
    updates = [(update, lax.ppermute(update, "chan", swap))]
    update, lefts = lax.optimization_barrier((update, lefts))
    for s in range(1, slots):
        (update,) = call(
            functools.partial(triplet_kernel, s, 16),
            "triplets",
            [picks, lefts, rights],
            [pltpu.VMEM((half, cells), BF16)],
            acc_scratch(16),
            smem=1,
        )
        updates.append((update, lax.ppermute(update, "chan", swap)))
    out = None
    for s, (mine, theirs) in enumerate(updates):
        out = finish(s, mine, theirs, gate, last_weight, out)
    return out


def solution(mesh):
    in_specs = (
        P(("parts", "row", "col"), "chan", None),
        P(),
        P(None, None, "chan"),
        P(None, None, "chan"),
        P(),
        P(None, "chan"),
        P(None, "chan"),
        P("parts", None),
        P("parts", None),
        P("parts"),
    )
    out_specs = P(("parts", "row", "col"), "chan", None)
    return jax.shard_map(
        per_device, mesh=mesh, in_specs=in_specs, out_specs=out_specs, check_vma=False
    )
```

```python
import functools

import jax
import jax.numpy as jnp
from jax import lax
from jax.experimental import pallas as pl
from jax.experimental.pallas import tpu as pltpu
from jax.sharding import PartitionSpec as P

BLK = 64
LANES = 128
epsilon = 1e-05
VMEM_LIMIT = 24 * 1024 * 1024
F32 = jnp.float32
BF16 = jnp.bfloat16


def sigmoid(x):
    return 0.5 * jnp.tanh(0.5 * x) + 0.5


def tile_of(row, col):
    return row * lax.axis_size("col") + col


def neighbour_tiles():
    rows = lax.axis_size("row")
    row, col = lax.axis_index("row"), lax.axis_index("col")
    behind = lax.rem(row + rows - 1, rows)
    ahead = lax.rem(row + 1, rows)
    return tile_of(row, col), tile_of(behind, col), tile_of(ahead, col)


def used_picks(s, slots, triplets, a_ref, b_ref, n_ref):
    me, behind, ahead = neighbour_tiles()
    block = me * slots + s
    count = n_ref[block]
    picks = []
    for left_at in range(4):
        pick = jnp.int32(4)
        for m in range(triplets):
            left = a_ref[m, block]
            if left_at < 2:
                hit = left == me * slots + left_at
            else:
                base = (behind, ahead)[left_at - 2] * slots
                hit = jnp.logical_and(left >= base, left < base + slots)
            hit = jnp.logical_and(hit, m < count)
            place = b_ref[m, block] - me * slots
            from_me = jnp.logical_and(place >= 0, place < slots)
            right = b_ref[m, block] - behind * slots
            from_behind = jnp.logical_and(right >= 0, right < slots)
            place = jnp.where(from_me, place, jnp.where(from_behind, 2, 3))
            pick = jnp.where(hit, place, pick)
        picks.append(pick)
    return picks


def select_kernel(slots, triplets, cuts, a_hbm, b_hbm, n_hbm, pair_hbm, *refs):
    pair_ref, *out_refs = refs[: 1 + 2 * len(cuts)]
    a_ref, b_ref, n_ref, sems = refs[1 + 2 * len(cuts) :]
    me, behind, ahead = neighbour_tiles()
    whole = pltpu.make_async_copy(pair_hbm, pair_ref, sems.at[0])
    tables = [
        pltpu.make_async_copy(source, target, sems.at[1 + at])
        for at, (source, target) in enumerate(((a_hbm, a_ref), (b_hbm, b_ref), (n_hbm, n_ref)))
    ]
    for copy in (*tables, whole):
        copy.start()
    for copy in tables:
        copy.wait()
    chosen = []
    for target in (ahead, behind):
        pick = jnp.int32(0)
        for s in range(slots):
            count = n_ref[target * slots + s]
            for m in range(triplets):
                for ids in (a_ref, b_ref):
                    name = ids[m, target * slots + s] - me * slots
                    mine = jnp.logical_and(name >= 0, name < slots)
                    pick = jnp.where(jnp.logical_and(m < count, mine), name, pick)
        chosen.append(pick)
    whole.wait()
    for at, (start, size) in enumerate(cuts):
        for which, pick in enumerate(chosen):
            out_refs[2 * at + which][...] = pair_ref[pick, :, start : start + size]


def select_blocks(pair, a_slots, b_slots, counts, cuts):
    slots, channels, cells = pair.shape
    hbm = pl.BlockSpec(memory_space=pltpu.HBM)
    vmem = pl.BlockSpec(memory_space=pltpu.VMEM)
    out_shape = [pltpu.VMEM(pair.shape, pair.dtype)] + [
        pltpu.VMEM((channels, size), pair.dtype) for _, size in cuts for _ in range(2)
    ]
    operands = [
        pltpu.with_memory_space_constraint(value, pltpu.HBM)
        for value in (a_slots, b_slots, counts, pair)
    ]
    return pl.pallas_call(
        functools.partial(select_kernel, slots, a_slots.shape[0], cuts),
        out_shape=out_shape,
        in_specs=[hbm] * 4,
        out_specs=[vmem] * len(out_shape),
        scratch_shapes=[pltpu.SMEM(value.shape, value.dtype) for value in operands[:3]]
        + [pltpu.SemaphoreType.DMA((4,))],
        name="select_blocks",
    )(*operands)


def prepared(weight, gain=None):
    if gain is not None:
        weight = weight * gain
    rolled = pltpu.roll(weight, weight.shape[1] // 2, 1)
    return jnp.where(lax.axis_index("chan") == 0, weight, rolled).astype(BF16)


def gated_rows(w_ref):
    gate, value = w_ref[0].astype(F32), w_ref[1].astype(F32)
    rows = []
    for at in range(0, gate.shape[0], 8):
        rows += [gate[at : at + 8], value[at : at + 8]]
    return [0.5 * row for row in rows]


def normed_of(mine, theirs, gain=None):
    total = 2 * mine.shape[0]
    mine = mine.astype(F32)
    theirs = theirs.astype(F32)
    mean = jnp.sum(mine + theirs, axis=0, keepdims=True) * (1.0 / total)
    mine = mine - mean
    theirs = theirs - mean
    spread = jnp.sum(mine * mine + theirs * theirs, axis=0, keepdims=True) * (1.0 / total)
    scale = lax.rsqrt(spread + epsilon)
    mine = mine * scale
    theirs = theirs * scale
    if gain is not None:
        half = mine.shape[0]
        mine = mine * gain[:half]
        theirs = theirs * gain[half:]
    return jnp.concatenate([mine.astype(BF16), theirs.astype(BF16)], axis=0)


def gated_sides(mine, theirs, weight, gain, half):
    y = jnp.dot(weight, normed_of(mine, theirs, gain), preferred_element_type=F32)
    sides = []
    for side in range(2):
        groups = []
        for row in range(2 * half * side, 2 * half * (side + 1), 16):
            groups.append((jnp.tanh(y[row : row + 8]) + 1.0) * y[row + 8 : row + 16])
        sides.append(groups)
    return sides, y[4 * half :]


def pair_chunk(sides_at, chunk, held):
    low = lax.broadcasted_iota(jnp.int32, (8, LANES), 1) < BLK
    pitch = held[0].shape[0] // (chunk // BLK)
    for start in range(0, chunk, LANES):
        first, second = sides_at(start)
        i = start // BLK
        for out, values0, values1 in zip(held, first, second):
            for at, (v0, v1) in enumerate(zip(values0, values1)):
                even = slice(i * pitch + 8 * at, i * pitch + 8 * at + 8)
                odd = slice((i + 1) * pitch + 8 * at, (i + 1) * pitch + 8 * at + 8)
                out[even, :] = jnp.where(low, v0, pltpu.roll(v1, BLK, 1))
                out[odd, :] = jnp.where(low, pltpu.roll(v0, BLK, 1), v1)
        yield


def spread_chunk(rows, held, l_ref, pair_of, l_row, p_ref, p_row, before, turned_ref, half):
    pitch = held[0].shape[0] // rows
    to = pl.ds(pl.multiple_of(l_row, 16), rows)
    for c in range(half):
        take = pl.ds(c, rows, stride=pitch)
        l_ref[pair_of, c, to, :] = held[0][take, :].astype(BF16)
        right = held[1][take, :]
        if turned_ref is None:
            p_ref[c, pl.ds(pl.multiple_of(p_row, 16), rows), :] = right.astype(BF16)
        else:
            whole = jnp.concatenate([ref[c, :size].astype(F32) for ref, size in before] + [right])
            turned = jnp.transpose(whole).astype(BF16)
            turned_ref[2 * pair_of, c] = turned[:BLK]
            turned_ref[2 * pair_of + 1, c] = turned[BLK:]
        if c % 8 == 7:
            yield


def two_chunks(sides_at, n, chunk, held, spread, after=()):
    steps = [
        pair_chunk(functools.partial(sides_at, n + k), chunk, held[2 * k : 2 * k + 2])
        for k in range(2)
    ]
    spreads = [spread(n + k, held[2 * k : 2 * k + 2], k) for k in range(2)]
    for _ in steps[0]:
        pass
    for _ in zip(steps[1], spreads[0]):
        pass
    for _ in spreads[0]:
        pass
    for at, _ in enumerate(spreads[1]):
        if at > 0:
            next(iter(after), None)
    for _ in after:
        pass


def cells_at(n, chunk, start):
    return pl.ds(pl.multiple_of(n * chunk + start, LANES), LANES)


def own_kernel(chunk, *refs):
    m_ref, t_ref = refs[:2]
    sources = refs[2:11]
    picks_ref, l_ref, turned_ref, gate_ref, w_ref, v_ref, gain_ref = refs[11:18]
    targets = refs[18:27]
    p_ref, held, sems = refs[27], refs[28:32], refs[32]
    copies = [
        pltpu.make_async_copy(source, target, sems.at[at])
        for at, (source, target) in enumerate(zip(sources, targets))
    ]
    for copy in copies:
        copy.start()
    half = l_ref.shape[1]

    @pl.loop(0, half)
    def _(c):
        turned_ref[4, c] = jnp.zeros((BLK, BLK), BF16)

    for copy in copies:
        copy.wait()
    a_ref, b_ref, o_ref, u_ref, g_ref, h_ref, *tables = targets
    slots = m_ref.shape[0]
    for s in range(slots):
        for at, pick in enumerate(used_picks(s, slots, tables[0].shape[0], *tables)):
            picks_ref[4 * s + at] = pick
    rows = gated_rows(a_ref) + gated_rows(b_ref) + [0.5 * o_ref[...].astype(F32)]
    weight = prepared(jnp.concatenate(rows, axis=0))
    w_ref[...] = weight[: 4 * half]
    v_ref[...] = prepared(0.5 * u_ref[...].astype(F32), h_ref[...])
    across = jnp.transpose(jnp.broadcast_to(g_ref[...], (2 * half, LANES)))
    in_order = lax.axis_index("chan") == 0
    gain_ref[:half] = jnp.where(in_order, across[:half], across[half:])
    gain_ref[half:] = jnp.where(in_order, across[half:], across[:half])
    chunks = m_ref.shape[-1] // chunk
    rows = chunk // BLK

    def sides_at(n, start):
        at = cells_at(n, chunk, start)
        both = []
        for x in range(2):
            sides, rest = gated_sides(m_ref[x, :, at], t_ref[x, :, at], weight, gain_ref[...], half)
            gate_ref[x, :, at] = (jnp.tanh(rest) + 1.0).astype(BF16)
            both.append(sides)
        return both

    def spread(last, n, held, k):
        before, turned = ([(p_ref, (chunks - 1) * rows)], turned_ref) if last and k else (None, None)
        return spread_chunk(rows, held, l_ref, 0, n * rows, p_ref, n * rows, before, turned, half)

    @pl.loop(0, chunks - 2, step=2)
    def _(n):
        two_chunks(sides_at, n, chunk, held, functools.partial(spread, False))

    two_chunks(sides_at, chunks - 2, chunk, held, functools.partial(spread, True))


def fetched_sides(chunk, ours, theirs, weight, gain_ref, half):
    def sides_at(n, start):
        at = n * chunk + start
        both = []
        for x, m in enumerate(ours):
            if len(theirs) == 1:
                other = theirs[0][x, :, at : at + LANES]
            else:
                other = theirs[2 * n + x][:, start : start + LANES]
            both.append(
                gated_sides(m[:, at : at + LANES], other, weight, gain_ref[...], half)[0]
            )
        return both

    return sides_at


def first_kernel(chunk, *refs):
    *ours_theirs, w_ref, gain_ref, _, l_ref, p_ref = refs[:-4]
    held = refs[-4:]
    half = l_ref.shape[1]
    rows = chunk // BLK
    sides_at = fetched_sides(
        chunk, ours_theirs[:2], ours_theirs[2:], w_ref[...], gain_ref, half
    )

    def spread(n, held, k):
        return spread_chunk(rows, held, l_ref, 1, n * rows, p_ref, n * rows, None, None, half)

    two_chunks(sides_at, 0, chunk, held, spread)


def last_kernel(chunk, first_row, group, picks_ref, *refs):
    *ours_theirs, p0_ref, w_ref, gain_ref, _, _, l_ref, turned_ref, out_ref, p_ref = refs[:-6]
    held, accs = refs[-6:-2], refs[-2:]
    before = [(p0_ref, p0_ref.shape[1]), (p_ref, p_ref.shape[1])]
    half = l_ref.shape[1]
    rows = chunk // BLK
    sides_at = fetched_sides(
        chunk, ours_theirs[:2], ours_theirs[2:], w_ref[...], gain_ref, half
    )

    def spread(n, held, k):
        done = (before, turned_ref) if k else (None, None)
        return spread_chunk(rows, held, l_ref, 1, first_row + n * rows, p_ref, n * rows, *done, half)

    products = triplet_steps(0, group, picks_ref, l_ref, turned_ref, out_ref, accs)
    two_chunks(sides_at, 0, chunk, held, spread, products)


def triplet_steps(s, group, picks_ref, l_ref, turned_ref, out_ref, accs):
    picks = [picks_ref[4 * s + at] for at in range(4)]
    take_low = lax.broadcasted_iota(jnp.int32, (group, LANES), 1) < BLK
    pitch = accs[0].shape[0] // BLK
    for first in range(0, l_ref.shape[1], group):
        acc = accs[first // group % len(accs)]
        for at in range(group):
            c = first + at
            lhs = jnp.concatenate([l_ref[0, c], l_ref[1, c]], axis=1)
            rhs = jnp.concatenate([turned_ref[pick, c] for pick in picks], axis=0)
            acc[pl.ds(at, BLK, stride=pitch), :BLK] = jnp.dot(
                lhs, rhs, preferred_element_type=F32
            )
            if at % 8 == 7 and at + 1 < group:
                yield
        for t in range(BLK // 2):
            even = acc[2 * t * pitch : 2 * t * pitch + group, :]
            odd = acc[(2 * t + 1) * pitch : (2 * t + 1) * pitch + group, :]
            out_ref[first : first + group, t * LANES : (t + 1) * LANES] = jnp.where(
                take_low, even, pltpu.roll(odd, BLK, 1)
            ).astype(BF16)
        yield


def triplet_kernel(s, group, picks_ref, l_ref, turned_ref, out_ref, *accs):
    for _ in triplet_steps(s, group, picks_ref, l_ref, turned_ref, out_ref, accs):
        pass


def acc_scratch(group):
    return [pltpu.VMEM((BLK * (group + 8), LANES), F32)] * 2


def chunk_scratch(half, chunk):
    return [pltpu.VMEM((chunk // BLK * (half + 8), LANES), F32)] * 4


def call(kernel, name, operands, out_shape, scratch, aliased=0, hbm=0, smem=0):
    spaces = [pltpu.SMEM] * smem + [pltpu.VMEM] * (len(operands) - smem - hbm) + [pltpu.HBM] * hbm
    plain = len(operands) - aliased
    operands = [
        value
        if space == pltpu.VMEM and at < plain
        else pltpu.with_memory_space_constraint(value, space)
        for at, (value, space) in enumerate(zip(operands, spaces))
    ]
    return pl.pallas_call(
        kernel,
        in_specs=[pl.BlockSpec(memory_space=space) for space in spaces],
        out_specs=[pl.BlockSpec(memory_space=value.memory_space) for value in out_shape],
        out_shape=out_shape,
        scratch_shapes=scratch,
        input_output_aliases={plain + at: at for at in range(aliased)},
        compiler_params=pltpu.CompilerParams(vmem_limit_bytes=VMEM_LIMIT),
        name=name,
    )(*operands)


def finish_kernel(s, run, pieces, mine_ref, theirs_ref, gate_ref, w_ref, *refs):
    weight = w_ref[...]
    cells = mine_ref.shape[-1]
    if s == 0:
        held = refs[0]
    else:
        before_ref, out_ref, held, sems = refs
        before = pltpu.make_async_copy(before_ref, out_ref.at[0], sems.at[pieces])
        before.start()
    size = cells // pieces

    def copy(n):
        to = pl.ds(pl.multiple_of(n * size, size), size)
        return pltpu.make_async_copy(held.at[:, to], out_ref.at[1, :, to], sems.at[n])

    @pl.loop(0, cells // run)
    def _(n):
        for start in range(0, run, LANES):
            to = cells_at(n, run, start)
            normed = normed_of(mine_ref[:, to], theirs_ref[:, to])
            projected = jnp.dot(weight, normed, preferred_element_type=F32)
            held[:, to] = (gate_ref[s, :, to].astype(F32) * projected).astype(BF16)
            done = start + LANES
            if s > 0 and done % size == 0:
                copy(n * (run // size) + done // size - 1).start()

    if s > 0:
        for n in range(pieces):
            copy(n).wait()
        before.wait()


def finish(s, mine, theirs, gate, weight, before=None):
    vmem = pl.BlockSpec(memory_space=pltpu.VMEM)
    operands = [mine, theirs, gate, weight]
    if s == 0:
        out_shape, out_specs, scratch = pltpu.VMEM(mine.shape, BF16), vmem, []
    else:
        operands.append(before)
        out_shape = jax.ShapeDtypeStruct(gate.shape, BF16)
        out_specs = pl.BlockSpec(memory_space=pltpu.HBM)
        scratch = [pltpu.VMEM(mine.shape, BF16), pltpu.SemaphoreType.DMA((5,))]
    return pl.pallas_call(
        functools.partial(finish_kernel, s, mine.shape[1] // 2, 4),
        in_specs=[vmem] * len(operands),
        out_specs=out_specs,
        out_shape=out_shape,
        scratch_shapes=scratch,
        compiler_params=pltpu.CompilerParams(vmem_limit_bytes=VMEM_LIMIT),
        name="finish",
    )(*operands)


def per_device(
    pair,
    ln_in_gain,
    a_weight,
    b_weight,
    ln_out_gain,
    out_gate_weight,
    out_weight,
    a_slots,
    b_slots,
    counts,
):
    slots, half, cells = pair.shape
    rows = lax.axis_size("row")
    swap = [(0, 1), (1, 0)]
    up = [(i, (i + 1) % rows) for i in range(rows)]
    down = [(i, (i - 1) % rows) for i in range(rows)]

    a_slots, b_slots = a_slots.T, b_slots.T
    weights = [
        jnp.swapaxes(a_weight, 1, 2),
        jnp.swapaxes(b_weight, 1, 2),
        out_gate_weight.T,
        out_weight.T,
        ln_in_gain[None, :],
        ln_out_gain[None, :],
    ]

    chunk = cells // 4
    cuts = ((0, 2 * chunk), (2 * chunk, 2 * chunk))
    pair, *chosen = select_blocks(pair, a_slots, b_slots, counts, cuts)
    arrived = [
        (lax.ppermute(chosen[2 * n], "row", up), lax.ppermute(chosen[2 * n + 1], "row", down))
        for n in range(len(cuts))
    ]
    pair_other = lax.ppermute(pair, "chan", swap)
    left_shape = pltpu.VMEM((2, half, BLK, LANES), BF16)
    right_shape = pltpu.VMEM((5, half, BLK, BLK), BF16)
    sources = [*weights, a_slots, b_slots, counts]
    picks, lefts, rights, gate, weight, last_weight, gain = call(
        functools.partial(own_kernel, chunk),
        "project_own",
        [pair, pair_other, *sources],
        [
            pltpu.SMEM((4 * slots,), jnp.int32),
            left_shape,
            right_shape,
            pltpu.VMEM((slots, half, cells), BF16),
            pltpu.VMEM((4 * half, 2 * half), BF16),
            pltpu.VMEM((half, 2 * half), BF16),
            pltpu.VMEM((2 * half, LANES), F32),
        ],
        [pltpu.VMEM(value.shape, value.dtype) for value in weights]
        + [pltpu.SMEM(value.shape, value.dtype) for value in (a_slots, b_slots, counts)]
        + [pltpu.VMEM((half, BLK, LANES), BF16)]
        + chunk_scratch(half, chunk)
        + [pltpu.SemaphoreType.DMA((len(sources),))],
        hbm=len(sources),
    )
    for (start, size), behind_ahead in zip(cuts, arrived):
        *behind_ahead, lefts = lax.optimization_barrier((*behind_ahead, lefts))
        if start == 0:
            others = [
                lax.ppermute(lax.slice_in_dim(value, at, at + chunk, axis=1), "chan", swap)
                for at in (0, chunk)
                for value in behind_ahead
            ]
        else:
            others = [lax.ppermute(jnp.stack(behind_ahead), "chan", swap)]
        paired = pltpu.VMEM((half, size // BLK, LANES), BF16)
        if start == 0:
            lefts, rights_first = call(
                functools.partial(first_kernel, chunk),
                "project_first",
                [*behind_ahead, *others, weight, gain, lefts],
                [left_shape, paired],
                chunk_scratch(half, chunk),
                aliased=1,
            )
        else:
            lefts, rights, update = call(
                functools.partial(last_kernel, chunk, start // BLK, 16),
                "project_last",
                [picks, *behind_ahead, *others, rights_first, weight, gain, lefts, rights],
                [left_shape, right_shape, pltpu.VMEM((half, cells), BF16)],
                [pltpu.VMEM((half, chunk // BLK, LANES), BF16)]
                + chunk_scratch(half, chunk)
                + acc_scratch(16),
                aliased=2,
                smem=1,
            )
    updates = [(update, lax.ppermute(update, "chan", swap))]
    update, lefts = lax.optimization_barrier((update, lefts))
    for s in range(1, slots):
        (update,) = call(
            functools.partial(triplet_kernel, s, 16),
            "triplets",
            [picks, lefts, rights],
            [pltpu.VMEM((half, cells), BF16)],
            acc_scratch(16),
            smem=1,
        )
        updates.append((update, lax.ppermute(update, "chan", swap)))
    out = None
    for s, (mine, theirs) in enumerate(updates):
        out = finish(s, mine, theirs, gate, last_weight, out)
    return out


def solution(mesh):
    in_specs = (
        P(("parts", "row", "col"), "chan", None),
        P(),
        P(None, None, "chan"),
        P(None, None, "chan"),
        P(),
        P(None, "chan"),
        P(None, "chan"),
        P("parts", None),
        P("parts", None),
        P("parts"),
    )
    out_specs = P(("parts", "row", "col"), "chan", None)
    return jax.shard_map(
        per_device, mesh=mesh, in_specs=in_specs, out_specs=out_specs, check_vma=False
    )
```

```python
import functools

import jax
import jax.numpy as jnp
from jax import lax
from jax.experimental import pallas as pl
from jax.experimental.pallas import tpu as pltpu
from jax.sharding import PartitionSpec as P

BLK = 64
LANES = 128
epsilon = 1e-05
VMEM_LIMIT = 24 * 1024 * 1024
F32 = jnp.float32
BF16 = jnp.bfloat16


def sigmoid(x):
    return 0.5 * jnp.tanh(0.5 * x) + 0.5


def tile_of(row, col):
    return row * lax.axis_size("col") + col


def neighbour_tiles():
    rows = lax.axis_size("row")
    row, col = lax.axis_index("row"), lax.axis_index("col")
    behind = lax.rem(row + rows - 1, rows)
    ahead = lax.rem(row + 1, rows)
    return tile_of(row, col), tile_of(behind, col), tile_of(ahead, col)


def used_picks(s, slots, triplets, a_ref, b_ref, n_ref):
    me, behind, ahead = neighbour_tiles()
    block = me * slots + s
    count = n_ref[block]
    picks = []
    for left_at in range(4):
        pick = jnp.int32(4)
        for m in range(triplets):
            left = a_ref[m, block]
            if left_at < 2:
                hit = left == me * slots + left_at
            else:
                base = (behind, ahead)[left_at - 2] * slots
                hit = jnp.logical_and(left >= base, left < base + slots)
            hit = jnp.logical_and(hit, m < count)
            place = b_ref[m, block] - me * slots
            from_me = jnp.logical_and(place >= 0, place < slots)
            right = b_ref[m, block] - behind * slots
            from_behind = jnp.logical_and(right >= 0, right < slots)
            place = jnp.where(from_me, place, jnp.where(from_behind, 2, 3))
            pick = jnp.where(hit, place, pick)
        picks.append(pick)
    return picks


def select_kernel(slots, triplets, cuts, a_hbm, b_hbm, n_hbm, pair_hbm, *refs):
    picks_ref, pair_ref, *out_refs = refs[: 2 + 2 * len(cuts)]
    a_ref, b_ref, n_ref, sems = refs[2 + 2 * len(cuts) :]
    me, behind, ahead = neighbour_tiles()
    whole = pltpu.make_async_copy(pair_hbm, pair_ref, sems.at[0])
    tables = [
        pltpu.make_async_copy(source, target, sems.at[1 + at])
        for at, (source, target) in enumerate(((a_hbm, a_ref), (b_hbm, b_ref), (n_hbm, n_ref)))
    ]
    for copy in (*tables, whole):
        copy.start()
    for copy in tables:
        copy.wait()
    chosen = []
    for target in (ahead, behind):
        pick = jnp.int32(0)
        for s in range(slots):
            count = n_ref[target * slots + s]
            for m in range(triplets):
                for ids in (a_ref, b_ref):
                    name = ids[m, target * slots + s] - me * slots
                    mine = jnp.logical_and(name >= 0, name < slots)
                    pick = jnp.where(jnp.logical_and(m < count, mine), name, pick)
        chosen.append(pick)
    for s in range(slots):
        for at, pick in enumerate(used_picks(s, slots, triplets, a_ref, b_ref, n_ref)):
            picks_ref[4 * s + at] = pick
    whole.wait()
    for at, (start, size) in enumerate(cuts):
        for which, pick in enumerate(chosen):
            out_refs[2 * at + which][...] = pair_ref[pick, :, start : start + size]


def select_blocks(pair, a_slots, b_slots, counts, cuts):
    slots, channels, cells = pair.shape
    hbm = pl.BlockSpec(memory_space=pltpu.HBM)
    vmem = pl.BlockSpec(memory_space=pltpu.VMEM)
    out_shape = [pltpu.SMEM((4 * slots,), jnp.int32), pltpu.VMEM(pair.shape, pair.dtype)] + [
        pltpu.VMEM((channels, size), pair.dtype) for _, size in cuts for _ in range(2)
    ]
    operands = [
        pltpu.with_memory_space_constraint(value, pltpu.HBM)
        for value in (a_slots, b_slots, counts, pair)
    ]
    return pl.pallas_call(
        functools.partial(select_kernel, slots, a_slots.shape[0], cuts),
        out_shape=out_shape,
        in_specs=[hbm] * 4,
        out_specs=[pl.BlockSpec(memory_space=pltpu.SMEM)] + [vmem] * (len(out_shape) - 1),
        scratch_shapes=[pltpu.SMEM(value.shape, value.dtype) for value in operands[:3]]
        + [pltpu.SemaphoreType.DMA((4,))],
        name="select_blocks",
    )(*operands)


def prepared(weight, gain=None):
    if gain is not None:
        weight = weight * gain
    rolled = pltpu.roll(weight, weight.shape[1] // 2, 1)
    return jnp.where(lax.axis_index("chan") == 0, weight, rolled).astype(BF16)


def gated_rows(w_ref):
    gate, value = w_ref[0].astype(F32), w_ref[1].astype(F32)
    rows = []
    for at in range(0, gate.shape[0], 8):
        rows += [gate[at : at + 8], value[at : at + 8]]
    return [0.5 * row for row in rows]


def normed_of(mine, theirs, gain=None):
    total = 2 * mine.shape[0]
    mine = mine.astype(F32)
    theirs = theirs.astype(F32)
    mean = jnp.sum(mine + theirs, axis=0, keepdims=True) * (1.0 / total)
    mine = mine - mean
    theirs = theirs - mean
    spread = jnp.sum(mine * mine + theirs * theirs, axis=0, keepdims=True) * (1.0 / total)
    scale = lax.rsqrt(spread + epsilon)
    mine = mine * scale
    theirs = theirs * scale
    if gain is not None:
        half = mine.shape[0]
        mine = mine * gain[:half]
        theirs = theirs * gain[half:]
    return jnp.concatenate([mine.astype(BF16), theirs.astype(BF16)], axis=0)


def gated_sides(mine, theirs, weight, gain, half):
    y = jnp.dot(weight, normed_of(mine, theirs, gain), preferred_element_type=F32)
    sides = []
    for side in range(2):
        groups = []
        for row in range(2 * half * side, 2 * half * (side + 1), 16):
            groups.append((jnp.tanh(y[row : row + 8]) + 1.0) * y[row + 8 : row + 16])
        sides.append(groups)
    return sides, y[4 * half :]


def pair_chunk(sides_at, chunk, held):
    low = lax.broadcasted_iota(jnp.int32, (8, LANES), 1) < BLK
    pitch = held[0].shape[0] // (chunk // BLK)
    for start in range(0, chunk, LANES):
        first, second = sides_at(start)
        i = start // BLK
        for out, values0, values1 in zip(held, first, second):
            for at, (v0, v1) in enumerate(zip(values0, values1)):
                even = slice(i * pitch + 8 * at, i * pitch + 8 * at + 8)
                odd = slice((i + 1) * pitch + 8 * at, (i + 1) * pitch + 8 * at + 8)
                out[even, :] = jnp.where(low, v0, pltpu.roll(v1, BLK, 1))
                out[odd, :] = jnp.where(low, pltpu.roll(v0, BLK, 1), v1)
        yield


def spread_chunk(rows, held, l_ref, pair_of, l_row, p_ref, p_row, before, turned_ref, half):
    pitch = held[0].shape[0] // rows
    to = pl.ds(pl.multiple_of(l_row, 16), rows)
    for c in range(half):
        take = pl.ds(c, rows, stride=pitch)
        l_ref[pair_of, c, to, :] = held[0][take, :].astype(BF16)
        right = held[1][take, :]
        if turned_ref is None:
            p_ref[c, pl.ds(pl.multiple_of(p_row, 16), rows), :] = right.astype(BF16)
        else:
            whole = jnp.concatenate([ref[c, :size].astype(F32) for ref, size in before] + [right])
            turned = jnp.transpose(whole).astype(BF16)
            turned_ref[2 * pair_of, c] = turned[:BLK]
            turned_ref[2 * pair_of + 1, c] = turned[BLK:]
        if c % 8 == 7:
            yield


def two_chunks(sides_at, n, chunk, held, spread, after=()):
    steps = [
        pair_chunk(functools.partial(sides_at, n + k), chunk, held[2 * k : 2 * k + 2])
        for k in range(2)
    ]
    spreads = [spread(n + k, held[2 * k : 2 * k + 2], k) for k in range(2)]
    for _ in steps[0]:
        pass
    for _ in zip(steps[1], spreads[0]):
        pass
    for _ in spreads[0]:
        pass
    for at, _ in enumerate(spreads[1]):
        if at > 0:
            next(iter(after), None)
    for _ in after:
        pass


def cells_at(n, chunk, start):
    return pl.ds(pl.multiple_of(n * chunk + start, LANES), LANES)


def own_kernel(chunk, *refs):
    m_ref, t_ref = refs[:2]
    sources = refs[2:8]
    l_ref, turned_ref, gate_ref, w_ref, v_ref, gain_ref = refs[8:14]
    targets = refs[14:20]
    p_ref, held, sems = refs[20], refs[21:25], refs[25]
    copies = [
        pltpu.make_async_copy(source, target, sems.at[at])
        for at, (source, target) in enumerate(zip(sources, targets))
    ]
    for copy in copies:
        copy.start()
    half = l_ref.shape[1]

    @pl.loop(0, half)
    def _(c):
        turned_ref[4, c] = jnp.zeros((BLK, BLK), BF16)

    for copy in copies:
        copy.wait()
    a_ref, b_ref, o_ref, u_ref, g_ref, h_ref = targets
    rows = gated_rows(a_ref) + gated_rows(b_ref) + [0.5 * o_ref[...].astype(F32)]
    weight = prepared(jnp.concatenate(rows, axis=0))
    w_ref[...] = weight[: 4 * half]
    v_ref[...] = prepared(0.5 * u_ref[...].astype(F32), h_ref[...])
    across = jnp.transpose(jnp.broadcast_to(g_ref[...], (2 * half, LANES)))
    in_order = lax.axis_index("chan") == 0
    gain_ref[:half] = jnp.where(in_order, across[:half], across[half:])
    gain_ref[half:] = jnp.where(in_order, across[half:], across[:half])
    chunks = m_ref.shape[-1] // chunk
    rows = chunk // BLK

    def sides_at(n, start):
        at = cells_at(n, chunk, start)
        both = []
        for x in range(2):
            sides, rest = gated_sides(m_ref[x, :, at], t_ref[x, :, at], weight, gain_ref[...], half)
            gate_ref[x, :, at] = (jnp.tanh(rest) + 1.0).astype(BF16)
            both.append(sides)
        return both

    def spread(last, n, held, k):
        before, turned = ([(p_ref, (chunks - 1) * rows)], turned_ref) if last and k else (None, None)
        return spread_chunk(rows, held, l_ref, 0, n * rows, p_ref, n * rows, before, turned, half)

    @pl.loop(0, chunks - 2, step=2)
    def _(n):
        two_chunks(sides_at, n, chunk, held, functools.partial(spread, False))

    two_chunks(sides_at, chunks - 2, chunk, held, functools.partial(spread, True))


def fetched_sides(chunk, ours, theirs, weight, gain_ref, half):
    wide = theirs[0].shape[1]

    def sides_at(n, start):
        at = n * chunk + start
        both = []
        for x, m in enumerate(ours):
            other = theirs[2 * (at // wide) + x][:, at % wide : at % wide + LANES]
            both.append(
                gated_sides(m[:, at : at + LANES], other, weight, gain_ref[...], half)[0]
            )
        return both

    return sides_at


def first_kernel(chunk, *refs):
    *ours_theirs, w_ref, gain_ref, _, l_ref, p_ref = refs[:-4]
    held = refs[-4:]
    half = l_ref.shape[1]
    rows = chunk // BLK
    sides_at = fetched_sides(
        chunk, ours_theirs[:2], ours_theirs[2:], w_ref[...], gain_ref, half
    )

    def spread(n, held, k):
        return spread_chunk(rows, held, l_ref, 1, n * rows, p_ref, n * rows, None, None, half)

    two_chunks(sides_at, 0, chunk, held, spread)


def last_kernel(chunk, first_row, group, picks_ref, *refs):
    *ours_theirs, p0_ref, w_ref, gain_ref, _, _, l_ref, turned_ref, out_ref, p_ref = refs[:-6]
    held, accs = refs[-6:-2], refs[-2:]
    before = [(p0_ref, p0_ref.shape[1]), (p_ref, p_ref.shape[1])]
    half = l_ref.shape[1]
    rows = chunk // BLK
    sides_at = fetched_sides(
        chunk, ours_theirs[:2], ours_theirs[2:], w_ref[...], gain_ref, half
    )

    def spread(n, held, k):
        done = (before, turned_ref) if k else (None, None)
        return spread_chunk(rows, held, l_ref, 1, first_row + n * rows, p_ref, n * rows, *done, half)

    products = triplet_steps(0, group, picks_ref, l_ref, turned_ref, out_ref, accs)
    two_chunks(sides_at, 0, chunk, held, spread, products)


def triplet_steps(s, group, picks_ref, l_ref, turned_ref, out_ref, accs):
    picks = [picks_ref[4 * s + at] for at in range(4)]
    take_low = lax.broadcasted_iota(jnp.int32, (group, LANES), 1) < BLK
    pitch = accs[0].shape[0] // BLK
    for first in range(0, l_ref.shape[1], group):
        acc = accs[first // group % len(accs)]
        for at in range(group):
            c = first + at
            lhs = jnp.concatenate([l_ref[0, c], l_ref[1, c]], axis=1)
            rhs = jnp.concatenate([turned_ref[pick, c] for pick in picks], axis=0)
            acc[pl.ds(at, BLK, stride=pitch), :BLK] = jnp.dot(
                lhs, rhs, preferred_element_type=F32
            )
            if at % 8 == 7 and at + 1 < group:
                yield
        for t in range(BLK // 2):
            even = acc[2 * t * pitch : 2 * t * pitch + group, :]
            odd = acc[(2 * t + 1) * pitch : (2 * t + 1) * pitch + group, :]
            out_ref[first : first + group, t * LANES : (t + 1) * LANES] = jnp.where(
                take_low, even, pltpu.roll(odd, BLK, 1)
            ).astype(BF16)
        yield


def triplet_kernel(s, group, picks_ref, l_ref, turned_ref, out_ref, *accs):
    for _ in triplet_steps(s, group, picks_ref, l_ref, turned_ref, out_ref, accs):
        pass


def acc_scratch(group):
    return [pltpu.VMEM((BLK * (group + 8), LANES), F32)] * 2


def chunk_scratch(half, chunk):
    return [pltpu.VMEM((chunk // BLK * (half + 8), LANES), F32)] * 4


def call(kernel, name, operands, out_shape, scratch, aliased=0, hbm=0, smem=0):
    spaces = [pltpu.SMEM] * smem + [pltpu.VMEM] * (len(operands) - smem - hbm) + [pltpu.HBM] * hbm
    plain = len(operands) - aliased
    operands = [
        value
        if space == pltpu.VMEM and at < plain
        else pltpu.with_memory_space_constraint(value, space)
        for at, (value, space) in enumerate(zip(operands, spaces))
    ]
    return pl.pallas_call(
        kernel,
        in_specs=[pl.BlockSpec(memory_space=space) for space in spaces],
        out_specs=[pl.BlockSpec(memory_space=pltpu.VMEM)] * len(out_shape),
        out_shape=out_shape,
        scratch_shapes=scratch,
        input_output_aliases={plain + at: at for at in range(aliased)},
        compiler_params=pltpu.CompilerParams(vmem_limit_bytes=VMEM_LIMIT),
        name=name,
    )(*operands)


def finish_kernel(s, pieces, mine_ref, theirs_ref, gate_ref, w_ref, *refs):
    weight = w_ref[...]
    cells = mine_ref.shape[-1]
    size = cells // pieces
    if s == 0:
        out_ref, rest_ref, held, sems = refs
        written = pieces // 2
    else:
        before_ref, _, out_ref, held, sems = refs
        written = pieces
        late = pl.ds(cells // 2, cells // 2)
        before = pltpu.make_async_copy(before_ref, out_ref.at[0, :, late], sems.at[pieces])
        before.start()
    copies = []
    for n in range(pieces):
        for start in range(n * size, (n + 1) * size, LANES):
            to = slice(start, start + LANES)
            normed = normed_of(mine_ref[:, to], theirs_ref[:, to])
            projected = jnp.dot(weight, normed, preferred_element_type=F32)
            value = (gate_ref[s, :, to].astype(F32) * projected).astype(BF16)
            if n < written:
                held[:, to] = value
            else:
                rest_ref[:, start - written * size : start - written * size + LANES] = value
        if n < written:
            to = pl.ds(n * size, size)
            copies.append(
                pltpu.make_async_copy(held.at[:, to], out_ref.at[s, :, to], sems.at[n])
            )
            copies[-1].start()
    for copy in copies:
        copy.wait()
    if s > 0:
        before.wait()


def finish(s, mine, theirs, gate, weight, before=()):
    vmem = pl.BlockSpec(memory_space=pltpu.VMEM)
    hbm = pl.BlockSpec(memory_space=pltpu.HBM)
    half, cells = mine.shape
    pieces = 4
    operands = [mine, theirs, gate, weight, *before]
    in_specs = [vmem] * len(operands)
    out_shape = [jax.ShapeDtypeStruct(gate.shape, BF16)]
    out_specs = [hbm]
    aliases = {}
    if s == 0:
        out_shape.append(pltpu.VMEM((half, cells // 2), BF16))
        out_specs.append(vmem)
        wide = cells // 2
    else:
        aliases = {len(operands) - 1: 0}
        in_specs[-1] = hbm
        wide = cells
    return pl.pallas_call(
        functools.partial(finish_kernel, s, pieces),
        in_specs=in_specs,
        out_specs=out_specs,
        out_shape=out_shape,
        scratch_shapes=[pltpu.VMEM((half, wide), BF16), pltpu.SemaphoreType.DMA((pieces + 1,))],
        input_output_aliases=aliases,
        compiler_params=pltpu.CompilerParams(vmem_limit_bytes=VMEM_LIMIT),
        name="finish",
    )(*operands)


def per_device(
    pair,
    ln_in_gain,
    a_weight,
    b_weight,
    ln_out_gain,
    out_gate_weight,
    out_weight,
    a_slots,
    b_slots,
    counts,
):
    slots, half, cells = pair.shape
    rows = lax.axis_size("row")
    swap = [(0, 1), (1, 0)]
    up = [(i, (i + 1) % rows) for i in range(rows)]
    down = [(i, (i - 1) % rows) for i in range(rows)]

    a_slots, b_slots = a_slots.T, b_slots.T
    weights = [
        jnp.swapaxes(a_weight, 1, 2),
        jnp.swapaxes(b_weight, 1, 2),
        out_gate_weight.T,
        out_weight.T,
        ln_in_gain[None, :],
        ln_out_gain[None, :],
    ]

    chunk = cells // 4
    cuts = ((0, 2 * chunk), (2 * chunk, 2 * chunk))
    picks, pair, *chosen = select_blocks(pair, a_slots, b_slots, counts, cuts)
    arrived = [
        (lax.ppermute(chosen[2 * n], "row", up), lax.ppermute(chosen[2 * n + 1], "row", down))
        for n in range(len(cuts))
    ]
    pair_other = lax.ppermute(pair, "chan", swap)
    left_shape = pltpu.VMEM((2, half, BLK, LANES), BF16)
    right_shape = pltpu.VMEM((5, half, BLK, BLK), BF16)
    lefts, rights, gate, weight, last_weight, gain = call(
        functools.partial(own_kernel, chunk),
        "project_own",
        [pair, pair_other, *weights],
        [
            left_shape,
            right_shape,
            pltpu.VMEM((slots, half, cells), BF16),
            pltpu.VMEM((4 * half, 2 * half), BF16),
            pltpu.VMEM((half, 2 * half), BF16),
            pltpu.VMEM((2 * half, LANES), F32),
        ],
        [pltpu.VMEM(value.shape, value.dtype) for value in weights]
        + [pltpu.VMEM((half, BLK, LANES), BF16)]
        + chunk_scratch(half, chunk)
        + [pltpu.SemaphoreType.DMA((len(weights),))],
        hbm=len(weights),
    )
    for (start, size), behind_ahead in zip(cuts, arrived):
        *behind_ahead, lefts = lax.optimization_barrier((*behind_ahead, lefts))
        wide = chunk if start == 0 else size
        others = [
            lax.ppermute(lax.slice_in_dim(value, at, at + wide, axis=1), "chan", swap)
            for at in range(0, size, wide)
            for value in behind_ahead
        ]
        paired = pltpu.VMEM((half, size // BLK, LANES), BF16)
        if start == 0:
            lefts, rights_first = call(
                functools.partial(first_kernel, chunk),
                "project_first",
                [*behind_ahead, *others, weight, gain, lefts],
                [left_shape, paired],
                chunk_scratch(half, chunk),
                aliased=1,
            )
        else:
            lefts, rights, update = call(
                functools.partial(last_kernel, chunk, start // BLK, 16),
                "project_last",
                [picks, *behind_ahead, *others, rights_first, weight, gain, lefts, rights],
                [left_shape, right_shape, pltpu.VMEM((half, cells), BF16)],
                [pltpu.VMEM((half, chunk // BLK, LANES), BF16)]
                + chunk_scratch(half, chunk)
                + acc_scratch(16),
                aliased=2,
                smem=1,
            )
    updates = [(update, lax.ppermute(update, "chan", swap))]
    update, lefts = lax.optimization_barrier((update, lefts))
    for s in range(1, slots):
        (update,) = call(
            functools.partial(triplet_kernel, s, 16),
            "triplets",
            [picks, lefts, rights],
            [pltpu.VMEM((half, cells), BF16)],
            acc_scratch(16),
            smem=1,
        )
        updates.append((update, lax.ppermute(update, "chan", swap)))
    out, rest = finish(0, *updates[0], gate, last_weight)
    (out,) = finish(1, *updates[1], gate, last_weight, (rest, out))
    return out


def solution(mesh):
    in_specs = (
        P(("parts", "row", "col"), "chan", None),
        P(),
        P(None, None, "chan"),
        P(None, None, "chan"),
        P(),
        P(None, "chan"),
        P(None, "chan"),
        P("parts", None),
        P("parts", None),
        P("parts"),
    )
    out_specs = P(("parts", "row", "col"), "chan", None)
    return jax.shard_map(
        per_device, mesh=mesh, in_specs=in_specs, out_specs=out_specs, check_vma=False
    )
```

```python
import functools

import jax
import jax.numpy as jnp
from jax import lax
from jax.experimental import pallas as pl
from jax.experimental.pallas import tpu as pltpu
from jax.sharding import PartitionSpec as P

BLK = 64
LANES = 128
epsilon = 1e-05
VMEM_LIMIT = 24 * 1024 * 1024
F32 = jnp.float32
BF16 = jnp.bfloat16


def sigmoid(x):
    return 0.5 * jnp.tanh(0.5 * x) + 0.5


def tile_of(row, col):
    return row * lax.axis_size("col") + col


def neighbour_tiles():
    rows = lax.axis_size("row")
    row, col = lax.axis_index("row"), lax.axis_index("col")
    behind = lax.rem(row + rows - 1, rows)
    ahead = lax.rem(row + 1, rows)
    return tile_of(row, col), tile_of(behind, col), tile_of(ahead, col)


def used_picks(s, slots, triplets, a_ref, b_ref, n_ref):
    me, behind, ahead = neighbour_tiles()
    block = me * slots + s
    count = n_ref[block]
    picks = []
    for left_at in range(4):
        pick = jnp.int32(4)
        for m in range(triplets):
            left = a_ref[m, block]
            if left_at < 2:
                hit = left == me * slots + left_at
            else:
                base = (behind, ahead)[left_at - 2] * slots
                hit = jnp.logical_and(left >= base, left < base + slots)
            hit = jnp.logical_and(hit, m < count)
            place = b_ref[m, block] - me * slots
            from_me = jnp.logical_and(place >= 0, place < slots)
            right = b_ref[m, block] - behind * slots
            from_behind = jnp.logical_and(right >= 0, right < slots)
            place = jnp.where(from_me, place, jnp.where(from_behind, 2, 3))
            pick = jnp.where(hit, place, pick)
        picks.append(pick)
    return picks


def select_kernel(slots, triplets, cuts, a_hbm, b_hbm, n_hbm, pair_hbm, *refs):
    picks_ref, pair_ref, *out_refs = refs[: 2 + 2 * len(cuts)]
    a_ref, b_ref, n_ref, sems = refs[2 + 2 * len(cuts) :]
    me, behind, ahead = neighbour_tiles()
    tables = [
        pltpu.make_async_copy(source, target, sems.at[at])
        for at, (source, target) in enumerate(((a_hbm, a_ref), (b_hbm, b_ref), (n_hbm, n_ref)))
    ]
    pieces = [(s, row) for s in range(slots) for row in range(0, pair_ref.shape[1], 16)]
    fetches = [
        pltpu.make_async_copy(
            pair_hbm.at[s, pl.ds(row, 16)], pair_ref.at[s, pl.ds(row, 16)], sems.at[3 + at]
        )
        for at, (s, row) in enumerate(pieces)
    ]
    for copy in (*tables, *fetches):
        copy.start()
    for copy in tables:
        copy.wait()
    chosen = []
    for target in (ahead, behind):
        pick = jnp.int32(0)
        for s in range(slots):
            count = n_ref[target * slots + s]
            for m in range(triplets):
                for ids in (a_ref, b_ref):
                    name = ids[m, target * slots + s] - me * slots
                    mine = jnp.logical_and(name >= 0, name < slots)
                    pick = jnp.where(jnp.logical_and(m < count, mine), name, pick)
        chosen.append(pick)
    for s in range(slots):
        for at, pick in enumerate(used_picks(s, slots, triplets, a_ref, b_ref, n_ref)):
            picks_ref[4 * s + at] = pick
    for copy in fetches:
        copy.wait()
    for at, (start, size) in enumerate(cuts):
        for which, pick in enumerate(chosen):
            out_refs[2 * at + which][...] = pair_ref[pick, :, start : start + size]


def select_blocks(pair, a_slots, b_slots, counts, cuts):
    slots, channels, cells = pair.shape
    hbm = pl.BlockSpec(memory_space=pltpu.HBM)
    vmem = pl.BlockSpec(memory_space=pltpu.VMEM)
    out_shape = [pltpu.SMEM((4 * slots,), jnp.int32), pltpu.VMEM(pair.shape, pair.dtype)] + [
        pltpu.VMEM((channels, size), pair.dtype) for _, size in cuts for _ in range(2)
    ]
    operands = [
        pltpu.with_memory_space_constraint(value, pltpu.HBM)
        for value in (a_slots, b_slots, counts, pair)
    ]
    return pl.pallas_call(
        functools.partial(select_kernel, slots, a_slots.shape[0], cuts),
        out_shape=out_shape,
        in_specs=[hbm] * 4,
        out_specs=[pl.BlockSpec(memory_space=pltpu.SMEM)] + [vmem] * (len(out_shape) - 1),
        scratch_shapes=[pltpu.SMEM(value.shape, value.dtype) for value in operands[:3]]
        + [pltpu.SemaphoreType.DMA((3 + slots * channels // 16,))],
        name="select_blocks",
    )(*operands)


def prepared(weight, gain=None):
    if gain is not None:
        weight = weight * gain
    rolled = pltpu.roll(weight, weight.shape[1] // 2, 1)
    return jnp.where(lax.axis_index("chan") == 0, weight, rolled).astype(BF16)


def gated_rows(w_ref):
    gate, value = w_ref[0].astype(F32), w_ref[1].astype(F32)
    rows = []
    for at in range(0, gate.shape[0], 8):
        rows += [gate[at : at + 8], value[at : at + 8]]
    return [0.5 * row for row in rows]


def normed_of(mine, theirs, gain=None):
    total = 2 * mine.shape[0]
    mine = mine.astype(F32)
    theirs = theirs.astype(F32)
    mean = jnp.sum(mine + theirs, axis=0, keepdims=True) * (1.0 / total)
    mine = mine - mean
    theirs = theirs - mean
    spread = jnp.sum(mine * mine + theirs * theirs, axis=0, keepdims=True) * (1.0 / total)
    scale = lax.rsqrt(spread + epsilon)
    mine = mine * scale
    theirs = theirs * scale
    if gain is not None:
        half = mine.shape[0]
        mine = mine * gain[:half]
        theirs = theirs * gain[half:]
    return jnp.concatenate([mine.astype(BF16), theirs.astype(BF16)], axis=0)


def gated_sides(mine, theirs, weight, gain, half):
    y = jnp.dot(weight, normed_of(mine, theirs, gain), preferred_element_type=F32)
    sides = []
    for side in range(2):
        groups = []
        for row in range(2 * half * side, 2 * half * (side + 1), 16):
            groups.append((jnp.tanh(y[row : row + 8]) + 1.0) * y[row + 8 : row + 16])
        sides.append(groups)
    return sides, y[4 * half :]


def pair_chunk(sides_at, chunk, held):
    low = lax.broadcasted_iota(jnp.int32, (8, LANES), 1) < BLK
    pitch = held[0].shape[0] // (chunk // BLK)
    for start in range(0, chunk, LANES):
        first, second = sides_at(start)
        i = start // BLK
        for out, values0, values1 in zip(held, first, second):
            for at, (v0, v1) in enumerate(zip(values0, values1)):
                even = slice(i * pitch + 8 * at, i * pitch + 8 * at + 8)
                odd = slice((i + 1) * pitch + 8 * at, (i + 1) * pitch + 8 * at + 8)
                out[even, :] = jnp.where(low, v0, pltpu.roll(v1, BLK, 1))
                out[odd, :] = jnp.where(low, pltpu.roll(v0, BLK, 1), v1)
        yield


def spread_chunk(rows, held, l_ref, pair_of, l_row, p_ref, p_row, before, turned_ref, half):
    pitch = held[0].shape[0] // rows
    to = pl.ds(pl.multiple_of(l_row, 16), rows)
    for c in range(half):
        take = pl.ds(c, rows, stride=pitch)
        l_ref[pair_of, c, to, :] = held[0][take, :].astype(BF16)
        right = held[1][take, :]
        if turned_ref is None:
            p_ref[c, pl.ds(pl.multiple_of(p_row, 16), rows), :] = right.astype(BF16)
        else:
            whole = jnp.concatenate([ref[c, :size].astype(F32) for ref, size in before] + [right])
            turned = jnp.transpose(whole).astype(BF16)
            turned_ref[2 * pair_of, c] = turned[:BLK]
            turned_ref[2 * pair_of + 1, c] = turned[BLK:]
        if c % 8 == 7:
            yield


def two_chunks(sides_at, n, chunk, held, spread, after=()):
    steps = [
        pair_chunk(functools.partial(sides_at, n + k), chunk, held[2 * k : 2 * k + 2])
        for k in range(2)
    ]
    spreads = [spread(n + k, held[2 * k : 2 * k + 2], k) for k in range(2)]
    for _ in steps[0]:
        pass
    for _ in zip(steps[1], spreads[0]):
        pass
    for _ in spreads[0]:
        pass
    for at, _ in enumerate(spreads[1]):
        if at > 0:
            next(iter(after), None)
    for _ in after:
        pass


def cells_at(n, chunk, start):
    return pl.ds(pl.multiple_of(n * chunk + start, LANES), LANES)


def own_kernel(chunk, *refs):
    m_ref, t_ref = refs[:2]
    sources = refs[2:8]
    l_ref, turned_ref, gate_ref, w_ref, v_ref, gain_ref = refs[8:14]
    targets = refs[14:20]
    p_ref, held, sems = refs[20], refs[21:25], refs[25]
    copies = [
        pltpu.make_async_copy(source, target, sems.at[at])
        for at, (source, target) in enumerate(zip(sources, targets))
    ]
    for copy in copies:
        copy.start()
    half = l_ref.shape[1]

    @pl.loop(0, half)
    def _(c):
        turned_ref[4, c] = jnp.zeros((BLK, BLK), BF16)

    for copy in copies:
        copy.wait()
    a_ref, b_ref, o_ref, u_ref, g_ref, h_ref = targets
    rows = gated_rows(a_ref) + gated_rows(b_ref) + [0.5 * o_ref[...].astype(F32)]
    weight = prepared(jnp.concatenate(rows, axis=0))
    w_ref[...] = weight[: 4 * half]
    v_ref[...] = prepared(0.5 * u_ref[...].astype(F32), h_ref[...])
    across = jnp.transpose(jnp.broadcast_to(g_ref[...], (2 * half, LANES)))
    in_order = lax.axis_index("chan") == 0
    gain_ref[:half] = jnp.where(in_order, across[:half], across[half:])
    gain_ref[half:] = jnp.where(in_order, across[half:], across[:half])
    chunks = m_ref.shape[-1] // chunk
    rows = chunk // BLK

    def sides_at(n, start):
        at = cells_at(n, chunk, start)
        both = []
        for x in range(2):
            sides, rest = gated_sides(m_ref[x, :, at], t_ref[x, :, at], weight, gain_ref[...], half)
            gate_ref[x, :, at] = (jnp.tanh(rest) + 1.0).astype(BF16)
            both.append(sides)
        return both

    def spread(last, n, held, k):
        before, turned = ([(p_ref, (chunks - 1) * rows)], turned_ref) if last and k else (None, None)
        return spread_chunk(rows, held, l_ref, 0, n * rows, p_ref, n * rows, before, turned, half)

    @pl.loop(0, chunks - 2, step=2)
    def _(n):
        two_chunks(sides_at, n, chunk, held, functools.partial(spread, False))

    two_chunks(sides_at, chunks - 2, chunk, held, functools.partial(spread, True))


def fetched_sides(chunk, ours, theirs, weight, gain_ref, half):
    wide = theirs[0].shape[1]

    def sides_at(n, start):
        at = n * chunk + start
        both = []
        for x, m in enumerate(ours):
            other = theirs[2 * (at // wide) + x][:, at % wide : at % wide + LANES]
            both.append(
                gated_sides(m[:, at : at + LANES], other, weight, gain_ref[...], half)[0]
            )
        return both

    return sides_at


def first_kernel(chunk, *refs):
    *ours_theirs, w_ref, gain_ref, _, l_ref, p_ref = refs[:-4]
    held = refs[-4:]
    half = l_ref.shape[1]
    rows = chunk // BLK
    sides_at = fetched_sides(
        chunk, ours_theirs[:2], ours_theirs[2:], w_ref[...], gain_ref, half
    )

    def spread(n, held, k):
        return spread_chunk(rows, held, l_ref, 1, n * rows, p_ref, n * rows, None, None, half)

    two_chunks(sides_at, 0, chunk, held, spread)


def last_kernel(chunk, first_row, group, picks_ref, *refs):
    *ours_theirs, p0_ref, w_ref, gain_ref, _, _, l_ref, turned_ref, out_ref, p_ref = refs[:-6]
    held, accs = refs[-6:-2], refs[-2:]
    before = [(p0_ref, p0_ref.shape[1]), (p_ref, p_ref.shape[1])]
    half = l_ref.shape[1]
    rows = chunk // BLK
    sides_at = fetched_sides(
        chunk, ours_theirs[:2], ours_theirs[2:], w_ref[...], gain_ref, half
    )

    def spread(n, held, k):
        done = (before, turned_ref) if k else (None, None)
        return spread_chunk(rows, held, l_ref, 1, first_row + n * rows, p_ref, n * rows, *done, half)

    products = triplet_steps(0, group, picks_ref, l_ref, turned_ref, out_ref, accs)
    two_chunks(sides_at, 0, chunk, held, spread, products)


def triplet_steps(s, group, picks_ref, l_ref, turned_ref, out_ref, accs):
    picks = [picks_ref[4 * s + at] for at in range(4)]
    take_low = lax.broadcasted_iota(jnp.int32, (group, LANES), 1) < BLK
    pitch = accs[0].shape[0] // BLK
    for first in range(0, l_ref.shape[1], group):
        acc = accs[first // group % len(accs)]
        for at in range(group):
            c = first + at
            lhs = jnp.concatenate([l_ref[0, c], l_ref[1, c]], axis=1)
            rhs = jnp.concatenate([turned_ref[pick, c] for pick in picks], axis=0)
            acc[pl.ds(at, BLK, stride=pitch), :BLK] = jnp.dot(
                lhs, rhs, preferred_element_type=F32
            )
            if at % 8 == 7 and at + 1 < group:
                yield
        for t in range(BLK // 2):
            even = acc[2 * t * pitch : 2 * t * pitch + group, :]
            odd = acc[(2 * t + 1) * pitch : (2 * t + 1) * pitch + group, :]
            out_ref[first : first + group, t * LANES : (t + 1) * LANES] = jnp.where(
                take_low, even, pltpu.roll(odd, BLK, 1)
            ).astype(BF16)
        yield


def triplet_kernel(s, group, picks_ref, l_ref, turned_ref, out_ref, *accs):
    for _ in triplet_steps(s, group, picks_ref, l_ref, turned_ref, out_ref, accs):
        pass


def acc_scratch(group):
    return [pltpu.VMEM((BLK * (group + 8), LANES), F32)] * 2


def chunk_scratch(half, chunk):
    return [pltpu.VMEM((chunk // BLK * (half + 8), LANES), F32)] * 4


def call(kernel, name, operands, out_shape, scratch, aliased=0, hbm=0, smem=0):
    spaces = [pltpu.SMEM] * smem + [pltpu.VMEM] * (len(operands) - smem - hbm) + [pltpu.HBM] * hbm
    plain = len(operands) - aliased
    operands = [
        value
        if space == pltpu.VMEM and at < plain
        else pltpu.with_memory_space_constraint(value, space)
        for at, (value, space) in enumerate(zip(operands, spaces))
    ]
    return pl.pallas_call(
        kernel,
        in_specs=[pl.BlockSpec(memory_space=space) for space in spaces],
        out_specs=[pl.BlockSpec(memory_space=pltpu.VMEM)] * len(out_shape),
        out_shape=out_shape,
        scratch_shapes=scratch,
        input_output_aliases={plain + at: at for at in range(aliased)},
        compiler_params=pltpu.CompilerParams(vmem_limit_bytes=VMEM_LIMIT),
        name=name,
    )(*operands)


def finish_kernel(s, run, pieces, mine_ref, theirs_ref, gate_ref, w_ref, *refs):
    weight = w_ref[...]
    cells = mine_ref.shape[-1]
    if s == 0:
        held = refs[0]
    else:
        before_ref, out_ref, held, sems = refs
        befores = [
            pltpu.make_async_copy(
                before_ref.at[pl.ds(row, 16)], out_ref.at[0, pl.ds(row, 16)], sems.at[pieces + row // 16]
            )
            for row in range(0, before_ref.shape[0], 16)
        ]
        for copy_before in befores:
            copy_before.start()
    size = cells // pieces

    def copy(n):
        to = pl.ds(pl.multiple_of(n * size, size), size)
        return pltpu.make_async_copy(held.at[:, to], out_ref.at[1, :, to], sems.at[n])

    @pl.loop(0, cells // run)
    def _(n):
        for start in range(0, run, LANES):
            to = cells_at(n, run, start)
            normed = normed_of(mine_ref[:, to], theirs_ref[:, to])
            projected = jnp.dot(weight, normed, preferred_element_type=F32)
            held[:, to] = (gate_ref[s, :, to].astype(F32) * projected).astype(BF16)
            done = start + LANES
            if s > 0 and done % size == 0:
                copy(n * (run // size) + done // size - 1).start()

    if s > 0:
        for n in range(pieces):
            copy(n).wait()
        for copy_before in befores:
            copy_before.wait()


def finish(s, mine, theirs, gate, weight, before=None):
    vmem = pl.BlockSpec(memory_space=pltpu.VMEM)
    operands = [mine, theirs, gate, weight]
    if s == 0:
        out_shape, out_specs, scratch = pltpu.VMEM(mine.shape, BF16), vmem, []
    else:
        operands.append(before)
        out_shape = jax.ShapeDtypeStruct(gate.shape, BF16)
        out_specs = pl.BlockSpec(memory_space=pltpu.HBM)
        scratch = [pltpu.VMEM(mine.shape, BF16), pltpu.SemaphoreType.DMA((4 + mine.shape[0] // 16,))]
    return pl.pallas_call(
        functools.partial(finish_kernel, s, mine.shape[1] // 2, 4),
        in_specs=[vmem] * len(operands),
        out_specs=out_specs,
        out_shape=out_shape,
        scratch_shapes=scratch,
        compiler_params=pltpu.CompilerParams(vmem_limit_bytes=VMEM_LIMIT),
        name="finish",
    )(*operands)


def per_device(
    pair,
    ln_in_gain,
    a_weight,
    b_weight,
    ln_out_gain,
    out_gate_weight,
    out_weight,
    a_slots,
    b_slots,
    counts,
):
    slots, half, cells = pair.shape
    rows = lax.axis_size("row")
    swap = [(0, 1), (1, 0)]
    up = [(i, (i + 1) % rows) for i in range(rows)]
    down = [(i, (i - 1) % rows) for i in range(rows)]

    a_slots, b_slots = a_slots.T, b_slots.T
    weights = [
        jnp.swapaxes(a_weight, 1, 2),
        jnp.swapaxes(b_weight, 1, 2),
        out_gate_weight.T,
        out_weight.T,
        ln_in_gain[None, :],
        ln_out_gain[None, :],
    ]

    chunk = cells // 4
    cuts = ((0, 2 * chunk), (2 * chunk, 2 * chunk))
    picks, pair, *chosen = select_blocks(pair, a_slots, b_slots, counts, cuts)
    arrived = [
        (lax.ppermute(chosen[2 * n], "row", up), lax.ppermute(chosen[2 * n + 1], "row", down))
        for n in range(len(cuts))
    ]
    pair_other = lax.ppermute(pair, "chan", swap)
    left_shape = pltpu.VMEM((2, half, BLK, LANES), BF16)
    right_shape = pltpu.VMEM((5, half, BLK, BLK), BF16)
    lefts, rights, gate, weight, last_weight, gain = call(
        functools.partial(own_kernel, chunk),
        "project_own",
        [pair, pair_other, *weights],
        [
            left_shape,
            right_shape,
            pltpu.VMEM((slots, half, cells), BF16),
            pltpu.VMEM((4 * half, 2 * half), BF16),
            pltpu.VMEM((half, 2 * half), BF16),
            pltpu.VMEM((2 * half, LANES), F32),
        ],
        [pltpu.VMEM(value.shape, value.dtype) for value in weights]
        + [pltpu.VMEM((half, BLK, LANES), BF16)]
        + chunk_scratch(half, chunk)
        + [pltpu.SemaphoreType.DMA((len(weights),))],
        hbm=len(weights),
    )
    for (start, size), behind_ahead in zip(cuts, arrived):
        *behind_ahead, lefts = lax.optimization_barrier((*behind_ahead, lefts))
        wide = chunk if start == 0 else size
        others = [
            lax.ppermute(lax.slice_in_dim(value, at, at + wide, axis=1), "chan", swap)
            for at in range(0, size, wide)
            for value in behind_ahead
        ]
        paired = pltpu.VMEM((half, size // BLK, LANES), BF16)
        if start == 0:
            lefts, rights_first = call(
                functools.partial(first_kernel, chunk),
                "project_first",
                [*behind_ahead, *others, weight, gain, lefts],
                [left_shape, paired],
                chunk_scratch(half, chunk),
                aliased=1,
            )
        else:
            lefts, rights, update = call(
                functools.partial(last_kernel, chunk, start // BLK, 16),
                "project_last",
                [picks, *behind_ahead, *others, rights_first, weight, gain, lefts, rights],
                [left_shape, right_shape, pltpu.VMEM((half, cells), BF16)],
                [pltpu.VMEM((half, chunk // BLK, LANES), BF16)]
                + chunk_scratch(half, chunk)
                + acc_scratch(16),
                aliased=2,
                smem=1,
            )
    updates = [(update, lax.ppermute(update, "chan", swap))]
    update, lefts = lax.optimization_barrier((update, lefts))
    for s in range(1, slots):
        (update,) = call(
            functools.partial(triplet_kernel, s, 16),
            "triplets",
            [picks, lefts, rights],
            [pltpu.VMEM((half, cells), BF16)],
            acc_scratch(16),
            smem=1,
        )
        updates.append((update, lax.ppermute(update, "chan", swap)))
    out = None
    for s, (mine, theirs) in enumerate(updates):
        out = finish(s, mine, theirs, gate, last_weight, out)
    return out


def solution(mesh):
    in_specs = (
        P(("parts", "row", "col"), "chan", None),
        P(),
        P(None, None, "chan"),
        P(None, None, "chan"),
        P(),
        P(None, "chan"),
        P(None, "chan"),
        P("parts", None),
        P("parts", None),
        P("parts"),
    )
    out_specs = P(("parts", "row", "col"), "chan", None)
    return jax.shard_map(
        per_device, mesh=mesh, in_specs=in_specs, out_specs=out_specs, check_vma=False
    )
```

```python
import functools

import jax
import jax.numpy as jnp
from jax import lax
from jax.experimental import pallas as pl
from jax.experimental.pallas import tpu as pltpu
from jax.sharding import PartitionSpec as P

BLK = 64
LANES = 128
epsilon = 1e-05
VMEM_LIMIT = 24 * 1024 * 1024
F32 = jnp.float32
BF16 = jnp.bfloat16


def sigmoid(x):
    return 0.5 * jnp.tanh(0.5 * x) + 0.5


def tile_of(row, col):
    return row * lax.axis_size("col") + col


def neighbour_tiles():
    rows = lax.axis_size("row")
    row, col = lax.axis_index("row"), lax.axis_index("col")
    behind = lax.rem(row + rows - 1, rows)
    ahead = lax.rem(row + 1, rows)
    return tile_of(row, col), tile_of(behind, col), tile_of(ahead, col)


def used_picks(s, slots, triplets, a_ref, b_ref, n_ref):
    me, behind, ahead = neighbour_tiles()
    block = me * slots + s
    count = n_ref[block]
    picks = []
    for left_at in range(4):
        pick = jnp.int32(4)
        for m in range(triplets):
            left = a_ref[m, block]
            if left_at < 2:
                hit = left == me * slots + left_at
            else:
                base = (behind, ahead)[left_at - 2] * slots
                hit = jnp.logical_and(left >= base, left < base + slots)
            hit = jnp.logical_and(hit, m < count)
            place = b_ref[m, block] - me * slots
            from_me = jnp.logical_and(place >= 0, place < slots)
            right = b_ref[m, block] - behind * slots
            from_behind = jnp.logical_and(right >= 0, right < slots)
            place = jnp.where(from_me, place, jnp.where(from_behind, 2, 3))
            pick = jnp.where(hit, place, pick)
        picks.append(pick)
    return picks


def select_kernel(slots, triplets, cuts, a_hbm, b_hbm, n_hbm, pair_hbm, *refs):
    picks_ref, pair_ref, *out_refs = refs[: 2 + 2 * len(cuts)]
    a_ref, b_ref, n_ref, sems = refs[2 + 2 * len(cuts) :]
    me, behind, ahead = neighbour_tiles()
    whole = pltpu.make_async_copy(pair_hbm, pair_ref, sems.at[0])
    tables = [
        pltpu.make_async_copy(source, target, sems.at[1 + at])
        for at, (source, target) in enumerate(((a_hbm, a_ref), (b_hbm, b_ref), (n_hbm, n_ref)))
    ]
    for copy in (*tables, whole):
        copy.start()
    for copy in tables:
        copy.wait()
    chosen = []
    for target in (ahead, behind):
        pick = jnp.int32(0)
        for s in range(slots):
            count = n_ref[target * slots + s]
            for m in range(triplets):
                for ids in (a_ref, b_ref):
                    name = ids[m, target * slots + s] - me * slots
                    mine = jnp.logical_and(name >= 0, name < slots)
                    pick = jnp.where(jnp.logical_and(m < count, mine), name, pick)
        chosen.append(pick)
    for s in range(slots):
        for at, pick in enumerate(used_picks(s, slots, triplets, a_ref, b_ref, n_ref)):
            picks_ref[4 * s + at] = pick
    whole.wait()
    for at, (start, size) in enumerate(cuts):
        for which, pick in enumerate(chosen):
            out_refs[2 * at + which][...] = pair_ref[pick, :, start : start + size]


def select_blocks(pair, a_slots, b_slots, counts, cuts):
    slots, channels, cells = pair.shape
    hbm = pl.BlockSpec(memory_space=pltpu.HBM)
    vmem = pl.BlockSpec(memory_space=pltpu.VMEM)
    out_shape = [pltpu.SMEM((4 * slots,), jnp.int32), pltpu.VMEM(pair.shape, pair.dtype)] + [
        pltpu.VMEM((channels, size), pair.dtype) for _, size in cuts for _ in range(2)
    ]
    operands = [
        pltpu.with_memory_space_constraint(value, pltpu.HBM)
        for value in (a_slots, b_slots, counts, pair)
    ]
    return pl.pallas_call(
        functools.partial(select_kernel, slots, a_slots.shape[0], cuts),
        out_shape=out_shape,
        in_specs=[hbm] * 4,
        out_specs=[pl.BlockSpec(memory_space=pltpu.SMEM)] + [vmem] * (len(out_shape) - 1),
        scratch_shapes=[pltpu.SMEM(value.shape, value.dtype) for value in operands[:3]]
        + [pltpu.SemaphoreType.DMA((4,))],
        name="select_blocks",
    )(*operands)


def prepared(weight, gain=None):
    if gain is not None:
        weight = weight * gain
    rolled = pltpu.roll(weight, weight.shape[1] // 2, 1)
    return jnp.where(lax.axis_index("chan") == 0, weight, rolled).astype(BF16)


def gated_rows(w_ref):
    gate, value = w_ref[0].astype(F32), w_ref[1].astype(F32)
    rows = []
    for at in range(0, gate.shape[0], 8):
        rows += [gate[at : at + 8], value[at : at + 8]]
    return [0.5 * row for row in rows]


def normed_of(mine, theirs, gain=None):
    total = 2 * mine.shape[0]
    mine = mine.astype(F32)
    theirs = theirs.astype(F32)
    mean = jnp.sum(mine + theirs, axis=0, keepdims=True) * (1.0 / total)
    mine = mine - mean
    theirs = theirs - mean
    spread = jnp.sum(mine * mine + theirs * theirs, axis=0, keepdims=True) * (1.0 / total)
    scale = lax.rsqrt(spread + epsilon)
    mine = mine * scale
    theirs = theirs * scale
    if gain is not None:
        half = mine.shape[0]
        mine = mine * gain[:half]
        theirs = theirs * gain[half:]
    return jnp.concatenate([mine.astype(BF16), theirs.astype(BF16)], axis=0)


def gated_sides(mine, theirs, weight, gain, half):
    y = jnp.dot(weight, normed_of(mine, theirs, gain), preferred_element_type=F32)
    sides = []
    for side in range(2):
        groups = []
        for row in range(2 * half * side, 2 * half * (side + 1), 16):
            groups.append((jnp.tanh(y[row : row + 8]) + 1.0) * y[row + 8 : row + 16])
        sides.append(groups)
    return sides, y[4 * half :]


def pair_chunk(sides_at, chunk, held):
    low = lax.broadcasted_iota(jnp.int32, (8, LANES), 1) < BLK
    pitch = held[0].shape[0] // (chunk // BLK)
    for start in range(0, chunk, LANES):
        first, second = sides_at(start)
        i = start // BLK
        for out, values0, values1 in zip(held, first, second):
            for at, (v0, v1) in enumerate(zip(values0, values1)):
                even = slice(i * pitch + 8 * at, i * pitch + 8 * at + 8)
                odd = slice((i + 1) * pitch + 8 * at, (i + 1) * pitch + 8 * at + 8)
                out[even, :] = jnp.where(low, v0, pltpu.roll(v1, BLK, 1))
                out[odd, :] = jnp.where(low, pltpu.roll(v0, BLK, 1), v1)
        yield


def spread_chunk(rows, held, l_ref, pair_of, l_row, p_ref, p_row, before, turned_ref, half):
    pitch = held[0].shape[0] // rows
    to = pl.ds(pl.multiple_of(l_row, 16), rows)
    for c in range(half):
        take = pl.ds(c, rows, stride=pitch)
        l_ref[pair_of, c, to, :] = held[0][take, :].astype(BF16)
        right = held[1][take, :]
        if turned_ref is None:
            p_ref[c, pl.ds(pl.multiple_of(p_row, 16), rows), :] = right.astype(BF16)
        else:
            whole = jnp.concatenate([ref[c, :size].astype(F32) for ref, size in before] + [right])
            turned = jnp.transpose(whole).astype(BF16)
            turned_ref[2 * pair_of, c] = turned[:BLK]
            turned_ref[2 * pair_of + 1, c] = turned[BLK:]
        if c % 8 == 7:
            yield


def two_chunks(sides_at, n, chunk, held, spread, after=()):
    steps = [
        pair_chunk(functools.partial(sides_at, n + k), chunk, held[2 * k : 2 * k + 2])
        for k in range(2)
    ]
    spreads = [spread(n + k, held[2 * k : 2 * k + 2], k) for k in range(2)]
    for _ in steps[0]:
        pass
    for _ in zip(steps[1], spreads[0]):
        pass
    for _ in spreads[0]:
        pass
    for at, _ in enumerate(spreads[1]):
        if at > 0:
            next(iter(after), None)
    for _ in after:
        pass


def cells_at(n, chunk, start):
    return pl.ds(pl.multiple_of(n * chunk + start, LANES), LANES)


def own_kernel(chunk, *refs):
    m_ref, t_ref = refs[:2]
    sources = refs[2:8]
    l_ref, turned_ref, gate_ref, w_ref, v_ref, gain_ref = refs[8:14]
    targets = refs[14:20]
    p_ref, held, sems = refs[20], refs[21:25], refs[25]
    copies = [
        pltpu.make_async_copy(source, target, sems.at[at])
        for at, (source, target) in enumerate(zip(sources, targets))
    ]
    for copy in copies:
        copy.start()
    half = l_ref.shape[1]

    @pl.loop(0, half)
    def _(c):
        turned_ref[4, c] = jnp.zeros((BLK, BLK), BF16)

    for copy in copies:
        copy.wait()
    a_ref, b_ref, o_ref, u_ref, g_ref, h_ref = targets
    rows = gated_rows(a_ref) + gated_rows(b_ref) + [0.5 * o_ref[...].astype(F32)]
    weight = prepared(jnp.concatenate(rows, axis=0))
    w_ref[...] = weight[: 4 * half]
    v_ref[...] = prepared(0.5 * u_ref[...].astype(F32), h_ref[...])
    across = jnp.transpose(jnp.broadcast_to(g_ref[...], (2 * half, LANES)))
    in_order = lax.axis_index("chan") == 0
    gain_ref[:half] = jnp.where(in_order, across[:half], across[half:])
    gain_ref[half:] = jnp.where(in_order, across[half:], across[:half])
    chunks = m_ref.shape[-1] // chunk
    rows = chunk // BLK

    def sides_at(n, start):
        at = cells_at(n, chunk, start)
        both = []
        for x in range(2):
            sides, rest = gated_sides(m_ref[x, :, at], t_ref[x, :, at], weight, gain_ref[...], half)
            gate_ref[x, :, at] = (jnp.tanh(rest) + 1.0).astype(BF16)
            both.append(sides)
        return both

    def spread(last, n, held, k):
        before, turned = ([(p_ref, (chunks - 1) * rows)], turned_ref) if last and k else (None, None)
        return spread_chunk(rows, held, l_ref, 0, n * rows, p_ref, n * rows, before, turned, half)

    @pl.loop(0, chunks - 2, step=2)
    def _(n):
        two_chunks(sides_at, n, chunk, held, functools.partial(spread, False))

    two_chunks(sides_at, chunks - 2, chunk, held, functools.partial(spread, True))


def fetched_sides(chunk, ours, theirs, weight, gain_ref, half):
    wide = theirs[0].shape[1]

    def sides_at(n, start):
        at = n * chunk + start
        both = []
        for x, m in enumerate(ours):
            other = theirs[2 * (at // wide) + x][:, at % wide : at % wide + LANES]
            both.append(
                gated_sides(m[:, at : at + LANES], other, weight, gain_ref[...], half)[0]
            )
        return both

    return sides_at


def first_kernel(chunk, *refs):
    *ours_theirs, w_ref, gain_ref, _, l_ref, p_ref = refs[:-4]
    held = refs[-4:]
    half = l_ref.shape[1]
    rows = chunk // BLK
    sides_at = fetched_sides(
        chunk, ours_theirs[:2], ours_theirs[2:], w_ref[...], gain_ref, half
    )

    def spread(n, held, k):
        return spread_chunk(rows, held, l_ref, 1, n * rows, p_ref, n * rows, None, None, half)

    two_chunks(sides_at, 0, chunk, held, spread)


def last_kernel(chunk, first_row, group, picks_ref, *refs):
    *ours_theirs, p0_ref, w_ref, gain_ref, _, _, l_ref, turned_ref, out_ref, p_ref = refs[:-6]
    held, accs = refs[-6:-2], refs[-2:]
    before = [(p0_ref, p0_ref.shape[1]), (p_ref, p_ref.shape[1])]
    half = l_ref.shape[1]
    rows = chunk // BLK
    sides_at = fetched_sides(
        chunk, ours_theirs[:2], ours_theirs[2:], w_ref[...], gain_ref, half
    )

    def spread(n, held, k):
        done = (before, turned_ref) if k else (None, None)
        return spread_chunk(rows, held, l_ref, 1, first_row + n * rows, p_ref, n * rows, *done, half)

    products = triplet_steps(0, group, picks_ref, l_ref, turned_ref, out_ref, accs)
    two_chunks(sides_at, 0, chunk, held, spread, products)


def triplet_steps(s, group, picks_ref, l_ref, turned_ref, out_ref, accs):
    picks = [picks_ref[4 * s + at] for at in range(4)]
    take_low = lax.broadcasted_iota(jnp.int32, (group, LANES), 1) < BLK
    pitch = accs[0].shape[0] // BLK
    for first in range(0, l_ref.shape[1], group):
        acc = accs[first // group % len(accs)]
        for at in range(group):
            c = first + at
            lhs = jnp.concatenate([l_ref[0, c], l_ref[1, c]], axis=1)
            rhs = jnp.concatenate([turned_ref[pick, c] for pick in picks], axis=0)
            acc[pl.ds(at, BLK, stride=pitch), :BLK] = jnp.dot(
                lhs, rhs, preferred_element_type=F32
            )
            if at % 8 == 7 and at + 1 < group:
                yield
        for t in range(BLK // 2):
            even = acc[2 * t * pitch : 2 * t * pitch + group, :]
            odd = acc[(2 * t + 1) * pitch : (2 * t + 1) * pitch + group, :]
            out_ref[first : first + group, t * LANES : (t + 1) * LANES] = jnp.where(
                take_low, even, pltpu.roll(odd, BLK, 1)
            ).astype(BF16)
        yield


def triplet_kernel(s, group, picks_ref, l_ref, turned_ref, out_ref, *accs):
    for _ in triplet_steps(s, group, picks_ref, l_ref, turned_ref, out_ref, accs):
        pass


def acc_scratch(group):
    return [pltpu.VMEM((BLK * (group + 8), LANES), F32)] * 2


def chunk_scratch(half, chunk):
    return [pltpu.VMEM((chunk // BLK * (half + 8), LANES), F32)] * 4


def call(kernel, name, operands, out_shape, scratch, aliased=0, hbm=0, smem=0):
    spaces = [pltpu.SMEM] * smem + [pltpu.VMEM] * (len(operands) - smem - hbm) + [pltpu.HBM] * hbm
    plain = len(operands) - aliased
    operands = [
        value
        if space == pltpu.VMEM and at < plain
        else pltpu.with_memory_space_constraint(value, space)
        for at, (value, space) in enumerate(zip(operands, spaces))
    ]
    return pl.pallas_call(
        kernel,
        in_specs=[pl.BlockSpec(memory_space=space) for space in spaces],
        out_specs=[pl.BlockSpec(memory_space=pltpu.VMEM)] * len(out_shape),
        out_shape=out_shape,
        scratch_shapes=scratch,
        input_output_aliases={plain + at: at for at in range(aliased)},
        compiler_params=pltpu.CompilerParams(vmem_limit_bytes=VMEM_LIMIT),
        name=name,
    )(*operands)


def finish_kernel(s, run, pieces, mine_ref, theirs_ref, gate_ref, w_ref, *refs):
    weight = w_ref[...]
    cells = mine_ref.shape[-1]
    if s == 0:
        held = refs[0]
    else:
        before_ref, out_ref, held, sems = refs
        before = pltpu.make_async_copy(before_ref, out_ref.at[0], sems.at[pieces])
        before.start()
    size = cells // pieces

    def copy(n):
        to = pl.ds(pl.multiple_of(n * size, size), size)
        return pltpu.make_async_copy(held.at[:, to], out_ref.at[1, :, to], sems.at[n])

    @pl.loop(0, cells // run)
    def _(n):
        for start in range(0, run, LANES):
            to = cells_at(n, run, start)
            normed = normed_of(mine_ref[:, to], theirs_ref[:, to])
            projected = jnp.dot(weight, normed, preferred_element_type=F32)
            held[:, to] = (gate_ref[s, :, to].astype(F32) * projected).astype(BF16)
            done = start + LANES
            if s > 0 and done % size == 0:
                copy(n * (run // size) + done // size - 1).start()

    if s > 0:
        for n in range(pieces):
            copy(n).wait()
        before.wait()


def finish(s, mine, theirs, gate, weight, before=None):
    vmem = pl.BlockSpec(memory_space=pltpu.VMEM)
    operands = [mine, theirs, gate, weight]
    if s == 0:
        out_shape, out_specs, scratch = pltpu.VMEM(mine.shape, BF16), vmem, []
    else:
        operands.append(before)
        out_shape = jax.ShapeDtypeStruct(gate.shape, BF16)
        out_specs = pl.BlockSpec(memory_space=pltpu.HBM)
        scratch = [pltpu.VMEM(mine.shape, BF16), pltpu.SemaphoreType.DMA((5,))]
    return pl.pallas_call(
        functools.partial(finish_kernel, s, mine.shape[1], 4),
        in_specs=[vmem] * len(operands),
        out_specs=out_specs,
        out_shape=out_shape,
        scratch_shapes=scratch,
        compiler_params=pltpu.CompilerParams(vmem_limit_bytes=VMEM_LIMIT),
        name="finish",
    )(*operands)


def per_device(
    pair,
    ln_in_gain,
    a_weight,
    b_weight,
    ln_out_gain,
    out_gate_weight,
    out_weight,
    a_slots,
    b_slots,
    counts,
):
    slots, half, cells = pair.shape
    rows = lax.axis_size("row")
    swap = [(0, 1), (1, 0)]
    up = [(i, (i + 1) % rows) for i in range(rows)]
    down = [(i, (i - 1) % rows) for i in range(rows)]

    a_slots, b_slots = a_slots.T, b_slots.T
    weights = [
        jnp.swapaxes(a_weight, 1, 2),
        jnp.swapaxes(b_weight, 1, 2),
        out_gate_weight.T,
        out_weight.T,
        ln_in_gain[None, :],
        ln_out_gain[None, :],
    ]

    chunk = cells // 4
    cuts = ((0, 2 * chunk), (2 * chunk, 2 * chunk))
    picks, pair, *chosen = select_blocks(pair, a_slots, b_slots, counts, cuts)
    arrived = []
    for n in range(len(cuts)):
        moved = {}
        for which in (0, 1) if n == 0 else (1, 0):
            moved[which] = lax.ppermute(chosen[2 * n + which], "row", (up, down)[which])
        arrived.append((moved[0], moved[1]))
    pair_other = lax.ppermute(pair, "chan", swap)
    left_shape = pltpu.VMEM((2, half, BLK, LANES), BF16)
    right_shape = pltpu.VMEM((5, half, BLK, BLK), BF16)
    lefts, rights, gate, weight, last_weight, gain = call(
        functools.partial(own_kernel, chunk),
        "project_own",
        [pair, pair_other, *weights],
        [
            left_shape,
            right_shape,
            pltpu.VMEM((slots, half, cells), BF16),
            pltpu.VMEM((4 * half, 2 * half), BF16),
            pltpu.VMEM((half, 2 * half), BF16),
            pltpu.VMEM((2 * half, LANES), F32),
        ],
        [pltpu.VMEM(value.shape, value.dtype) for value in weights]
        + [pltpu.VMEM((half, BLK, LANES), BF16)]
        + chunk_scratch(half, chunk)
        + [pltpu.SemaphoreType.DMA((len(weights),))],
        hbm=len(weights),
    )
    for (start, size), behind_ahead in zip(cuts, arrived):
        *behind_ahead, lefts = lax.optimization_barrier((*behind_ahead, lefts))
        wide = chunk if start == 0 else size
        others = [
            lax.ppermute(lax.slice_in_dim(value, at, at + wide, axis=1), "chan", swap)
            for at in range(0, size, wide)
            for value in behind_ahead
        ]
        paired = pltpu.VMEM((half, size // BLK, LANES), BF16)
        if start == 0:
            lefts, rights_first = call(
                functools.partial(first_kernel, chunk),
                "project_first",
                [*behind_ahead, *others, weight, gain, lefts],
                [left_shape, paired],
                chunk_scratch(half, chunk),
                aliased=1,
            )
        else:
            lefts, rights, update = call(
                functools.partial(last_kernel, chunk, start // BLK, 16),
                "project_last",
                [picks, *behind_ahead, *others, rights_first, weight, gain, lefts, rights],
                [left_shape, right_shape, pltpu.VMEM((half, cells), BF16)],
                [pltpu.VMEM((half, chunk // BLK, LANES), BF16)]
                + chunk_scratch(half, chunk)
                + acc_scratch(16),
                aliased=2,
                smem=1,
            )
    updates = [(update, lax.ppermute(update, "chan", swap))]
    update, lefts = lax.optimization_barrier((update, lefts))
    for s in range(1, slots):
        (update,) = call(
            functools.partial(triplet_kernel, s, 16),
            "triplets",
            [picks, lefts, rights],
            [pltpu.VMEM((half, cells), BF16)],
            acc_scratch(16),
            smem=1,
        )
        updates.append((update, lax.ppermute(update, "chan", swap)))
    out = None
    for s, (mine, theirs) in enumerate(updates):
        out = finish(s, mine, theirs, gate, last_weight, out)
    return out


def solution(mesh):
    in_specs = (
        P(("parts", "row", "col"), "chan", None),
        P(),
        P(None, None, "chan"),
        P(None, None, "chan"),
        P(),
        P(None, "chan"),
        P(None, "chan"),
        P("parts", None),
        P("parts", None),
        P("parts"),
    )
    out_specs = P(("parts", "row", "col"), "chan", None)
    return jax.shard_map(
        per_device, mesh=mesh, in_specs=in_specs, out_specs=out_specs, check_vma=False
    )
```

```python
import functools

import jax
import jax.numpy as jnp
from jax import lax
from jax.experimental import pallas as pl
from jax.experimental.pallas import tpu as pltpu
from jax.sharding import PartitionSpec as P

BLK = 64
LANES = 128
epsilon = 1e-05
VMEM_LIMIT = 24 * 1024 * 1024
F32 = jnp.float32
BF16 = jnp.bfloat16


def sigmoid(x):
    return 0.5 * jnp.tanh(0.5 * x) + 0.5


def tile_of(row, col):
    return row * lax.axis_size("col") + col


def neighbour_tiles():
    rows = lax.axis_size("row")
    row, col = lax.axis_index("row"), lax.axis_index("col")
    behind = lax.rem(row + rows - 1, rows)
    ahead = lax.rem(row + 1, rows)
    return tile_of(row, col), tile_of(behind, col), tile_of(ahead, col)


def used_picks(s, slots, triplets, a_ref, b_ref, n_ref):
    me, behind, ahead = neighbour_tiles()
    block = me * slots + s
    count = n_ref[block]
    picks = []
    for left_at in range(4):
        pick = jnp.int32(4)
        for m in range(triplets):
            left = a_ref[m, block]
            if left_at < 2:
                hit = left == me * slots + left_at
            else:
                base = (behind, ahead)[left_at - 2] * slots
                hit = jnp.logical_and(left >= base, left < base + slots)
            hit = jnp.logical_and(hit, m < count)
            place = b_ref[m, block] - me * slots
            from_me = jnp.logical_and(place >= 0, place < slots)
            right = b_ref[m, block] - behind * slots
            from_behind = jnp.logical_and(right >= 0, right < slots)
            place = jnp.where(from_me, place, jnp.where(from_behind, 2, 3))
            pick = jnp.where(hit, place, pick)
        picks.append(pick)
    return picks


def select_kernel(slots, triplets, cuts, a_hbm, b_hbm, n_hbm, pair_hbm, *refs):
    picks_ref, pair_ref, *out_refs = refs[: 2 + 2 * len(cuts)]
    a_ref, b_ref, n_ref, sems = refs[2 + 2 * len(cuts) :]
    me, behind, ahead = neighbour_tiles()
    whole = pltpu.make_async_copy(pair_hbm, pair_ref, sems.at[0])
    tables = [
        pltpu.make_async_copy(source, target, sems.at[1 + at])
        for at, (source, target) in enumerate(((a_hbm, a_ref), (b_hbm, b_ref), (n_hbm, n_ref)))
    ]
    for copy in (*tables, whole):
        copy.start()
    for copy in tables:
        copy.wait()
    chosen = []
    for target in (ahead, behind):
        pick = jnp.int32(0)
        for s in range(slots):
            count = n_ref[target * slots + s]
            for m in range(triplets):
                for ids in (a_ref, b_ref):
                    name = ids[m, target * slots + s] - me * slots
                    mine = jnp.logical_and(name >= 0, name < slots)
                    pick = jnp.where(jnp.logical_and(m < count, mine), name, pick)
        chosen.append(pick)
    for s in range(slots):
        for at, pick in enumerate(used_picks(s, slots, triplets, a_ref, b_ref, n_ref)):
            picks_ref[4 * s + at] = pick
    whole.wait()
    for at, (start, size) in enumerate(cuts):
        for which, pick in enumerate(chosen):
            out_refs[2 * at + which][...] = pair_ref[pick, :, start : start + size]


def select_blocks(pair, a_slots, b_slots, counts, cuts):
    slots, channels, cells = pair.shape
    hbm = pl.BlockSpec(memory_space=pltpu.HBM)
    vmem = pl.BlockSpec(memory_space=pltpu.VMEM)
    out_shape = [pltpu.SMEM((4 * slots,), jnp.int32), pltpu.VMEM(pair.shape, pair.dtype)] + [
        pltpu.VMEM((channels, size), pair.dtype) for _, size in cuts for _ in range(2)
    ]
    operands = [
        pltpu.with_memory_space_constraint(value, pltpu.HBM)
        for value in (a_slots, b_slots, counts, pair)
    ]
    return pl.pallas_call(
        functools.partial(select_kernel, slots, a_slots.shape[0], cuts),
        out_shape=out_shape,
        in_specs=[hbm] * 4,
        out_specs=[pl.BlockSpec(memory_space=pltpu.SMEM)] + [vmem] * (len(out_shape) - 1),
        scratch_shapes=[pltpu.SMEM(value.shape, value.dtype) for value in operands[:3]]
        + [pltpu.SemaphoreType.DMA((4,))],
        name="select_blocks",
    )(*operands)


def prepared(weight, gain=None):
    if gain is not None:
        weight = weight * gain
    rolled = pltpu.roll(weight, weight.shape[1] // 2, 1)
    return jnp.where(lax.axis_index("chan") == 0, weight, rolled).astype(BF16)


def gated_rows(w_ref):
    gate, value = w_ref[0].astype(F32), w_ref[1].astype(F32)
    rows = []
    for at in range(0, gate.shape[0], 8):
        rows += [gate[at : at + 8], value[at : at + 8]]
    return [0.5 * row for row in rows]


def normed_of(mine, theirs, gain=None):
    total = 2 * mine.shape[0]
    mine = mine.astype(F32)
    theirs = theirs.astype(F32)
    mean = jnp.sum(mine + theirs, axis=0, keepdims=True) * (1.0 / total)
    mine = mine - mean
    theirs = theirs - mean
    spread = jnp.sum(mine * mine + theirs * theirs, axis=0, keepdims=True) * (1.0 / total)
    scale = lax.rsqrt(spread + epsilon)
    mine = mine * scale
    theirs = theirs * scale
    if gain is not None:
        half = mine.shape[0]
        mine = mine * gain[:half]
        theirs = theirs * gain[half:]
    return jnp.concatenate([mine.astype(BF16), theirs.astype(BF16)], axis=0)


def gated_sides(mine, theirs, weight, gain, half):
    y = jnp.dot(weight, normed_of(mine, theirs, gain), preferred_element_type=F32)
    sides = []
    for side in range(2):
        groups = []
        for row in range(2 * half * side, 2 * half * (side + 1), 16):
            groups.append((jnp.tanh(y[row : row + 8]) + 1.0) * y[row + 8 : row + 16])
        sides.append(groups)
    return sides, y[4 * half :]


def pair_chunk(sides_at, chunk, held):
    low = lax.broadcasted_iota(jnp.int32, (8, LANES), 1) < BLK
    pitch = held[0].shape[0] // (chunk // BLK)
    for start in range(0, chunk, LANES):
        first, second = sides_at(start)
        i = start // BLK
        for out, values0, values1 in zip(held, first, second):
            for at, (v0, v1) in enumerate(zip(values0, values1)):
                even = slice(i * pitch + 8 * at, i * pitch + 8 * at + 8)
                odd = slice((i + 1) * pitch + 8 * at, (i + 1) * pitch + 8 * at + 8)
                out[even, :] = jnp.where(low, v0, pltpu.roll(v1, BLK, 1))
                out[odd, :] = jnp.where(low, pltpu.roll(v0, BLK, 1), v1)
        yield


def spread_chunk(rows, held, l_ref, pair_of, l_row, p_ref, p_row, before, turned_ref, half):
    pitch = held[0].shape[0] // rows
    to = pl.ds(pl.multiple_of(l_row, 16), rows)
    for c in range(half):
        take = pl.ds(c, rows, stride=pitch)
        l_ref[pair_of, c, to, :] = held[0][take, :].astype(BF16)
        right = held[1][take, :]
        if turned_ref is None:
            p_ref[c, pl.ds(pl.multiple_of(p_row, 16), rows), :] = right.astype(BF16)
        else:
            whole = jnp.concatenate([ref[c, :size].astype(F32) for ref, size in before] + [right])
            turned = jnp.transpose(whole).astype(BF16)
            turned_ref[2 * pair_of, c] = turned[:BLK]
            turned_ref[2 * pair_of + 1, c] = turned[BLK:]
        if c % 8 == 7:
            yield


def two_chunks(sides_at, n, chunk, held, spread, after=()):
    steps = [
        pair_chunk(functools.partial(sides_at, n + k), chunk, held[2 * k : 2 * k + 2])
        for k in range(2)
    ]
    spreads = [spread(n + k, held[2 * k : 2 * k + 2], k) for k in range(2)]
    for _ in steps[0]:
        pass
    for _ in zip(steps[1], spreads[0]):
        pass
    for _ in spreads[0]:
        pass
    for at, _ in enumerate(spreads[1]):
        if at > 0:
            next(iter(after), None)
    for _ in after:
        pass


def cells_at(n, chunk, start):
    return pl.ds(pl.multiple_of(n * chunk + start, LANES), LANES)


def own_kernel(chunk, *refs):
    m_ref, t_ref = refs[:2]
    sources = refs[2:8]
    l_ref, turned_ref, gate_ref, w_ref, v_ref, gain_ref = refs[8:14]
    targets = refs[14:20]
    p_ref, held, sems = refs[20], refs[21:25], refs[25]
    copies = [
        pltpu.make_async_copy(source, target, sems.at[at])
        for at, (source, target) in enumerate(zip(sources, targets))
    ]
    for copy in copies:
        copy.start()
    half = l_ref.shape[1]

    @pl.loop(0, half)
    def _(c):
        turned_ref[4, c] = jnp.zeros((BLK, BLK), BF16)

    for copy in copies:
        copy.wait()
    a_ref, b_ref, o_ref, u_ref, g_ref, h_ref = targets
    rows = gated_rows(a_ref) + gated_rows(b_ref) + [0.5 * o_ref[...].astype(F32)]
    weight = prepared(jnp.concatenate(rows, axis=0))
    w_ref[...] = weight[: 4 * half]
    v_ref[...] = prepared(0.5 * u_ref[...].astype(F32), h_ref[...])
    across = jnp.transpose(jnp.broadcast_to(g_ref[...], (2 * half, LANES)))
    in_order = lax.axis_index("chan") == 0
    gain_ref[:half] = jnp.where(in_order, across[:half], across[half:])
    gain_ref[half:] = jnp.where(in_order, across[half:], across[:half])
    chunks = m_ref.shape[-1] // chunk
    rows = chunk // BLK

    def sides_at(n, start):
        at = cells_at(n, chunk, start)
        both = []
        for x in range(2):
            sides, rest = gated_sides(m_ref[x, :, at], t_ref[x, :, at], weight, gain_ref[...], half)
            gate_ref[x, :, at] = (jnp.tanh(rest) + 1.0).astype(BF16)
            both.append(sides)
        return both

    def spread(last, n, held, k):
        before, turned = ([(p_ref, (chunks - 1) * rows)], turned_ref) if last and k else (None, None)
        return spread_chunk(rows, held, l_ref, 0, n * rows, p_ref, n * rows, before, turned, half)

    @pl.loop(0, chunks - 2, step=2)
    def _(n):
        two_chunks(sides_at, n, chunk, held, functools.partial(spread, False))

    two_chunks(sides_at, chunks - 2, chunk, held, functools.partial(spread, True))


def fetched_sides(chunk, ours, theirs, weight, gain_ref, half):
    wide = theirs[0].shape[1]

    def sides_at(n, start):
        at = n * chunk + start
        both = []
        for x, m in enumerate(ours):
            other = theirs[2 * (at // wide) + x][:, at % wide : at % wide + LANES]
            both.append(
                gated_sides(m[:, at : at + LANES], other, weight, gain_ref[...], half)[0]
            )
        return both

    return sides_at


def first_kernel(chunk, *refs):
    *ours_theirs, w_ref, gain_ref, _, l_ref, p_ref = refs[:-4]
    held = refs[-4:]
    half = l_ref.shape[1]
    rows = chunk // BLK
    sides_at = fetched_sides(
        chunk, ours_theirs[:2], ours_theirs[2:], w_ref[...], gain_ref, half
    )

    def spread(n, held, k):
        return spread_chunk(rows, held, l_ref, 1, n * rows, p_ref, n * rows, None, None, half)

    two_chunks(sides_at, 0, chunk, held, spread)


def last_kernel(chunk, first_row, group, picks_ref, *refs):
    *ours_theirs, p0_ref, w_ref, gain_ref, _, _, l_ref, turned_ref, out_ref, p_ref = refs[:-6]
    held, accs = refs[-6:-2], refs[-2:]
    before = [(p0_ref, p0_ref.shape[1]), (p_ref, p_ref.shape[1])]
    half = l_ref.shape[1]
    rows = chunk // BLK
    sides_at = fetched_sides(
        chunk, ours_theirs[:2], ours_theirs[2:], w_ref[...], gain_ref, half
    )

    def spread(n, held, k):
        done = (before, turned_ref) if k else (None, None)
        return spread_chunk(rows, held, l_ref, 1, first_row + n * rows, p_ref, n * rows, *done, half)

    products = triplet_steps(0, group, picks_ref, l_ref, turned_ref, out_ref, accs)
    two_chunks(sides_at, 0, chunk, held, spread, products)


def triplet_steps(s, group, picks_ref, l_ref, turned_ref, out_ref, accs):
    picks = [picks_ref[4 * s + at] for at in range(4)]
    take_low = lax.broadcasted_iota(jnp.int32, (group, LANES), 1) < BLK
    pitch = accs[0].shape[0] // BLK
    for first in range(0, l_ref.shape[1], group):
        acc = accs[first // group % len(accs)]
        for at in range(group):
            c = first + at
            lhs = jnp.concatenate([l_ref[0, c], l_ref[1, c]], axis=1)
            rhs = jnp.concatenate([turned_ref[pick, c] for pick in picks], axis=0)
            acc[pl.ds(at, BLK, stride=pitch), :BLK] = jnp.dot(
                lhs, rhs, preferred_element_type=F32
            )
            if at % 8 == 7 and at + 1 < group:
                yield
        for t in range(BLK // 2):
            even = acc[2 * t * pitch : 2 * t * pitch + group, :]
            odd = acc[(2 * t + 1) * pitch : (2 * t + 1) * pitch + group, :]
            out_ref[first : first + group, t * LANES : (t + 1) * LANES] = jnp.where(
                take_low, even, pltpu.roll(odd, BLK, 1)
            ).astype(BF16)
        yield


def triplet_kernel(s, group, picks_ref, l_ref, turned_ref, out_ref, *accs):
    for _ in triplet_steps(s, group, picks_ref, l_ref, turned_ref, out_ref, accs):
        pass


def acc_scratch(group):
    return [pltpu.VMEM((BLK * (group + 8), LANES), F32)] * 2


def chunk_scratch(half, chunk):
    return [pltpu.VMEM((chunk // BLK * (half + 8), LANES), F32)] * 4


def call(kernel, name, operands, out_shape, scratch, aliased=0, hbm=0, smem=0):
    spaces = [pltpu.SMEM] * smem + [pltpu.VMEM] * (len(operands) - smem - hbm) + [pltpu.HBM] * hbm
    plain = len(operands) - aliased
    operands = [
        value
        if space == pltpu.VMEM and at < plain
        else pltpu.with_memory_space_constraint(value, space)
        for at, (value, space) in enumerate(zip(operands, spaces))
    ]
    return pl.pallas_call(
        kernel,
        in_specs=[pl.BlockSpec(memory_space=space) for space in spaces],
        out_specs=[pl.BlockSpec(memory_space=pltpu.VMEM)] * len(out_shape),
        out_shape=out_shape,
        scratch_shapes=scratch,
        input_output_aliases={plain + at: at for at in range(aliased)},
        compiler_params=pltpu.CompilerParams(vmem_limit_bytes=VMEM_LIMIT),
        name=name,
    )(*operands)


def finish_kernel(s, run, pieces, mine_ref, theirs_ref, gate_ref, w_ref, *refs):
    weight = w_ref[...]
    cells = mine_ref.shape[-1]
    if s == 0:
        held = refs[0]
    else:
        before_ref, out_ref, held, sems = refs
        before = pltpu.make_async_copy(before_ref, out_ref.at[0], sems.at[pieces])
        before.start()
    size = cells // pieces

    def copy(n):
        to = pl.ds(pl.multiple_of(n * size, size), size)
        return pltpu.make_async_copy(held.at[:, to], out_ref.at[1, :, to], sems.at[n])

    @pl.loop(0, cells // run)
    def _(n):
        for start in range(0, run, LANES):
            to = cells_at(n, run, start)
            normed = normed_of(mine_ref[:, to], theirs_ref[:, to])
            projected = jnp.dot(weight, normed, preferred_element_type=F32)
            held[:, to] = (gate_ref[s, :, to].astype(F32) * projected).astype(BF16)
            done = start + LANES
            if s > 0 and done % size == 0:
                copy(n * (run // size) + done // size - 1).start()

    if s > 0:
        for n in range(pieces):
            copy(n).wait()
        before.wait()


def finish(s, mine, theirs, gate, weight, before=None):
    vmem = pl.BlockSpec(memory_space=pltpu.VMEM)
    operands = [mine, theirs, gate, weight]
    if s == 0:
        out_shape, out_specs, scratch = pltpu.VMEM(mine.shape, BF16), vmem, []
    else:
        operands.append(before)
        out_shape = jax.ShapeDtypeStruct(gate.shape, BF16)
        out_specs = pl.BlockSpec(memory_space=pltpu.HBM)
        scratch = [pltpu.VMEM(mine.shape, BF16), pltpu.SemaphoreType.DMA((5,))]
    return pl.pallas_call(
        functools.partial(finish_kernel, s, mine.shape[1], 4),
        in_specs=[vmem] * len(operands),
        out_specs=out_specs,
        out_shape=out_shape,
        scratch_shapes=scratch,
        compiler_params=pltpu.CompilerParams(vmem_limit_bytes=VMEM_LIMIT),
        name="finish",
    )(*operands)


def per_device(
    pair,
    ln_in_gain,
    a_weight,
    b_weight,
    ln_out_gain,
    out_gate_weight,
    out_weight,
    a_slots,
    b_slots,
    counts,
):
    slots, half, cells = pair.shape
    rows = lax.axis_size("row")
    swap = [(0, 1), (1, 0)]
    up = [(i, (i + 1) % rows) for i in range(rows)]
    down = [(i, (i - 1) % rows) for i in range(rows)]

    a_slots, b_slots = a_slots.T, b_slots.T
    weights = [
        jnp.swapaxes(a_weight, 1, 2),
        jnp.swapaxes(b_weight, 1, 2),
        out_gate_weight.T,
        out_weight.T,
        ln_in_gain[None, :],
        ln_out_gain[None, :],
    ]

    chunk = cells // 4
    cuts = ((0, 2 * chunk), (2 * chunk, 2 * chunk))
    picks, pair, *chosen = select_blocks(pair, a_slots, b_slots, counts, cuts)
    arrived = []
    for n in range(len(cuts)):
        moved = {}
        for which in (0, 1) if n == 0 else (1, 0):
            moved[which] = lax.ppermute(chosen[2 * n + which], "row", (up, down)[which])
        arrived.append((moved[0], moved[1]))
    pair_other = lax.ppermute(pair, "chan", swap)
    left_shape = pltpu.VMEM((2, half, BLK, LANES), BF16)
    right_shape = pltpu.VMEM((5, half, BLK, BLK), BF16)
    lefts, rights, gate, weight, last_weight, gain = call(
        functools.partial(own_kernel, chunk),
        "project_own",
        [pair, pair_other, *weights],
        [
            left_shape,
            right_shape,
            pltpu.VMEM((slots, half, cells), BF16),
            pltpu.VMEM((4 * half, 2 * half), BF16),
            pltpu.VMEM((half, 2 * half), BF16),
            pltpu.VMEM((2 * half, LANES), F32),
        ],
        [pltpu.VMEM(value.shape, value.dtype) for value in weights]
        + [pltpu.VMEM((half, BLK, LANES), BF16)]
        + chunk_scratch(half, chunk)
        + [pltpu.SemaphoreType.DMA((len(weights),))],
        hbm=len(weights),
    )
    for (start, size), behind_ahead in zip(cuts, arrived):
        *behind_ahead, lefts = lax.optimization_barrier((*behind_ahead, lefts))
        wide = chunk if start == 0 else size
        others = [
            lax.ppermute(lax.slice_in_dim(value, at, at + wide, axis=1), "chan", swap)
            for at in range(0, size, wide)
            for value in behind_ahead
        ]
        paired = pltpu.VMEM((half, size // BLK, LANES), BF16)
        if start == 0:
            lefts, rights_first = call(
                functools.partial(first_kernel, chunk),
                "project_first",
                [*behind_ahead, *others, weight, gain, lefts],
                [left_shape, paired],
                chunk_scratch(half, chunk),
                aliased=1,
            )
        else:
            lefts, rights, update = call(
                functools.partial(last_kernel, chunk, start // BLK, 16),
                "project_last",
                [picks, *behind_ahead, *others, rights_first, weight, gain, lefts, rights],
                [left_shape, right_shape, pltpu.VMEM((half, cells), BF16)],
                [pltpu.VMEM((half, chunk // BLK, LANES), BF16)]
                + chunk_scratch(half, chunk)
                + acc_scratch(16),
                aliased=2,
                smem=1,
            )
    updates = [(update, lax.ppermute(update, "chan", swap))]
    update, lefts = lax.optimization_barrier((update, lefts))
    for s in range(1, slots):
        (update,) = call(
            functools.partial(triplet_kernel, s, 16),
            "triplets",
            [picks, lefts, rights],
            [pltpu.VMEM((half, cells), BF16)],
            acc_scratch(16) * 2,
            smem=1,
        )
        updates.append((update, lax.ppermute(update, "chan", swap)))
    out = None
    for s, (mine, theirs) in enumerate(updates):
        out = finish(s, mine, theirs, gate, last_weight, out)
    return out


def solution(mesh):
    in_specs = (
        P(("parts", "row", "col"), "chan", None),
        P(),
        P(None, None, "chan"),
        P(None, None, "chan"),
        P(),
        P(None, "chan"),
        P(None, "chan"),
        P("parts", None),
        P("parts", None),
        P("parts"),
    )
    out_specs = P(("parts", "row", "col"), "chan", None)
    return jax.shard_map(
        per_device, mesh=mesh, in_specs=in_specs, out_specs=out_specs, check_vma=False
    )
```
